32 devices in a mesh: dap: 16 (over z, x, core), grp: 2 (over y).
Axes of the slice: x: 2, y: 2, z: 4, core: 2. Of those that a mesh axis runs over, the one named last changes fastest.
Arguments:
- homolog_activity: bfloat16 [32, 256, 256], P(None, ('dap', 'grp')), may hold values from -6 to 6
- alignment_mask: int32 [32, 256], P(None, ('dap', 'grp')), may hold values from 0 to 1, as said below
- sequence_row_mask: int32 [32], replicated, may hold values from 0 to 1, as said below
- pairwise_bias: bfloat16 [8, 256, 256], P(None, 'dap', 'grp'), may hold values from -400 to 400
- horizontal_projection_matrix: bfloat16 [256, 4, 256], P(None, None, 'grp'), may hold values from -0.375 to 0.375
- horizontal_final_matrix: bfloat16 [256, 256], P('grp'), may hold values from -0.375 to 0.375
- column_query_weight: bfloat16 [256, 256], replicated, may hold values from -1 to 1
- column_key_weight: bfloat16 [256, 256], replicated, may hold values from -50 to 50
- vertical_content_sigmoid_matrix: bfloat16 [256, 2, 256], replicated, may hold values from -0.375 to 0.375
- vertical_final_matrix: bfloat16 [256, 256], replicated, may hold values from -0.375 to 0.375
- first_operand_matrix: bfloat16 [256, 32], replicated, may hold values from -0.375 to 0.375
- second_operand_matrix: bfloat16 [256, 32], replicated, may hold values from -0.375 to 0.375
- outer_output_weight: bfloat16 [1024, 128], replicated, may hold values from -1 to 1
Outputs:
- alignment_output: bfloat16 [32, 256, 256], P(None, ('dap', 'grp'))
- pairwise_update: bfloat16 [256, 256, 128], P(('dap', 'grp'))
The draws below stay inside these ranges and needn't reach their ends.
Inputs may be any that keep to these rules, and one draw needn't show every extreme that they name: `alignment_mask`: row 0 is all ones. `sequence_row_mask`: entry 0 is 1; at least one entry is 0.
All inputs are finite; a program needn't handle non-finite values.
Results may differ from the reference program's by a relative error of at most 0.023.
Values may be sent and summed in bfloat16 or wider, within the bound.
No kernel may reach another device: no remote copies, remote signals or barrier semaphores. Data moves between devices by JAX's collectives and lax.ppermute only.
A program may use at most 192 MiB of HBM per device.

```python
import jax
import jax.numpy as jnp
from jax import lax

FEATURE_DEPTH = 256
CZ = 128
FOCUS_SPLITS = 8
PER_SPLIT_DIM = 32
PROJ_DEPTH = 32
CHAIN_POSITIONS = 256
HOMOLOG_TOTAL = 32


def draw_column_query_weight(key, part):
    key = jax.random.fold_in(key, 5)
    private_random_state = jnp.clip(jax.random.normal(key, (FEATURE_DEPTH, FOCUS_SPLITS * PER_SPLIT_DIM), jnp.float32), -6.0, 6.0)
    return (private_random_state / FEATURE_DEPTH ** 0.5).astype(jnp.bfloat16)


def draw_column_key_weight(key, part):
    key = jax.random.fold_in(key, 6)
    private_random_state = jnp.clip(jax.random.normal(key, (FEATURE_DEPTH, FOCUS_SPLITS * PER_SPLIT_DIM), jnp.float32), -6.0, 6.0) / FEATURE_DEPTH ** 0.5
    return private_random_state.astype(jnp.bfloat16)


def draw_pairwise_bias(key, part):
    key = jax.random.fold_in(key, 3)
    full_shape = (FOCUS_SPLITS, CHAIN_POSITIONS, CHAIN_POSITIONS)
    primary_random_state = jnp.clip(jax.random.normal(key, full_shape, jnp.float32), -6.0, 6.0)
    return primary_random_state.astype(jnp.bfloat16)


def draw_alignment_mask(key, part):
    key = jax.random.fold_in(key, 7)
    draws_int = jax.random.randint(key, (HOMOLOG_TOTAL, CHAIN_POSITIONS), 0, 20)
    present = (draws_int >= 3).astype(jnp.int32)
    row_ids = lax.broadcasted_iota(jnp.int32, (HOMOLOG_TOTAL, CHAIN_POSITIONS), 0)
    return jnp.where(row_ids == 0, 1, present).astype(jnp.int32)


def draw_sequence_row_mask(key, part):
    key = jax.random.fold_in(key, 9)
    first_key, second_key = jax.random.split(key)
    draws_int = jax.random.randint(first_key, (HOMOLOG_TOTAL,), 0, 8)
    present = (draws_int >= 1).astype(jnp.int32)
    dropped_row = jax.random.randint(second_key, (), 1, HOMOLOG_TOTAL)
    row_ids = lax.broadcasted_iota(jnp.int32, (HOMOLOG_TOTAL,), 0)
    present = jnp.where(row_ids == dropped_row, 0, present)
    return jnp.where(row_ids == 0, 1, present).astype(jnp.int32)


def shard_levels(key, shape, cuts, least, high):
    factor_of, own = 1.0, jax.random.fold_in(key, 6)
    for axis_at, parts in cuts:
        heights = jnp.exp(jax.random.uniform(jax.random.fold_in(own, axis_at), (parts,), jnp.float32, least / len(cuts), high / len(cuts)))
        factor_of = factor_of * jnp.repeat(heights, shape[axis_at] // parts).reshape([-1 if axis == axis_at else 1 for axis in range(len(shape))])
    return factor_of


def normal_values(key, dims, spread, reach, cuts=(), held_as=jnp.bfloat16):
    array = spread * jax.random.normal(key, dims, jnp.float32)
    if cuts:
        array = array * shard_levels(key, dims, cuts, -0.22, 0.18)
    return jnp.clip(array, -reach, reach).astype(held_as)


def setup_inputs(seed: int = 0) -> dict:
    seeds = jax.random.split(jax.random.key(seed), 14)
    homolog_activity = normal_values(seeds[0], (HOMOLOG_TOTAL, CHAIN_POSITIONS, FEATURE_DEPTH), 1.0, 6.0, ((1, 32),))
    alignment_mask = draw_alignment_mask(jax.random.fold_in(seeds[13], 71), 0)
    sequence_row_mask = draw_sequence_row_mask(jax.random.fold_in(seeds[13], 71), 0)
    pairwise_bias = draw_pairwise_bias(jax.random.fold_in(seeds[13], 71), 0)
    horizontal_projection_matrix = normal_values(seeds[4], (FEATURE_DEPTH, 4, FOCUS_SPLITS * PER_SPLIT_DIM), FEATURE_DEPTH ** -0.5, 0.375, ((2, 2),))
    horizontal_final_matrix = normal_values(seeds[5], (FOCUS_SPLITS * PER_SPLIT_DIM, FEATURE_DEPTH), (FOCUS_SPLITS * PER_SPLIT_DIM) ** -0.5, 0.375, ((0, 2),))
    column_query_weight = draw_column_query_weight(jax.random.fold_in(seeds[13], 71), 0)
    column_key_weight = draw_column_key_weight(jax.random.fold_in(seeds[13], 71), 0)
    vertical_content_sigmoid_matrix = normal_values(seeds[8], (FEATURE_DEPTH, 2, FOCUS_SPLITS * PER_SPLIT_DIM), FEATURE_DEPTH ** -0.5, 0.375)
    vertical_final_matrix = normal_values(seeds[9], (FOCUS_SPLITS * PER_SPLIT_DIM, FEATURE_DEPTH), (FOCUS_SPLITS * PER_SPLIT_DIM) ** -0.5, 0.375)
    first_operand_matrix = normal_values(seeds[10], (FEATURE_DEPTH, PROJ_DEPTH), FEATURE_DEPTH ** -0.5, 0.375)
    second_operand_matrix = normal_values(seeds[11], (FEATURE_DEPTH, PROJ_DEPTH), FEATURE_DEPTH ** -0.5, 0.375)
    outer_output_weight = normal_values(seeds[12], (PROJ_DEPTH * PROJ_DEPTH, CZ), (max(1, PROJ_DEPTH * PROJ_DEPTH // HOMOLOG_TOTAL)) ** -0.5, 1.0)
    return {"homolog_activity": homolog_activity, "alignment_mask": alignment_mask, "sequence_row_mask": sequence_row_mask, "pairwise_bias": pairwise_bias, "horizontal_projection_matrix": horizontal_projection_matrix, "horizontal_final_matrix": horizontal_final_matrix, "column_query_weight": column_query_weight, "column_key_weight": column_key_weight, "vertical_content_sigmoid_matrix": vertical_content_sigmoid_matrix, "vertical_final_matrix": vertical_final_matrix, "first_operand_matrix": first_operand_matrix, "second_operand_matrix": second_operand_matrix, "outer_output_weight": outer_output_weight}


def layer_normalize(values):
    widened = values.astype(jnp.float32)
    centered = widened - lax.optimization_barrier(jnp.mean(widened, axis=-1, keepdims=True))
    variance = lax.optimization_barrier(jnp.mean(centered * centered, axis=-1, keepdims=True))
    return (centered * lax.rsqrt(variance + 1e-05)).astype(jnp.bfloat16)

def reference(homolog_activity, alignment_mask, sequence_row_mask, pairwise_bias, horizontal_projection_matrix, horizontal_final_matrix, column_query_weight, column_key_weight, vertical_content_sigmoid_matrix, vertical_final_matrix, first_operand_matrix, second_operand_matrix, outer_output_weight):
    query_factor = PER_SPLIT_DIM ** (-0.5)
    retain_everything = (alignment_mask * sequence_row_mask[:, None]).astype(jnp.float32)
    normalized_input = layer_normalize(homolog_activity)
    normed_wide = normalized_input.astype(jnp.float32)
    left_fac = (jnp.einsum('snc,co->sno', normed_wide, first_operand_matrix.astype(jnp.float32)) * retain_everything[..., None]).astype(jnp.bfloat16)
    right_fac = (jnp.einsum('snc,co->sno', normed_wide, second_operand_matrix.astype(jnp.float32)) * retain_everything[..., None]).astype(jnp.bfloat16)
    counts = jnp.dot(retain_everything.T, retain_everything, precision=lax.Precision.HIGHEST)
    block_len = min(64, CHAIN_POSITIONS)

    def opm_block(block_index):
        left_part = lax.dynamic_slice_in_dim(left_fac, block_index * block_len, block_len, 1)
        count_part = lax.dynamic_slice_in_dim(counts, block_index * block_len, block_len, 0)
        outer_prod = jnp.einsum('sic,sjd->ijcd', left_part.astype(jnp.float32), right_fac.astype(jnp.float32))
        outer_prod = outer_prod.reshape(block_len, CHAIN_POSITIONS, PROJ_DEPTH * PROJ_DEPTH).astype(jnp.bfloat16)
        projected = jnp.einsum('ijf,fz->ijz', outer_prod.astype(jnp.float32), outer_output_weight.astype(jnp.float32))
        return (projected / count_part[..., None]).astype(jnp.bfloat16)
    pairwise_update = lax.map(opm_block, jnp.arange(CHAIN_POSITIONS // block_len, dtype=jnp.int32)).reshape(CHAIN_POSITIONS, CHAIN_POSITIONS, CZ)
    projected = jnp.einsum('snc,cfe->snfe', normed_wide, horizontal_projection_matrix.astype(jnp.float32))
    row_q = (projected[:, :, 0] * query_factor).astype(jnp.bfloat16).reshape(HOMOLOG_TOTAL, CHAIN_POSITIONS, FOCUS_SPLITS, PER_SPLIT_DIM)
    row_k = projected[:, :, 1].astype(jnp.bfloat16).reshape(HOMOLOG_TOTAL, CHAIN_POSITIONS, FOCUS_SPLITS, PER_SPLIT_DIM)
    row_v = projected[:, :, 2].astype(jnp.bfloat16).reshape(HOMOLOG_TOTAL, CHAIN_POSITIONS, FOCUS_SPLITS, PER_SPLIT_DIM)
    row_gate = jax.nn.sigmoid(projected[:, :, 3]).reshape(HOMOLOG_TOTAL, CHAIN_POSITIONS, FOCUS_SPLITS, PER_SPLIT_DIM)
    bias_wide = pairwise_bias.astype(jnp.float32)

    def row_one(element):
        queries, key_rows, value_rows, gating, keep_row = element
        scores = jnp.einsum('ihd,jhd->hij', queries.astype(jnp.float32), key_rows.astype(jnp.float32)) + bias_wide
        scores = jnp.where(keep_row[None, None, :] > 0, scores, -1000000000.0)
        weights = jax.nn.softmax(scores, axis=-1).astype(jnp.bfloat16)
        mixture = jnp.einsum('hij,jhd->ihd', weights.astype(jnp.float32), value_rows.astype(jnp.float32)) * gating
        mixture = mixture.astype(jnp.bfloat16).reshape(CHAIN_POSITIONS, FOCUS_SPLITS * PER_SPLIT_DIM)
        return jnp.dot(mixture, horizontal_final_matrix, preferred_element_type=jnp.float32)
    row_output = lax.map(row_one, (row_q, row_k, row_v, row_gate, retain_everything))
    row_result = (homolog_activity.astype(jnp.float32) + row_output).astype(jnp.bfloat16)
    column_normalized = layer_normalize(row_result).astype(jnp.float32)
    column_query = (jnp.einsum('ruj,jp->rup', column_normalized, column_query_weight.astype(jnp.float32)) * query_factor).astype(jnp.bfloat16).reshape(HOMOLOG_TOTAL, CHAIN_POSITIONS, FOCUS_SPLITS, PER_SPLIT_DIM)
    column_key = jnp.einsum('ruj,jp->rup', column_normalized, column_key_weight.astype(jnp.float32)).astype(jnp.bfloat16).reshape(HOMOLOG_TOTAL, CHAIN_POSITIONS, FOCUS_SPLITS, PER_SPLIT_DIM)
    col_vg = jnp.einsum('snc,cfe->snfe', column_normalized, vertical_content_sigmoid_matrix.astype(jnp.float32))
    col_v = col_vg[:, :, 0].astype(jnp.bfloat16).reshape(HOMOLOG_TOTAL, CHAIN_POSITIONS, FOCUS_SPLITS, PER_SPLIT_DIM)
    col_gate = jax.nn.sigmoid(col_vg[:, :, 1]).reshape(HOMOLOG_TOTAL, CHAIN_POSITIONS, FOCUS_SPLITS, PER_SPLIT_DIM)
    col_len = min(64, CHAIN_POSITIONS)

    def col_block(block_index):
        start_at = block_index * col_len
        queries = lax.dynamic_slice_in_dim(column_query, start_at, col_len, 1).astype(jnp.float32)
        key_rows = lax.dynamic_slice_in_dim(column_key, start_at, col_len, 1).astype(jnp.float32)
        value_rows = lax.dynamic_slice_in_dim(col_v, start_at, col_len, 1).astype(jnp.float32)
        gating = lax.dynamic_slice_in_dim(col_gate, start_at, col_len, 1)
        keep_part = lax.dynamic_slice_in_dim(retain_everything, start_at, col_len, 1)
        scores = jnp.einsum('snhd,tnhd->nhst', queries, key_rows)
        scores = jnp.where(keep_part.T[:, None, None, :] > 0, scores, -1000000000.0)
        weights = jax.nn.softmax(scores, axis=-1).astype(jnp.bfloat16)
        mixture = jnp.einsum('nhst,tnhd->snhd', weights.astype(jnp.float32), value_rows) * gating
        mixture = mixture.astype(jnp.bfloat16).reshape(HOMOLOG_TOTAL, col_len, FOCUS_SPLITS * PER_SPLIT_DIM)
        return jnp.dot(mixture, vertical_final_matrix, preferred_element_type=jnp.float32)
    vertical_mixed = lax.map(col_block, jnp.arange(CHAIN_POSITIONS // col_len, dtype=jnp.int32))
    vertical_mixed = vertical_mixed.transpose(1, 0, 2, 3).reshape(HOMOLOG_TOTAL, CHAIN_POSITIONS, FEATURE_DEPTH)
    alignment_output = (row_result.astype(jnp.float32) + vertical_mixed).astype(jnp.bfloat16)
    return (alignment_output, pairwise_update)
```

```python
import functools

import jax
import jax.numpy as jnp
from jax import lax
from jax.experimental import pallas as pl
from jax.experimental.pallas import tpu as pltpu
from jax.sharding import PartitionSpec as P

PER_SPLIT_DIM = 32
LANES = 128
MASKED = -1000000000.0
F32 = jnp.float32
BF16 = jnp.bfloat16


def matmul(lhs, rhs):
    return jnp.dot(lhs, rhs, preferred_element_type=F32)


def matmul_nt(lhs, rhs):
    return lax.dot_general(lhs, rhs, (((1,), (1,)), ((), ())), preferred_element_type=F32)


def matmul_tn(lhs, rhs):
    return lax.dot_general(lhs, rhs, (((0,), (0,)), ((), ())), preferred_element_type=F32)


def rows_of(shape):
    return lax.broadcasted_iota(jnp.int32, shape, 0)


def lanes_of(shape):
    return lax.broadcasted_iota(jnp.int32, shape, 1)


def quotient(values, divisor):
    return lax.shift_right_logical(values, divisor.bit_length() - 1)


def remainder(values, divisor):
    return values & (divisor - 1)


def one_hot(condition):
    return condition.astype(F32).astype(BF16)


def flat_rows(tiles):
    blocks, sublanes, lanes = tiles.shape
    return tiles.astype(F32).reshape(blocks * sublanes, lanes).astype(BF16)


def layer_normalize(widened):
    centered = widened - jnp.mean(widened, axis=-1, keepdims=True)
    variance = jnp.mean(centered * centered, axis=-1, keepdims=True)
    return (centered * lax.rsqrt(variance + 1e-05)).astype(BF16)


def residue_major(sequences, residues):
    total = sequences * residues
    row, lane = rows_of((total, total)), lanes_of((total, total))
    return one_hot(lane == remainder(row, sequences) * residues + quotient(row, sequences))


def prepare_kernel(
    sizes, x_ref, mask_ref, present_ref, bias_ref, left_w_ref, right_w_ref,
    rows_ref, right_ref, left_ref, keep_ref,
):
    groups, sequences_here = sizes
    sequences, residues, width = x_ref.shape
    total = sequences * residues
    channels = left_w_ref.shape[1]
    keep = (mask_ref[...] * present_ref[...]).astype(F32)
    keep_padded = jnp.pad(keep, ((0, 0), (0, LANES - sequences))) if sequences < LANES else keep
    keep_ref[...] = keep_padded
    normed = layer_normalize(x_ref[...].astype(F32).reshape(total, width))
    normed_tiles = normed.astype(F32).reshape(sequences, residues, width).astype(BF16)
    halves = width // LANES
    heads, bias_rows, bias_columns = bias_ref.shape
    heads_here = heads // groups
    keep_tile = keep_padded.astype(BF16)
    for group in range(groups):
        for part in range(sequences // sequences_here):
            target = part * groups + group
            for own in range(sequences_here):
                for half in range(halves):
                    rows_ref[target, own * halves + half] = normed_tiles[
                        part * sequences_here + own, :, half * LANES : (half + 1) * LANES
                    ]
            rows_ref[target, sequences_here * halves] = keep_tile
            slot = sequences_here * halves + 1
            for head in range(heads_here):
                for block in range(bias_rows // residues):
                    for half in range(bias_columns // LANES):
                        rows_ref[target, slot] = bias_ref[
                            group * heads_here + head,
                            block * residues : (block + 1) * residues,
                            half * LANES : (half + 1) * LANES,
                        ]
                        slot += 1

    to_residue_major = residue_major(sequences, residues)
    left = matmul(normed, left_w_ref[...]).astype(BF16)
    left = matmul(to_residue_major, left)
    pick = one_hot(
        quotient(rows_of((total, residues)), sequences) == lanes_of((total, residues))
    )
    own_keep = matmul(pick, keep.astype(BF16))
    at_sequence = remainder(rows_of((total, sequences)), sequences) == lanes_of((total, sequences))
    own_keep = jnp.sum(jnp.where(at_sequence, own_keep, 0.0), axis=1, keepdims=True)
    left_ref[...] = (left * own_keep).astype(BF16)

    right = matmul(normed, right_w_ref[...]).astype(BF16)
    residue_pick = one_hot(
        remainder(lanes_of((residues, total)), residues) == rows_of((residues, total))
    )
    per_tile = LANES // sequences
    spread = one_hot(
        remainder(lanes_of((sequences, LANES)), sequences) == rows_of((sequences, LANES))
    )
    keep_spread = matmul(keep.astype(BF16), spread)
    same_sequence = quotient(rows_of((total, LANES)), residues) == remainder(
        lanes_of((total, LANES)), sequences
    )
    for tile in range(channels // per_tile):
        select = one_hot(
            rows_of((channels, LANES))
            == tile * per_tile + quotient(lanes_of((channels, LANES)), sequences)
        )
        expanded = jnp.where(same_sequence, matmul(right, select), 0.0).astype(BF16)
        result = (matmul(residue_pick, expanded) * keep_spread).astype(BF16)
        for target in range(right_ref.shape[0]):
            right_ref[target, tile] = result


def row_kernel(sizes, place_ref, rows_ref, weight_ref, mix_ref, query_s, key_s, value_s, gate_s):
    parallel, groups, sequences_here, heads_here = sizes
    blocks, tiles, residues, _ = rows_ref.shape
    residues_overall = blocks * residues
    halves = weight_ref.shape[1] // LANES
    head_lanes = heads_here * PER_SPLIT_DIM
    bias_row_blocks = residues_overall // parallel // residues
    bias_column_blocks = residues_overall // groups // LANES
    query_factor = PER_SPLIT_DIM ** (-0.5)
    block_rows = min(residues_overall, 256)

    keep_all = flat_rows(rows_ref[:, sequences_here * halves])
    chosen = one_hot(
        lanes_of((8, LANES)) == place_ref[0] * sequences_here + rows_of((8, LANES))
    )
    key_keep = matmul_nt(chosen, keep_all)

    for own in range(sequences_here):
        normed = jnp.concatenate(
            [flat_rows(rows_ref[:, own * halves + half]) for half in range(halves)], axis=1
        )
        query_s[own] = (matmul(normed, weight_ref[0]) * query_factor).astype(BF16)
        key_s[own] = matmul(normed, weight_ref[1]).astype(BF16)
        value_s[own] = matmul(normed, weight_ref[2]).astype(BF16)
        gate_s[own] = jax.nn.sigmoid(matmul(normed, weight_ref[3]))

    def attend(block):
        start = block * block_rows
        first_part = block * (block_rows // (bias_row_blocks * residues))
        parts = block_rows // (bias_row_blocks * residues)
        head_of = quotient(lanes_of((residues_overall, head_lanes)), PER_SPLIT_DIM)
        query_head = quotient(lanes_of((block_rows, head_lanes)), PER_SPLIT_DIM)
        biases = []
        for head in range(heads_here):
            columns = []
            for group in range(groups):
                for half in range(bias_column_blocks):
                    pieces = []
                    for part in range(parts):
                        for row_block in range(bias_row_blocks):
                            slot = (
                                sequences_here * halves
                                + 1
                                + (head * bias_row_blocks + row_block) * bias_column_blocks
                                + half
                            )
                            pieces.append(
                                rows_ref[(first_part + part) * groups + group, slot].astype(F32)
                            )
                    columns.append(jnp.concatenate(pieces, axis=0))
            biases.append(jnp.concatenate(columns, axis=1))
        for own in range(sequences_here):
            queries = query_s[own, pl.ds(start, block_rows), :]
            keys, values = key_s[own], value_s[own]
            keep_row = key_keep[own : own + 1, :] > 0.5
            total = jnp.zeros((block_rows, 2 * head_lanes), F32)
            for head in range(heads_here):
                query_part = jnp.where(query_head == head, queries, jnp.zeros_like(queries))
                scores = matmul_nt(query_part, keys) + biases[head]
                scores = jnp.where(keep_row, scores, MASKED)
                scores = scores - jnp.max(scores, axis=1, keepdims=True)
                weights = jnp.exp(scores).astype(BF16)
                mine = head_of == head
                value_part = jnp.where(mine, values, jnp.zeros_like(values))
                total = total + matmul(
                    weights, jnp.concatenate([value_part, one_hot(mine)], axis=1)
                )
            mixed = total[:, :head_lanes] / total[:, head_lanes:]
            mixed = mixed * gate_s[own, pl.ds(start, block_rows), :]
            mix_ref[pl.ds(block * (block_rows // residues), block_rows // residues), own] = (
                mixed.reshape(block_rows // residues, residues, head_lanes).astype(BF16)
            )

    if residues_overall == block_rows:
        attend(0)
    else:
        pl.loop(0, residues_overall // block_rows)(attend)


def outer_kernel(sizes, rows_ref, right_ref, left_ref, keep_ref, weight_ref, out_ref, mixed_s):
    keep_slot, sequences, pair = sizes
    blocks, right_tiles, residues, _ = right_ref.shape
    segment = blocks * residues
    channels, _, depth = weight_ref.shape
    left = left_ref[...]
    per_step = 2 if depth == LANES else 1
    for channel in range(0, channels, per_step):
        weights = jnp.concatenate(
            [weight_ref[channel + at] for at in range(per_step)], axis=1
        )
        product = matmul(left, weights).astype(BF16)
        for residue in range(residues):
            for at in range(per_step):
                mixed_s[
                    residue, (channel + at) * sequences : (channel + at + 1) * sequences, :
                ] = product[
                    residue * sequences : (residue + 1) * sequences, at * depth : (at + 1) * depth
                ]
    right = jnp.concatenate(
        [flat_rows(right_ref[:, tile]) for tile in range(right_tiles)], axis=1
    )
    keep_all = flat_rows(rows_ref[:, keep_slot])
    for first in range(0, residues, pair):
        members = range(first, first + pair)
        mixed = jnp.concatenate([mixed_s[residue] for residue in members], axis=1)
        keep_rows = jnp.concatenate(
            [
                jnp.broadcast_to(keep_ref[residue : residue + 1, :], (depth, LANES))
                for residue in members
            ],
            axis=0,
        ).astype(BF16)
        result = matmul(right, mixed) / matmul_nt(keep_all, keep_rows)
        for at, residue in enumerate(members):
            out_ref[residue] = result[:, at * depth : (at + 1) * depth].astype(BF16)
    del segment


def column_kernel(
    sizes, place_ref, x_ref, mix_ref, keep_ref, row_out_ref, query_w_ref, key_w_ref, vg_w_ref,
    out_w_ref, out_ref,
):
    groups = sizes
    sequences, residues, width = x_ref.shape
    total = sequences * residues
    heads = query_w_ref.shape[1] // PER_SPLIT_DIM
    query_factor = PER_SPLIT_DIM ** (-0.5)
    own_group = place_ref[1]
    after = x_ref[...].astype(F32).reshape(total, width)
    for at in range(groups):
        group = own_group + at
        group = jnp.where(group >= groups, group - groups, group)
        mixed = mix_ref[:, pl.ds(group, 1)]
        mixed = mixed.astype(F32).reshape(total, mixed.shape[-1]).astype(BF16)
        after = after + matmul(mixed, row_out_ref[at])
    after = after.astype(BF16).astype(F32)
    permutation = residue_major(sequences, residues)
    normed = matmul(permutation, layer_normalize(after)).astype(BF16)
    queries = (matmul(normed, query_w_ref[...]) * query_factor).astype(BF16)
    keys = matmul(normed, key_w_ref[...]).astype(BF16)
    values = matmul(normed, vg_w_ref[0]).astype(BF16)
    gate = jax.nn.sigmoid(matmul(normed, vg_w_ref[1]))

    together = max(1, min(residues, 256 // sequences))
    span = together * sequences
    head_rows = heads * sequences
    inner = heads * PER_SPLIT_DIM
    block_diagonal = quotient(rows_of((head_rows, inner)), sequences) == quotient(
        lanes_of((head_rows, inner)), PER_SPLIT_DIM
    )
    zero = jnp.zeros((head_rows, inner), BF16)

    def by_head(part):
        return jnp.where(block_diagonal, jnp.concatenate([part] * heads, axis=0), zero)

    mixes = []
    for first in range(0, residues, together):
        base = first * sequences
        query_span = queries[base : base + span]
        owner = quotient(rows_of((span, inner)), sequences)
        scores = jnp.zeros((head_rows, span), F32)
        for at in range(together):
            key_part = by_head(keys[base + at * sequences : base + (at + 1) * sequences])
            query_part = jnp.where(owner == at, query_span, jnp.zeros_like(query_span))
            scores = scores + matmul_nt(key_part, query_part)
        spread = one_hot(
            rows_of((residues, span)) == first + quotient(lanes_of((residues, span)), sequences)
        )
        key_keep = matmul_tn(keep_ref[...].astype(BF16), spread)[:sequences]
        scores = scores.reshape(heads, sequences, span)
        scores = jnp.where(key_keep[None] > 0.5, scores, MASKED)
        scores = jnp.exp(scores - jnp.max(scores, axis=1, keepdims=True))
        weights = scores / jnp.sum(scores, axis=1, keepdims=True)
        weights = weights.reshape(head_rows, span).T.astype(BF16)
        for at in range(together):
            value_part = by_head(values[base + at * sequences : base + (at + 1) * sequences])
            mixes.append(matmul(weights[at * sequences : (at + 1) * sequences], value_part))
    mixed = (jnp.concatenate(mixes, axis=0) * gate).astype(BF16)
    mixed = matmul_tn(permutation, mixed).astype(BF16)
    result = after + matmul(mixed, out_w_ref[...])
    out_ref[...] = result.reshape(sequences, residues, width).astype(BF16)


def call(kernel, outs, scratch=(), scalars=0, arguments=(), mib=32):
    vmem = pl.BlockSpec(memory_space=pltpu.VMEM)
    smem = pl.BlockSpec(memory_space=pltpu.SMEM)
    return pl.pallas_call(
        kernel,
        out_shape=outs,
        in_specs=[smem] * scalars + [vmem] * (len(arguments) - scalars),
        out_specs=jax.tree.map(lambda _: vmem, outs),
        scratch_shapes=list(scratch),
        compiler_params=pltpu.CompilerParams(vmem_limit_bytes=mib * 1024 * 1024),
    )(*arguments)


def shards(
    homolog_activity,
    alignment_mask,
    sequence_row_mask,
    pairwise_bias,
    horizontal_projection_matrix,
    horizontal_final_matrix,
    column_query_weight,
    column_key_weight,
    vertical_content_sigmoid_matrix,
    vertical_final_matrix,
    first_operand_matrix,
    second_operand_matrix,
    outer_output_weight,
):
    parallel = lax.axis_size("dap")
    groups = lax.axis_size("grp")
    devices = parallel * groups
    sequences, residues, width = homolog_activity.shape
    residues_overall = residues * devices
    sequences_here = sequences // parallel
    heads, bias_rows, bias_columns = pairwise_bias.shape
    heads_here = heads // groups
    head_lanes = heads_here * PER_SPLIT_DIM
    channels = first_operand_matrix.shape[1]
    depth = outer_output_weight.shape[1]
    large = residues_overall > 256
    place = jnp.stack([lax.axis_index("dap"), lax.axis_index("grp")]).astype(jnp.int32)

    keep_slot = sequences_here * (width // LANES)
    tiles = keep_slot + 1 + heads_here * (bias_rows // residues) * (bias_columns // LANES)
    right_tiles = channels * sequences // LANES
    shape = jax.ShapeDtypeStruct
    rows_out, right_out, left, keep = call(
        functools.partial(prepare_kernel, (groups, sequences_here)),
        (
            shape((devices, tiles, residues, LANES), BF16),
            shape((devices, right_tiles, residues, LANES), BF16),
            shape((sequences * residues, channels), BF16),
            shape((residues, LANES), F32),
        ),
        arguments=(
            homolog_activity,
            alignment_mask.T,
            sequence_row_mask.reshape(1, sequences),
            pairwise_bias,
            first_operand_matrix,
            second_operand_matrix,
        ),
        mib=56 if large else 32,
    )
    both = ("dap", "grp")
    final_parts = [horizontal_final_matrix]
    for step in range(1, groups):
        final_parts.append(
            lax.ppermute(
                horizontal_final_matrix,
                "grp",
                [(source, (source - step) % groups) for source in range(groups)],
            )
        )
    row_out_weight = jnp.stack(final_parts)
    rows_in = lax.all_to_all(rows_out, both, split_axis=0, concat_axis=0, tiled=True)
    right_in = lax.all_to_all(right_out, both, split_axis=0, concat_axis=0, tiled=True)

    mix_out = call(
        functools.partial(row_kernel, (parallel, groups, sequences_here, heads_here)),
        shape((devices, sequences_here, residues, head_lanes), BF16),
        scratch=[pltpu.VMEM((sequences_here, residues_overall, head_lanes), BF16)] * 3
        + [pltpu.VMEM((sequences_here, residues_overall, head_lanes), F32)],
        scalars=1,
        arguments=(place, rows_in, horizontal_projection_matrix.transpose(1, 0, 2)),
        mib=56 if large else 32,
    )
    mix_in = lax.all_to_all(mix_out, both, split_axis=0, concat_axis=0, tiled=True)

    pairwise_update = call(
        functools.partial(outer_kernel, (keep_slot, sequences, 2)),
        shape((residues, residues_overall, depth), BF16),
        scratch=[pltpu.VMEM((residues, channels * sequences, depth), BF16)],
        arguments=(
            rows_in,
            right_in,
            left,
            keep,
            outer_output_weight.reshape(channels, channels, depth).transpose(1, 0, 2),
        ),
        mib=60 if large else 32,
    )

    alignment_output = call(
        functools.partial(column_kernel, groups),
        shape((sequences, residues, width), BF16),
        scalars=1,
        arguments=(
            place,
            homolog_activity,
            mix_in.reshape(parallel, groups, sequences_here, residues, head_lanes),
            keep,
            row_out_weight,
            column_query_weight,
            column_key_weight,
            vertical_content_sigmoid_matrix.transpose(1, 0, 2),
            vertical_final_matrix,
        ),
        mib=56 if large else 32,
    )
    return (alignment_output, pairwise_update)


def solution(mesh):
    return jax.shard_map(
        shards,
        mesh=mesh,
        in_specs=(
            P(None, ("dap", "grp"), None),
            P(None, ("dap", "grp")),
            P(),
            P(None, "dap", "grp"),
            P(None, None, "grp"),
            P("grp", None),
            P(),
            P(),
            P(),
            P(),
            P(),
            P(),
            P(),
        ),
        out_specs=(P(None, ("dap", "grp"), None), P(("dap", "grp"), None, None)),
        check_vma=False,
    )
```

```python
import functools

import jax
import jax.numpy as jnp
from jax import lax
from jax.experimental import pallas as pl
from jax.experimental.pallas import tpu as pltpu
from jax.sharding import PartitionSpec as P

PER_SPLIT_DIM = 32
LANES = 128
MASKED = -1000000000.0
F32 = jnp.float32
BF16 = jnp.bfloat16


def matmul(lhs, rhs):
    return jnp.dot(lhs, rhs, preferred_element_type=F32)


def matmul_nt(lhs, rhs):
    return lax.dot_general(lhs, rhs, (((1,), (1,)), ((), ())), preferred_element_type=F32)


def matmul_tn(lhs, rhs):
    return lax.dot_general(lhs, rhs, (((0,), (0,)), ((), ())), preferred_element_type=F32)


def rows_of(shape):
    return lax.broadcasted_iota(jnp.int32, shape, 0)


def lanes_of(shape):
    return lax.broadcasted_iota(jnp.int32, shape, 1)


def quotient(values, divisor):
    return lax.shift_right_logical(values, divisor.bit_length() - 1)


def remainder(values, divisor):
    return values & (divisor - 1)


def one_hot(condition):
    return condition.astype(F32).astype(BF16)


def flat_rows(tiles):
    blocks, sublanes, lanes = tiles.shape
    return tiles.astype(F32).reshape(blocks * sublanes, lanes).astype(BF16)


def layer_normalize(widened):
    centered = widened - jnp.mean(widened, axis=-1, keepdims=True)
    variance = jnp.mean(centered * centered, axis=-1, keepdims=True)
    return (centered * lax.rsqrt(variance + 1e-05)).astype(BF16)


def residue_major(sequences, residues):
    total = sequences * residues
    row, lane = rows_of((total, total)), lanes_of((total, total))
    return one_hot(lane == remainder(row, sequences) * residues + quotient(row, sequences))


def tile_count(bias_shape, groups):
    heads, bias_rows, bias_columns = bias_shape
    return heads // groups, bias_rows // 8, bias_columns // LANES


def share_kernel(groups, place_ref, mask_ref, present_ref, bias_ref, *out_refs):
    *piece_refs, keep_ref = out_refs
    heads_here, row_tiles, column_tiles = tile_count(bias_ref.shape, groups)
    sequences = mask_ref.shape[1]
    keep = (mask_ref[...] * present_ref[...]).astype(F32)
    if sequences < LANES:
        keep = jnp.pad(keep, ((0, 0), (0, LANES - sequences)))
    keep_ref[...] = keep
    own_group = place_ref[0] & (groups - 1)
    for relative, piece_ref in enumerate(piece_refs):
        group = own_group ^ relative
        slot = 0
        for head in range(heads_here):
            for row in range(row_tiles):
                for column in range(column_tiles):
                    piece_ref[slot] = bias_ref[
                        group * heads_here + head,
                        row * 8 : (row + 1) * 8,
                        column * LANES : (column + 1) * LANES,
                    ]
                    slot += 1
        piece_ref[slot] = keep.astype(BF16)


def prepare_kernel(
    sizes, x_ref, keep_ref, left_w_ref, right_w_ref, rows_ref, right_ref, left_ref
):
    groups, sequences_here = sizes
    sequences, residues, width = x_ref.shape
    total = sequences * residues
    channels = left_w_ref.shape[0]
    keep = keep_ref[:, :sequences]
    normed = layer_normalize(x_ref[...].astype(F32).reshape(total, width))
    normed_tiles = normed.astype(F32).reshape(sequences, residues, width).astype(BF16)
    halves = width // LANES
    for part in range(sequences // sequences_here):
        for own in range(sequences_here):
            for half in range(halves):
                for group in range(groups):
                    rows_ref[part * groups + group, own * halves + half] = normed_tiles[
                        part * sequences_here + own, :, half * LANES : (half + 1) * LANES
                    ]

    to_residue_major = residue_major(sequences, residues)
    left = matmul_nt(normed, left_w_ref[...]).astype(BF16)
    left = matmul(to_residue_major, left)
    pick = one_hot(
        quotient(rows_of((total, residues)), sequences) == lanes_of((total, residues))
    )
    own_keep = matmul(pick, keep.astype(BF16))
    at_sequence = remainder(rows_of((total, sequences)), sequences) == lanes_of((total, sequences))
    own_keep = jnp.sum(jnp.where(at_sequence, own_keep, 0.0), axis=1, keepdims=True)
    left_ref[...] = (left * own_keep).astype(BF16)

    right = matmul_nt(normed, right_w_ref[...]).astype(BF16)
    residue_pick = one_hot(
        remainder(lanes_of((residues, total)), residues) == rows_of((residues, total))
    )
    per_tile = LANES // sequences
    spread = one_hot(
        remainder(lanes_of((sequences, LANES)), sequences) == rows_of((sequences, LANES))
    )
    keep_spread = matmul(keep.astype(BF16), spread)
    same_sequence = quotient(rows_of((total, LANES)), residues) == remainder(
        lanes_of((total, LANES)), sequences
    )
    for tile in range(channels // per_tile):
        select = one_hot(
            rows_of((channels, LANES))
            == tile * per_tile + quotient(lanes_of((channels, LANES)), sequences)
        )
        expanded = jnp.where(same_sequence, matmul(right, select), 0.0).astype(BF16)
        right_ref[tile] = (matmul(residue_pick, expanded) * keep_spread).astype(BF16)


def sources(place, groups, pieces):
    for across in range(2):
        for core in range(2):
            for near in range(pieces):
                mask = near // groups * 4 * groups + near % groups
                yield across * 2 + core, near, place ^ (
                    mask + across * 2 * groups + core * groups
                )


def row_kernel(
    sizes, place_ref, rows_ref, piece0, piece1, piece2, piece3, weight_ref,
    mix_ref, keep_all_ref, bias_s, keep_s, query_s, key_s, value_s, gate_s,
):
    groups, sequences_here = sizes
    blocks, tiles, residues, _ = rows_ref.shape
    residues_overall = blocks * residues
    halves = weight_ref.shape[1] // LANES
    heads_here, all_columns, all_rows = bias_s.shape[:3]
    row_tiles = all_rows // (blocks // groups)
    column_tiles = all_columns // groups
    head_lanes = heads_here * PER_SPLIT_DIM
    query_factor = PER_SPLIT_DIM ** (-0.5)
    block_rows = min(residues_overall, 256)
    place = place_ref[0]
    pieces = (piece0, piece1, piece2, piece3)

    for own in range(sequences_here):
        normed = jnp.concatenate(
            [flat_rows(rows_ref[:, own * halves + half]) for half in range(halves)], axis=1
        )
        query_s[own] = (matmul(normed, weight_ref[0]) * query_factor).astype(BF16)
        key_s[own] = matmul(normed, weight_ref[1]).astype(BF16)
        value_s[own] = matmul(normed, weight_ref[2]).astype(BF16)
        gate_s[own] = jax.nn.sigmoid(matmul(normed, weight_ref[3]))

    for stack, near, source in sources(place, groups, piece0.shape[0]):
        group = source & (groups - 1)
        part = quotient(source, groups)
        slot = 0
        for head in range(heads_here):
            for row in range(row_tiles):
                for column in range(column_tiles):
                    bias_s[head, group * column_tiles + column, part * row_tiles + row] = pieces[
                        stack
                    ][near, slot]
                    slot += 1
        keep_s[source] = pieces[stack][near, slot]

    keep_all = flat_rows(keep_s[...])
    keep_all_ref[...] = keep_all
    chosen = one_hot(
        lanes_of((8, LANES)) == quotient(place, groups) * sequences_here + rows_of((8, LANES))
    )
    key_keep = matmul_nt(chosen, keep_all)

    def attend(block):
        start = block * block_rows
        count = block_rows // 8
        head_of = quotient(lanes_of((residues_overall, head_lanes)), PER_SPLIT_DIM)
        query_head = quotient(lanes_of((block_rows, head_lanes)), PER_SPLIT_DIM)
        biases = []
        for head in range(heads_here):
            columns = [
                bias_s[head, column, pl.ds(block * count, count)]
                .astype(F32)
                .reshape(block_rows, LANES)
                for column in range(all_columns)
            ]
            biases.append(jnp.concatenate(columns, axis=1))
        for own in range(sequences_here):
            queries = query_s[own, pl.ds(start, block_rows), :]
            keys, values = key_s[own], value_s[own]
            keep_row = key_keep[own : own + 1, :] > 0.5
            total = jnp.zeros((block_rows, 2 * head_lanes), F32)
            for head in range(heads_here):
                query_part = jnp.where(query_head == head, queries, jnp.zeros_like(queries))
                scores = matmul_nt(query_part, keys) + biases[head]
                scores = jnp.where(keep_row, scores, MASKED)
                scores = scores - jnp.max(scores, axis=1, keepdims=True)
                weights = jnp.exp(scores).astype(BF16)
                mine = head_of == head
                value_part = jnp.where(mine, values, jnp.zeros_like(values))
                total = total + matmul(
                    weights, jnp.concatenate([value_part, one_hot(mine)], axis=1)
                )
            mixed = total[:, :head_lanes] / total[:, head_lanes:]
            mixed = mixed * gate_s[own, pl.ds(start, block_rows), :]
            mix_ref[pl.ds(block * (block_rows // residues), block_rows // residues), own] = (
                mixed.reshape(block_rows // residues, residues, head_lanes).astype(BF16)
            )

    if residues_overall == block_rows:
        attend(0)
    else:
        pl.loop(0, residues_overall // block_rows)(attend)


def outer_kernel(
    sizes, place_ref, keep_all_ref, piece0, piece1, piece2, piece3, left_ref, keep_ref,
    weight_ref, out_ref, mixed_s, right_s,
):
    groups, sequences, pair = sizes
    right_tiles = right_s.shape[1]
    residues = keep_ref.shape[0]
    channels, _, depth = weight_ref.shape
    left = left_ref[...]
    per_step = 2 if depth == LANES else 1
    for channel in range(0, channels, per_step):
        weights = jnp.concatenate(
            [weight_ref[channel + at] for at in range(per_step)], axis=1
        )
        product = matmul(left, weights).astype(BF16)
        for residue in range(residues):
            for at in range(per_step):
                mixed_s[
                    residue, (channel + at) * sequences : (channel + at + 1) * sequences, :
                ] = product[
                    residue * sequences : (residue + 1) * sequences, at * depth : (at + 1) * depth
                ]
    pieces = (piece0, piece1, piece2, piece3)
    for stack, near, source in sources(place_ref[0], groups, piece0.shape[0]):
        right_s[source] = pieces[stack][near]
    right = jnp.concatenate(
        [flat_rows(right_s[:, tile]) for tile in range(right_tiles)], axis=1
    )
    keep_all = keep_all_ref[...]
    for first in range(0, residues, pair):
        members = range(first, first + pair)
        mixed = jnp.concatenate([mixed_s[residue] for residue in members], axis=1)
        keep_rows = jnp.concatenate(
            [
                jnp.broadcast_to(keep_ref[residue : residue + 1, :], (depth, LANES))
                for residue in members
            ],
            axis=0,
        ).astype(BF16)
        result = matmul(right, mixed) / matmul_nt(keep_all, keep_rows)
        for at, residue in enumerate(members):
            out_ref[residue] = result[:, at * depth : (at + 1) * depth].astype(BF16)


def column_kernel(
    sizes, place_ref, x_ref, mix_ref, keep_ref, row_out_ref, query_w_ref, key_w_ref, vg_w_ref,
    out_w_ref, out_ref,
):
    groups = sizes
    sequences, residues, width = x_ref.shape
    total = sequences * residues
    heads = query_w_ref.shape[1] // PER_SPLIT_DIM
    query_factor = PER_SPLIT_DIM ** (-0.5)
    own_group = place_ref[0] & (groups - 1)
    after = x_ref[...].astype(F32).reshape(total, width)
    for at in range(groups):
        group = own_group ^ at
        mixed = mix_ref[:, pl.ds(group, 1)]
        mixed = mixed.astype(F32).reshape(total, mixed.shape[-1]).astype(BF16)
        after = after + matmul(mixed, row_out_ref[at])
    after = after.astype(BF16).astype(F32)
    permutation = residue_major(sequences, residues)
    normed = matmul(permutation, layer_normalize(after)).astype(BF16)
    queries = (matmul(normed, query_w_ref[...]) * query_factor).astype(BF16)
    keys = matmul(normed, key_w_ref[...]).astype(BF16)
    values = matmul(normed, vg_w_ref[0]).astype(BF16)
    gate = jax.nn.sigmoid(matmul(normed, vg_w_ref[1]))

    together = max(1, min(residues, 256 // sequences))
    span = together * sequences
    head_rows = heads * sequences
    inner = heads * PER_SPLIT_DIM
    block_diagonal = quotient(rows_of((head_rows, inner)), sequences) == quotient(
        lanes_of((head_rows, inner)), PER_SPLIT_DIM
    )
    zero = jnp.zeros((head_rows, inner), BF16)

    def by_head(part):
        return jnp.where(block_diagonal, jnp.concatenate([part] * heads, axis=0), zero)

    mixes = []
    for first in range(0, residues, together):
        base = first * sequences
        query_span = queries[base : base + span]
        owner = quotient(rows_of((span, inner)), sequences)
        scores = jnp.zeros((head_rows, span), F32)
        for at in range(together):
            key_part = by_head(keys[base + at * sequences : base + (at + 1) * sequences])
            query_part = jnp.where(owner == at, query_span, jnp.zeros_like(query_span))
            scores = scores + matmul_nt(key_part, query_part)
        spread = one_hot(
            rows_of((residues, span)) == first + quotient(lanes_of((residues, span)), sequences)
        )
        key_keep = matmul_tn(keep_ref[...].astype(BF16), spread)[:sequences]
        scores = scores.reshape(heads, sequences, span)
        scores = jnp.where(key_keep[None] > 0.5, scores, MASKED)
        scores = jnp.exp(scores - jnp.max(scores, axis=1, keepdims=True))
        weights = scores / jnp.sum(scores, axis=1, keepdims=True)
        weights = weights.reshape(head_rows, span).T.astype(BF16)
        for at in range(together):
            value_part = by_head(values[base + at * sequences : base + (at + 1) * sequences])
            mixes.append(matmul(weights[at * sequences : (at + 1) * sequences], value_part))
    mixed = (jnp.concatenate(mixes, axis=0) * gate).astype(BF16)
    mixed = matmul_tn(permutation, mixed).astype(BF16)
    result = after + matmul(mixed, out_w_ref[...])
    out_ref[...] = result.reshape(sequences, residues, width).astype(BF16)


def call(kernel, outs, arguments, scratch=(), scalars=0, mib=32, micros=2):
    vmem = pl.BlockSpec(memory_space=pltpu.VMEM)
    smem = pl.BlockSpec(memory_space=pltpu.SMEM)
    return pl.pallas_call(
        kernel,
        out_shape=outs,
        in_specs=[smem] * scalars + [vmem] * (len(arguments) - scalars),
        out_specs=jax.tree.map(lambda _: vmem, outs),
        scratch_shapes=list(scratch),
        compiler_params=pltpu.CompilerParams(vmem_limit_bytes=mib * 1024 * 1024),
        cost_estimate=pl.CostEstimate(
            flops=micros * 1_000_000_000, bytes_accessed=micros * 1_000_000, transcendentals=0
        ),
    )(*arguments)


def shards(
    homolog_activity,
    alignment_mask,
    sequence_row_mask,
    pairwise_bias,
    horizontal_projection_matrix,
    horizontal_final_matrix,
    column_query_weight,
    column_key_weight,
    vertical_content_sigmoid_matrix,
    vertical_final_matrix,
    first_operand_matrix,
    second_operand_matrix,
    outer_output_weight,
):
    parallel = lax.axis_size("dap")
    groups = lax.axis_size("grp")
    devices = parallel * groups
    both = ("dap", "grp")
    sequences, residues, width = homolog_activity.shape
    residues_overall = residues * devices
    sequences_here = sequences // parallel
    channels = first_operand_matrix.shape[1]
    depth = outer_output_weight.shape[1]
    heads_here, row_tiles, column_tiles = tile_count(pairwise_bias.shape, groups)
    head_lanes = heads_here * PER_SPLIT_DIM
    large = residues_overall > 256
    near_pieces = parallel // 4 * groups
    place = (lax.axis_index("dap") * groups + lax.axis_index("grp")).astype(jnp.int32).reshape(1)
    shape = jax.ShapeDtypeStruct

    def exchange(value, mask):
        return lax.ppermute(value, both, [(at, at ^ mask) for at in range(devices)])

    def gather(pieces):
        parts = [pieces[0]]
        for near in range(1, near_pieces):
            mask = near // groups * 4 * groups + near % groups
            parts.append(exchange(pieces[near % groups], mask))
        own = jnp.stack(parts)
        across = exchange(own, 2 * groups)
        return own, exchange(own, groups), across, exchange(across, groups)

    bias_tiles = heads_here * row_tiles * column_tiles
    *bias_pieces, keep = call(
        functools.partial(share_kernel, groups),
        tuple([shape((bias_tiles + 1, 8, LANES), BF16)] * groups + [shape((8, LANES), F32)]),
        (place, alignment_mask.T, sequence_row_mask.reshape(1, sequences), pairwise_bias),
        scalars=1,
        micros=1,
    )
    bias_stacks = gather(bias_pieces)
    row_out_weight = jnp.stack(
        [horizontal_final_matrix]
        + [exchange(horizontal_final_matrix, relative) for relative in range(1, groups)]
    )

    right_tiles = channels * sequences // LANES
    rows_out, right_piece, left = call(
        functools.partial(prepare_kernel, (groups, sequences_here)),
        (
            shape((devices, sequences_here * (width // LANES), residues, LANES), BF16),
            shape((right_tiles, residues, LANES), BF16),
            shape((sequences * residues, channels), BF16),
        ),
        (homolog_activity, keep, first_operand_matrix.T, second_operand_matrix.T),
        mib=56 if large else 32,
    )
    rows_in = lax.all_to_all(rows_out, both, split_axis=0, concat_axis=0, tiled=True)
    right_stacks = gather([right_piece] * groups)

    mix_out, keep_all = call(
        functools.partial(row_kernel, (groups, sequences_here)),
        (
            shape((devices, sequences_here, residues, head_lanes), BF16),
            shape((residues_overall, LANES), BF16),
        ),
        (place, rows_in, *bias_stacks, horizontal_projection_matrix.transpose(1, 0, 2)),
        scratch=[
            pltpu.VMEM(
                (heads_here, groups * column_tiles, parallel * row_tiles, 8, LANES), BF16
            ),
            pltpu.VMEM((devices, 8, LANES), BF16),
        ]
        + [pltpu.VMEM((sequences_here, residues_overall, head_lanes), BF16)] * 3
        + [pltpu.VMEM((sequences_here, residues_overall, head_lanes), F32)],
        scalars=1,
        mib=60 if large else 32,
    )
    mix_in = lax.all_to_all(mix_out, both, split_axis=0, concat_axis=0, tiled=True)

    pairwise_update = call(
        functools.partial(outer_kernel, (groups, sequences, 2)),
        shape((residues, residues_overall, depth), BF16),
        (
            place,
            keep_all,
            *right_stacks,
            left,
            keep,
            outer_output_weight.reshape(channels, channels, depth).transpose(1, 0, 2),
        ),
        scratch=[
            pltpu.VMEM((residues, channels * sequences, depth), BF16),
            pltpu.VMEM((devices, right_tiles, residues, LANES), BF16),
        ],
        scalars=1,
        mib=60 if large else 32,
    )

    alignment_output = call(
        functools.partial(column_kernel, groups),
        shape((sequences, residues, width), BF16),
        (
            place,
            homolog_activity,
            mix_in.reshape(parallel, groups, sequences_here, residues, head_lanes),
            keep,
            row_out_weight,
            column_query_weight,
            column_key_weight,
            vertical_content_sigmoid_matrix.transpose(1, 0, 2),
            vertical_final_matrix,
        ),
        scalars=1,
        mib=56 if large else 32,
        micros=3,
    )
    return (alignment_output, pairwise_update)


def solution(mesh):
    return jax.shard_map(
        shards,
        mesh=mesh,
        in_specs=(
            P(None, ("dap", "grp"), None),
            P(None, ("dap", "grp")),
            P(),
            P(None, "dap", "grp"),
            P(None, None, "grp"),
            P("grp", None),
            P(),
            P(),
            P(),
            P(),
            P(),
            P(),
            P(),
        ),
        out_specs=(P(None, ("dap", "grp"), None), P(("dap", "grp"), None, None)),
        check_vma=False,
    )
```

```python
import functools

import jax
import jax.numpy as jnp
from jax import lax
from jax.experimental import pallas as pl
from jax.experimental.pallas import tpu as pltpu
from jax.sharding import PartitionSpec as P

PER_SPLIT_DIM = 32
LANES = 128
MASKED = -1000000000.0
F32 = jnp.float32
BF16 = jnp.bfloat16


def matmul(lhs, rhs):
    return jnp.dot(lhs, rhs, preferred_element_type=F32)


def matmul_nt(lhs, rhs):
    return lax.dot_general(lhs, rhs, (((1,), (1,)), ((), ())), preferred_element_type=F32)


def matmul_tn(lhs, rhs):
    return lax.dot_general(lhs, rhs, (((0,), (0,)), ((), ())), preferred_element_type=F32)


def rows_of(shape):
    return lax.broadcasted_iota(jnp.int32, shape, 0)


def lanes_of(shape):
    return lax.broadcasted_iota(jnp.int32, shape, 1)


def quotient(values, divisor):
    return lax.shift_right_logical(values, divisor.bit_length() - 1)


def remainder(values, divisor):
    return values & (divisor - 1)


def one_hot(condition):
    return condition.astype(F32).astype(BF16)


def flat_rows(tiles):
    blocks, sublanes, lanes = tiles.shape
    return tiles.astype(F32).reshape(blocks * sublanes, lanes).astype(BF16)


def layer_normalize(widened):
    centered = widened - jnp.mean(widened, axis=-1, keepdims=True)
    variance = jnp.mean(centered * centered, axis=-1, keepdims=True)
    return (centered * lax.rsqrt(variance + 1e-05)).astype(BF16)


def residue_major(sequences, residues):
    total = sequences * residues
    row, lane = rows_of((total, total)), lanes_of((total, total))
    return one_hot(lane == remainder(row, sequences) * residues + quotient(row, sequences))


def tile_count(bias_shape, groups):
    heads, bias_rows, bias_columns = bias_shape
    return heads // groups, bias_rows // 8, bias_columns // LANES


def share_kernel(groups, mask_ref, present_ref, bias_ref, out_ref, keep_ref):
    heads_here, row_tiles, column_tiles = tile_count(bias_ref.shape, groups)
    half_heads = heads_here // 2
    sequences = mask_ref.shape[1]
    keep = (mask_ref[...] * present_ref[...]).astype(F32)
    if sequences < LANES:
        keep = jnp.pad(keep, ((0, 0), (0, LANES - sequences)))
    keep_ref[...] = keep
    keep_tile = keep.astype(BF16)
    for target in range(out_ref.shape[0]):
        part, group = divmod(target, groups)
        slot = 0
        for head in range(half_heads):
            for row in range(row_tiles):
                for column in range(column_tiles):
                    out_ref[target, slot] = bias_ref[
                        group * heads_here + part % 2 * half_heads + head,
                        row * 8 : (row + 1) * 8,
                        column * LANES : (column + 1) * LANES,
                    ]
                    slot += 1
        out_ref[target, slot] = keep_tile


def prepare_kernel(
    sizes, x_ref, keep_ref, left_w_ref, right_w_ref, rows_ref, right_ref, left_ref
):
    groups, sequences_here = sizes
    sequences, residues, width = x_ref.shape
    total = sequences * residues
    channels = left_w_ref.shape[0]
    keep = keep_ref[:, :sequences]
    normed = layer_normalize(x_ref[...].astype(F32).reshape(total, width))
    normed_tiles = normed.astype(F32).reshape(sequences, residues, width).astype(BF16)
    halves = width // LANES
    for part in range(sequences // sequences_here):
        for own in range(sequences_here):
            for half in range(halves):
                for group in range(groups):
                    rows_ref[part * groups + group, own * halves + half] = normed_tiles[
                        part * sequences_here + own, :, half * LANES : (half + 1) * LANES
                    ]

    to_residue_major = residue_major(sequences, residues)
    left = matmul_nt(normed, left_w_ref[...]).astype(BF16)
    left = matmul(to_residue_major, left)
    pick = one_hot(
        quotient(rows_of((total, residues)), sequences) == lanes_of((total, residues))
    )
    own_keep = matmul(pick, keep.astype(BF16))
    at_sequence = remainder(rows_of((total, sequences)), sequences) == lanes_of((total, sequences))
    own_keep = jnp.sum(jnp.where(at_sequence, own_keep, 0.0), axis=1, keepdims=True)
    left_ref[...] = (left * own_keep).astype(BF16)

    right = matmul_nt(normed, right_w_ref[...]).astype(BF16)
    residue_pick = one_hot(
        remainder(lanes_of((residues, total)), residues) == rows_of((residues, total))
    )
    per_tile = LANES // sequences
    spread = one_hot(
        remainder(lanes_of((sequences, LANES)), sequences) == rows_of((sequences, LANES))
    )
    keep_spread = matmul(keep.astype(BF16), spread)
    same_sequence = quotient(rows_of((total, LANES)), residues) == remainder(
        lanes_of((total, LANES)), sequences
    )
    for tile in range(channels // per_tile):
        select = one_hot(
            rows_of((channels, LANES))
            == tile * per_tile + quotient(lanes_of((channels, LANES)), sequences)
        )
        expanded = jnp.where(same_sequence, matmul(right, select), 0.0).astype(BF16)
        result = (matmul(residue_pick, expanded) * keep_spread).astype(BF16)
        core, slot = divmod(tile, right_ref.shape[1])
        for target in range(right_ref.shape[0]):
            if target // groups % 2 == core:
                right_ref[target, slot] = result


def row_kernel(
    sizes, place_ref, own_bias_ref, other_bias_ref, rows_ref, weight_ref,
    mix_ref, keep_all_ref, query_s, key_s, value_s, gate_s,
):
    groups, sequences_here, row_tiles, column_tiles = sizes
    blocks, tiles, residues, _ = rows_ref.shape
    residues_overall = blocks * residues
    halves = weight_ref.shape[1] // LANES
    head_lanes = weight_ref.shape[2]
    half_heads = head_lanes // PER_SPLIT_DIM // 2
    query_factor = PER_SPLIT_DIM ** (-0.5)
    block_rows = min(residues_overall, 256)
    part = quotient(place_ref[0], groups)
    core = part & 1

    for own in range(sequences_here):
        normed = jnp.concatenate(
            [flat_rows(rows_ref[:, own * halves + half]) for half in range(halves)], axis=1
        )
        query_s[own] = (matmul(normed, weight_ref[0]) * query_factor).astype(BF16)
        key_s[own] = matmul(normed, weight_ref[1]).astype(BF16)
        value_s[own] = matmul(normed, weight_ref[2]).astype(BF16)
        gate_s[own] = jax.nn.sigmoid(matmul(normed, weight_ref[3]))

    keep_all = flat_rows(own_bias_ref[:, half_heads * row_tiles * column_tiles])
    keep_all_ref[...] = keep_all
    chosen = one_hot(lanes_of((8, LANES)) == part * sequences_here + rows_of((8, LANES)))
    key_keep = matmul_nt(chosen, keep_all)

    def attend(block):
        start = block * block_rows
        parts = block_rows // (row_tiles * 8)
        head_of = quotient(lanes_of((residues_overall, head_lanes)), PER_SPLIT_DIM)
        query_head = quotient(lanes_of((block_rows, head_lanes)), PER_SPLIT_DIM)
        biases = []
        for bias_ref in (own_bias_ref, other_bias_ref):
            for head in range(half_heads):
                columns = []
                for group in range(groups):
                    for column in range(column_tiles):
                        pieces = []
                        for at in range(parts):
                            for row in range(row_tiles):
                                slot = (head * row_tiles + row) * column_tiles + column
                                source = (block * parts + at) * groups + group
                                pieces.append(bias_ref[source, slot].astype(F32))
                        columns.append(jnp.concatenate(pieces, axis=0))
                biases.append(jnp.concatenate(columns, axis=1))
        for own in range(sequences_here):
            queries = query_s[own, pl.ds(start, block_rows), :]
            keys, values = key_s[own], value_s[own]
            keep_row = key_keep[own : own + 1, :] > 0.5
            total = jnp.zeros((block_rows, 2 * head_lanes), F32)
            for at in range(2 * half_heads):
                head = (core ^ (at // half_heads)) * half_heads + at % half_heads
                query_part = jnp.where(query_head == head, queries, jnp.zeros_like(queries))
                scores = matmul_nt(query_part, keys) + biases[at]
                scores = jnp.where(keep_row, scores, MASKED)
                scores = scores - jnp.max(scores, axis=1, keepdims=True)
                weights = jnp.exp(scores).astype(BF16)
                mine = head_of == head
                value_part = jnp.where(mine, values, jnp.zeros_like(values))
                total = total + matmul(
                    weights, jnp.concatenate([value_part, one_hot(mine)], axis=1)
                )
            mixed = total[:, :head_lanes] / total[:, head_lanes:]
            mixed = mixed * gate_s[own, pl.ds(start, block_rows), :]
            mix_ref[pl.ds(block * (block_rows // residues), block_rows // residues), own] = (
                mixed.reshape(block_rows // residues, residues, head_lanes).astype(BF16)
            )

    if residues_overall == block_rows:
        attend(0)
    else:
        pl.loop(0, residues_overall // block_rows)(attend)


def outer_kernel(
    sizes, place_ref, keep_all_ref, own_right_ref, other_right_ref, left_ref, keep_ref,
    weight_ref, out_ref, mixed_s,
):
    groups, sequences, pair = sizes
    residues = keep_ref.shape[0]
    channels, _, depth = weight_ref.shape
    core = quotient(place_ref[0], groups) & 1
    left = left_ref[...]
    half_channels = channels // 2
    for at in range(0, channels, 2):
        channel = (core ^ (at // half_channels)) * half_channels + at % half_channels
        weights = jnp.concatenate([weight_ref[channel], weight_ref[channel + 1]], axis=1)
        product = matmul(left, weights).astype(BF16)
        for residue in range(residues):
            for step in range(2):
                mixed_s[residue, (at + step) * sequences : (at + step + 1) * sequences, :] = product[
                    residue * sequences : (residue + 1) * sequences,
                    step * depth : (step + 1) * depth,
                ]
    right = jnp.concatenate(
        [
            flat_rows(right_ref[:, tile])
            for right_ref in (own_right_ref, other_right_ref)
            for tile in range(right_ref.shape[1])
        ],
        axis=1,
    )
    keep_all = keep_all_ref[...]
    for first in range(0, residues, pair):
        members = range(first, first + pair)
        mixed = jnp.concatenate([mixed_s[residue] for residue in members], axis=1)
        keep_rows = jnp.concatenate(
            [
                jnp.broadcast_to(keep_ref[residue : residue + 1, :], (depth, LANES))
                for residue in members
            ],
            axis=0,
        ).astype(BF16)
        result = matmul(right, mixed) / matmul_nt(keep_all, keep_rows)
        for at, residue in enumerate(members):
            out_ref[residue] = result[:, at * depth : (at + 1) * depth].astype(BF16)


def column_kernel(
    sizes, place_ref, x_ref, mix_ref, keep_ref, row_out_ref, query_w_ref, key_w_ref, vg_w_ref,
    out_w_ref, out_ref,
):
    groups = sizes
    sequences, residues, width = x_ref.shape
    total = sequences * residues
    heads = query_w_ref.shape[1] // PER_SPLIT_DIM
    query_factor = PER_SPLIT_DIM ** (-0.5)
    own_group = place_ref[0] & (groups - 1)
    after = x_ref[...].astype(F32).reshape(total, width)
    for at in range(groups):
        group = own_group ^ at
        mixed = mix_ref[:, pl.ds(group, 1)]
        mixed = mixed.astype(F32).reshape(total, mixed.shape[-1]).astype(BF16)
        after = after + matmul(mixed, row_out_ref[at])
    after = after.astype(BF16).astype(F32)
    permutation = residue_major(sequences, residues)
    normed = matmul(permutation, layer_normalize(after)).astype(BF16)
    queries = (matmul(normed, query_w_ref[...]) * query_factor).astype(BF16)
    keys = matmul(normed, key_w_ref[...]).astype(BF16)
    values = matmul(normed, vg_w_ref[0]).astype(BF16)
    gate = jax.nn.sigmoid(matmul(normed, vg_w_ref[1]))

    together = max(1, min(residues, 256 // sequences))
    span = together * sequences
    head_rows = heads * sequences
    inner = heads * PER_SPLIT_DIM
    block_diagonal = quotient(rows_of((head_rows, inner)), sequences) == quotient(
        lanes_of((head_rows, inner)), PER_SPLIT_DIM
    )
    zero = jnp.zeros((head_rows, inner), BF16)

    def by_head(part):
        return jnp.where(block_diagonal, jnp.concatenate([part] * heads, axis=0), zero)

    mixes = []
    for first in range(0, residues, together):
        base = first * sequences
        query_span = queries[base : base + span]
        owner = quotient(rows_of((span, inner)), sequences)
        scores = jnp.zeros((head_rows, span), F32)
        for at in range(together):
            key_part = by_head(keys[base + at * sequences : base + (at + 1) * sequences])
            query_part = jnp.where(owner == at, query_span, jnp.zeros_like(query_span))
            scores = scores + matmul_nt(key_part, query_part)
        spread = one_hot(
            rows_of((residues, span)) == first + quotient(lanes_of((residues, span)), sequences)
        )
        key_keep = matmul_tn(keep_ref[...].astype(BF16), spread)[:sequences]
        scores = scores.reshape(heads, sequences, span)
        scores = jnp.where(key_keep[None] > 0.5, scores, MASKED)
        scores = jnp.exp(scores - jnp.max(scores, axis=1, keepdims=True))
        weights = scores / jnp.sum(scores, axis=1, keepdims=True)
        weights = weights.reshape(head_rows, span).T.astype(BF16)
        for at in range(together):
            value_part = by_head(values[base + at * sequences : base + (at + 1) * sequences])
            mixes.append(matmul(weights[at * sequences : (at + 1) * sequences], value_part))
    mixed = (jnp.concatenate(mixes, axis=0) * gate).astype(BF16)
    mixed = matmul_tn(permutation, mixed).astype(BF16)
    result = after + matmul(mixed, out_w_ref[...])
    out_ref[...] = result.reshape(sequences, residues, width).astype(BF16)


def call(kernel, outs, arguments, scratch=(), scalars=0, mib=32, micros=2, loose=False):
    vmem = pl.BlockSpec(memory_space=pltpu.VMEM)
    read = pl.BlockSpec() if loose else vmem
    smem = pl.BlockSpec(memory_space=pltpu.SMEM)
    return pl.pallas_call(
        kernel,
        out_shape=outs,
        in_specs=[smem] * scalars + [read] * (len(arguments) - scalars),
        out_specs=jax.tree.map(lambda _: vmem, outs),
        scratch_shapes=list(scratch),
        compiler_params=pltpu.CompilerParams(vmem_limit_bytes=mib * 1024 * 1024),
        cost_estimate=pl.CostEstimate(
            flops=micros * 1_000_000_000, bytes_accessed=micros * 1_000_000, transcendentals=0
        ),
    )(*arguments)


def shards(
    homolog_activity,
    alignment_mask,
    sequence_row_mask,
    pairwise_bias,
    horizontal_projection_matrix,
    horizontal_final_matrix,
    column_query_weight,
    column_key_weight,
    vertical_content_sigmoid_matrix,
    vertical_final_matrix,
    first_operand_matrix,
    second_operand_matrix,
    outer_output_weight,
):
    parallel = lax.axis_size("dap")
    groups = lax.axis_size("grp")
    devices = parallel * groups
    both = ("dap", "grp")
    sequences, residues, width = homolog_activity.shape
    residues_overall = residues * devices
    sequences_here = sequences // parallel
    channels = first_operand_matrix.shape[1]
    depth = outer_output_weight.shape[1]
    heads_here, row_tiles, column_tiles = tile_count(pairwise_bias.shape, groups)
    head_lanes = heads_here * PER_SPLIT_DIM
    large = residues_overall > 256
    place = (lax.axis_index("dap") * groups + lax.axis_index("grp")).astype(jnp.int32).reshape(1)
    shape = jax.ShapeDtypeStruct

    def exchange(value, mask):
        return lax.ppermute(value, both, [(at, at ^ mask) for at in range(devices)])

    def to_all(value):
        return lax.all_to_all(value, both, split_axis=0, concat_axis=0, tiled=True)

    half_tiles = heads_here // 2 * row_tiles * column_tiles
    bias_out, keep = call(
        functools.partial(share_kernel, groups),
        (shape((devices, half_tiles + 1, 8, LANES), BF16), shape((8, LANES), F32)),
        (alignment_mask.T, sequence_row_mask.reshape(1, sequences), pairwise_bias),
        micros=1,
        loose=True,
    )
    own_bias = to_all(bias_out)
    other_bias = exchange(own_bias, groups)
    row_out_weight = jnp.stack(
        [horizontal_final_matrix]
        + [exchange(horizontal_final_matrix, relative) for relative in range(1, groups)]
    )

    right_tiles = channels * sequences // LANES
    rows_out, right_out, left = call(
        functools.partial(prepare_kernel, (groups, sequences_here)),
        (
            shape((devices, sequences_here * (width // LANES), residues, LANES), BF16),
            shape((devices, right_tiles // 2, residues, LANES), BF16),
            shape((sequences * residues, channels), BF16),
        ),
        (homolog_activity, keep, first_operand_matrix.T, second_operand_matrix.T),
        mib=56 if large else 32,
    )
    rows_in = to_all(rows_out)
    own_right = to_all(right_out)
    other_right = exchange(own_right, groups)

    mix_out, keep_all = call(
        functools.partial(row_kernel, (groups, sequences_here, row_tiles, column_tiles)),
        (
            shape((devices, sequences_here, residues, head_lanes), BF16),
            shape((residues_overall, LANES), BF16),
        ),
        (
            place,
            own_bias,
            other_bias,
            rows_in,
            horizontal_projection_matrix.transpose(1, 0, 2),
        ),
        scratch=[pltpu.VMEM((sequences_here, residues_overall, head_lanes), BF16)] * 3
        + [pltpu.VMEM((sequences_here, residues_overall, head_lanes), F32)],
        scalars=1,
        mib=60 if large else 32,
    )
    mix_in = to_all(mix_out)

    pairwise_update = call(
        functools.partial(outer_kernel, (groups, sequences, 2)),
        shape((residues, residues_overall, depth), BF16),
        (
            place,
            keep_all,
            own_right,
            other_right,
            left,
            keep,
            outer_output_weight.reshape(channels, channels, depth).transpose(1, 0, 2),
        ),
        scratch=[pltpu.VMEM((residues, channels * sequences, depth), BF16)],
        scalars=1,
        mib=60 if large else 32,
    )

    alignment_output = call(
        functools.partial(column_kernel, groups),
        shape((sequences, residues, width), BF16),
        (
            place,
            homolog_activity,
            mix_in.reshape(parallel, groups, sequences_here, residues, head_lanes),
            keep,
            row_out_weight,
            column_query_weight,
            column_key_weight,
            vertical_content_sigmoid_matrix.transpose(1, 0, 2),
            vertical_final_matrix,
        ),
        scalars=1,
        mib=56 if large else 32,
        micros=3,
    )
    return (alignment_output, pairwise_update)


def solution(mesh):
    return jax.shard_map(
        shards,
        mesh=mesh,
        in_specs=(
            P(None, ("dap", "grp"), None),
            P(None, ("dap", "grp")),
            P(),
            P(None, "dap", "grp"),
            P(None, None, "grp"),
            P("grp", None),
            P(),
            P(),
            P(),
            P(),
            P(),
            P(),
            P(),
        ),
        out_specs=(P(None, ("dap", "grp"), None), P(("dap", "grp"), None, None)),
        check_vma=False,
    )
```

```python
import functools

import jax
import jax.numpy as jnp
from jax import lax
from jax.experimental import pallas as pl
from jax.experimental.pallas import tpu as pltpu
from jax.sharding import PartitionSpec as P

PER_SPLIT_DIM = 32
LANES = 128
MASKED = -1000000000.0
F32 = jnp.float32
BF16 = jnp.bfloat16


def matmul(lhs, rhs):
    return jnp.dot(lhs, rhs, preferred_element_type=F32)


def matmul_nt(lhs, rhs):
    return lax.dot_general(lhs, rhs, (((1,), (1,)), ((), ())), preferred_element_type=F32)


def matmul_tn(lhs, rhs):
    return lax.dot_general(lhs, rhs, (((0,), (0,)), ((), ())), preferred_element_type=F32)


def rows_of(shape):
    return lax.broadcasted_iota(jnp.int32, shape, 0)


def lanes_of(shape):
    return lax.broadcasted_iota(jnp.int32, shape, 1)


def quotient(values, divisor):
    return lax.shift_right_logical(values, divisor.bit_length() - 1)


def remainder(values, divisor):
    return values & (divisor - 1)


def one_hot(condition):
    return condition.astype(F32).astype(BF16)


def flat_rows(tiles):
    blocks, sublanes, lanes = tiles.shape
    return tiles.astype(F32).reshape(blocks * sublanes, lanes).astype(BF16)


def layer_normalize(widened):
    centered = widened - jnp.mean(widened, axis=-1, keepdims=True)
    variance = jnp.mean(centered * centered, axis=-1, keepdims=True)
    return (centered * lax.rsqrt(variance + 1e-05)).astype(BF16)


def residue_major(sequences, residues):
    total = sequences * residues
    row, lane = rows_of((total, total)), lanes_of((total, total))
    return one_hot(lane == remainder(row, sequences) * residues + quotient(row, sequences))


def tile_count(bias_shape, groups):
    heads, bias_rows, bias_columns = bias_shape
    return heads // groups, bias_rows // 8, bias_columns // LANES


def share_kernel(
    groups, mask_hbm, present_hbm, bias_hbm, out_ref, keep_ref, mask_ref, present_ref, bias_ref,
    sems,
):
    pairs = ((bias_hbm, bias_ref), (mask_hbm, mask_ref), (present_hbm, present_ref))
    copies = [
        pltpu.make_async_copy(source, target, sems.at[at])
        for at, (source, target) in enumerate(pairs)
    ]
    for copy in copies:
        copy.start()
    for copy in copies:
        copy.wait()
    heads_here, row_tiles, column_tiles = tile_count(bias_ref.shape, groups)
    half_heads = heads_here // 2
    sequences = mask_ref.shape[1]
    keep = (mask_ref[...] * present_ref[...]).astype(F32)
    if sequences < LANES:
        keep = jnp.pad(keep, ((0, 0), (0, LANES - sequences)))
    keep_ref[...] = keep
    keep_tile = keep.astype(BF16)
    for target in range(out_ref.shape[0]):
        part, group = divmod(target, groups)
        slot = 0
        for head in range(half_heads):
            for row in range(row_tiles):
                for column in range(column_tiles):
                    out_ref[target, slot] = bias_ref[
                        group * heads_here + part % 2 * half_heads + head,
                        row * 8 : (row + 1) * 8,
                        column * LANES : (column + 1) * LANES,
                    ]
                    slot += 1
        out_ref[target, slot] = keep_tile


def prepare_kernel(
    sizes, x_ref, keep_ref, left_w_ref, right_w_ref, rows_ref, left_ref
):
    groups, sequences_here = sizes
    sequences, residues, width = x_ref.shape
    total = sequences * residues
    channels = left_w_ref.shape[0]
    keep = keep_ref[:, :sequences]
    normed = layer_normalize(x_ref[...].astype(F32).reshape(total, width))
    normed_tiles = normed.astype(F32).reshape(sequences, residues, width).astype(BF16)
    halves = width // LANES
    for part in range(sequences // sequences_here):
        for own in range(sequences_here):
            for half in range(halves):
                for group in range(groups):
                    rows_ref[part * groups + group, own * halves + half] = normed_tiles[
                        part * sequences_here + own, :, half * LANES : (half + 1) * LANES
                    ]

    to_residue_major = residue_major(sequences, residues)
    left = matmul_nt(normed, left_w_ref[...]).astype(BF16)
    left = matmul(to_residue_major, left)
    pick = one_hot(
        quotient(rows_of((total, residues)), sequences) == lanes_of((total, residues))
    )
    own_keep = matmul(pick, keep.astype(BF16))
    at_sequence = remainder(rows_of((total, sequences)), sequences) == lanes_of((total, sequences))
    own_keep = jnp.sum(jnp.where(at_sequence, own_keep, 0.0), axis=1, keepdims=True)
    left_ref[...] = (left * own_keep).astype(BF16)

    right = matmul_nt(normed, right_w_ref[...]).astype(BF16)
    residue_pick = one_hot(
        remainder(lanes_of((residues, total)), residues) == rows_of((residues, total))
    )
    per_tile = LANES // sequences
    spread = one_hot(
        remainder(lanes_of((sequences, LANES)), sequences) == rows_of((sequences, LANES))
    )
    keep_spread = matmul(keep.astype(BF16), spread)
    same_sequence = quotient(rows_of((total, LANES)), residues) == remainder(
        lanes_of((total, LANES)), sequences
    )
    for tile in range(channels // per_tile):
        select = one_hot(
            rows_of((channels, LANES))
            == tile * per_tile + quotient(lanes_of((channels, LANES)), sequences)
        )
        expanded = jnp.where(same_sequence, matmul(right, select), 0.0).astype(BF16)
        result = (matmul(residue_pick, expanded) * keep_spread).astype(BF16)
        quarter, slot = divmod(tile, channels // per_tile // 4)
        for target in range(rows_ref.shape[0]):
            if target // groups % 4 == quarter:
                rows_ref[target, sequences_here * halves + slot] = result


def row_kernel(
    sizes, place_ref, own_bias_ref, other_bias_ref, rows_ref, weight_ref,
    mix_ref, keep_all_ref, query_s, key_s, value_s, gate_s,
):
    groups, sequences_here, row_tiles, column_tiles = sizes
    blocks, tiles, residues, _ = rows_ref.shape
    residues_overall = blocks * residues
    halves = weight_ref.shape[1] // LANES
    head_lanes = weight_ref.shape[2]
    half_heads = head_lanes // PER_SPLIT_DIM // 2
    query_factor = PER_SPLIT_DIM ** (-0.5)
    block_rows = min(residues_overall, 256)
    part = quotient(place_ref[0], groups)
    core = part & 1

    for own in range(sequences_here):
        normed = jnp.concatenate(
            [flat_rows(rows_ref[:, own * halves + half]) for half in range(halves)], axis=1
        )
        query_s[own] = (matmul(normed, weight_ref[0]) * query_factor).astype(BF16)
        key_s[own] = matmul(normed, weight_ref[1]).astype(BF16)
        value_s[own] = matmul(normed, weight_ref[2]).astype(BF16)
        gate_s[own] = jax.nn.sigmoid(matmul(normed, weight_ref[3]))

    keep_all = flat_rows(own_bias_ref[:, half_heads * row_tiles * column_tiles])
    keep_all_ref[...] = keep_all
    chosen = one_hot(lanes_of((8, LANES)) == part * sequences_here + rows_of((8, LANES)))
    key_keep = matmul_nt(chosen, keep_all)

    def attend(block):
        start = block * block_rows
        parts = block_rows // (row_tiles * 8)
        head_of = quotient(lanes_of((residues_overall, head_lanes)), PER_SPLIT_DIM)
        query_head = quotient(lanes_of((block_rows, head_lanes)), PER_SPLIT_DIM)
        biases = []
        for bias_ref in (own_bias_ref, other_bias_ref):
            for head in range(half_heads):
                columns = []
                for group in range(groups):
                    for column in range(column_tiles):
                        pieces = []
                        for at in range(parts):
                            for row in range(row_tiles):
                                slot = (head * row_tiles + row) * column_tiles + column
                                source = (block * parts + at) * groups + group
                                pieces.append(bias_ref[source, slot].astype(F32))
                        columns.append(jnp.concatenate(pieces, axis=0))
                biases.append(jnp.concatenate(columns, axis=1))
        for own in range(sequences_here):
            queries = query_s[own, pl.ds(start, block_rows), :]
            keys, values = key_s[own], value_s[own]
            keep_row = key_keep[own : own + 1, :] > 0.5
            total = jnp.zeros((block_rows, 2 * head_lanes), F32)
            for at in range(2 * half_heads):
                head = (core ^ (at // half_heads)) * half_heads + at % half_heads
                query_part = jnp.where(query_head == head, queries, jnp.zeros_like(queries))
                scores = matmul_nt(query_part, keys) + biases[at]
                scores = jnp.where(keep_row, scores, MASKED)
                scores = scores - jnp.max(scores, axis=1, keepdims=True)
                weights = jnp.exp(scores).astype(BF16)
                mine = head_of == head
                value_part = jnp.where(mine, values, jnp.zeros_like(values))
                total = total + matmul(
                    weights, jnp.concatenate([value_part, one_hot(mine)], axis=1)
                )
            mixed = total[:, :head_lanes] / total[:, head_lanes:]
            mixed = mixed * gate_s[own, pl.ds(start, block_rows), :]
            mix_ref[pl.ds(block * (block_rows // residues), block_rows // residues), own] = (
                mixed.reshape(block_rows // residues, residues, head_lanes).astype(BF16)
            )

    if residues_overall == block_rows:
        attend(0)
    else:
        pl.loop(0, residues_overall // block_rows)(attend)


def outer_kernel(
    sizes, place_ref, keep_all_ref, right0, right1, right2, right3, left_ref, keep_ref,
    weight_ref, out_ref, mixed_s,
):
    groups, sequences, pair = sizes
    residues = keep_ref.shape[0]
    channels, _, depth = weight_ref.shape
    quarter = quotient(place_ref[0], groups) & 3
    left = left_ref[...]
    quarter_channels = channels // 4
    for at in range(0, channels, 2):
        channel = (quarter ^ (at // quarter_channels)) * quarter_channels + at % quarter_channels
        weights = jnp.concatenate([weight_ref[channel], weight_ref[channel + 1]], axis=1)
        product = matmul(left, weights).astype(BF16)
        for residue in range(residues):
            for step in range(2):
                mixed_s[residue, (at + step) * sequences : (at + step + 1) * sequences, :] = product[
                    residue * sequences : (residue + 1) * sequences,
                    step * depth : (step + 1) * depth,
                ]
    right = jnp.concatenate(
        [
            flat_rows(right_ref[:, tile])
            for right_ref in (right0, right1, right2, right3)
            for tile in range(right_ref.shape[1])
        ],
        axis=1,
    )
    keep_all = keep_all_ref[...]
    for first in range(0, residues, pair):
        members = range(first, first + pair)
        mixed = jnp.concatenate([mixed_s[residue] for residue in members], axis=1)
        keep_rows = jnp.concatenate(
            [
                jnp.broadcast_to(keep_ref[residue : residue + 1, :], (depth, LANES))
                for residue in members
            ],
            axis=0,
        ).astype(BF16)
        result = matmul(right, mixed) / matmul_nt(keep_all, keep_rows)
        for at, residue in enumerate(members):
            out_ref[residue] = result[:, at * depth : (at + 1) * depth].astype(BF16)


def column_kernel(
    sizes, place_ref, x_ref, mix_ref, keep_ref, row_out_ref, query_w_ref, key_w_ref, vg_w_ref,
    out_w_ref, out_ref,
):
    groups = sizes
    sequences, residues, width = x_ref.shape
    total = sequences * residues
    heads = query_w_ref.shape[1] // PER_SPLIT_DIM
    query_factor = PER_SPLIT_DIM ** (-0.5)
    own_group = place_ref[0] & (groups - 1)
    after = x_ref[...].astype(F32).reshape(total, width)
    for at in range(groups):
        group = own_group ^ at
        mixed = mix_ref[:, pl.ds(group, 1)]
        mixed = mixed.astype(F32).reshape(total, mixed.shape[-1]).astype(BF16)
        after = after + matmul(mixed, row_out_ref[at])
    after = after.astype(BF16).astype(F32)
    permutation = residue_major(sequences, residues)
    normed = matmul(permutation, layer_normalize(after)).astype(BF16)
    queries = (matmul(normed, query_w_ref[...]) * query_factor).astype(BF16)
    keys = matmul(normed, key_w_ref[...]).astype(BF16)
    values = matmul(normed, vg_w_ref[0]).astype(BF16)
    gate = jax.nn.sigmoid(matmul(normed, vg_w_ref[1]))

    together = max(1, min(residues, 256 // sequences))
    span = together * sequences
    head_rows = heads * sequences
    inner = heads * PER_SPLIT_DIM
    block_diagonal = quotient(rows_of((head_rows, inner)), sequences) == quotient(
        lanes_of((head_rows, inner)), PER_SPLIT_DIM
    )
    zero = jnp.zeros((head_rows, inner), BF16)

    def by_head(part):
        return jnp.where(block_diagonal, jnp.concatenate([part] * heads, axis=0), zero)

    mixes = []
    for first in range(0, residues, together):
        base = first * sequences
        query_span = queries[base : base + span]
        owner = quotient(rows_of((span, inner)), sequences)
        scores = jnp.zeros((head_rows, span), F32)
        for at in range(together):
            key_part = by_head(keys[base + at * sequences : base + (at + 1) * sequences])
            query_part = jnp.where(owner == at, query_span, jnp.zeros_like(query_span))
            scores = scores + matmul_nt(key_part, query_part)
        spread = one_hot(
            rows_of((residues, span)) == first + quotient(lanes_of((residues, span)), sequences)
        )
        key_keep = matmul_tn(keep_ref[...].astype(BF16), spread)[:sequences]
        scores = scores.reshape(heads, sequences, span)
        scores = jnp.where(key_keep[None] > 0.5, scores, MASKED)
        scores = jnp.exp(scores - jnp.max(scores, axis=1, keepdims=True))
        weights = scores / jnp.sum(scores, axis=1, keepdims=True)
        weights = weights.reshape(head_rows, span).T.astype(BF16)
        for at in range(together):
            value_part = by_head(values[base + at * sequences : base + (at + 1) * sequences])
            mixes.append(matmul(weights[at * sequences : (at + 1) * sequences], value_part))
    mixed = (jnp.concatenate(mixes, axis=0) * gate).astype(BF16)
    mixed = matmul_tn(permutation, mixed).astype(BF16)
    result = after + matmul(mixed, out_w_ref[...])
    out_ref[...] = result.reshape(sequences, residues, width).astype(BF16)


def call(kernel, outs, arguments, scratch=(), scalars=0, mib=32, micros=2, fetch=False):
    vmem = pl.BlockSpec(memory_space=pltpu.VMEM)
    read = pl.BlockSpec(memory_space=pltpu.HBM) if fetch else vmem
    smem = pl.BlockSpec(memory_space=pltpu.SMEM)
    return pl.pallas_call(
        kernel,
        out_shape=outs,
        in_specs=[smem] * scalars + [read] * (len(arguments) - scalars),
        out_specs=jax.tree.map(lambda _: vmem, outs),
        scratch_shapes=list(scratch),
        compiler_params=pltpu.CompilerParams(vmem_limit_bytes=mib * 1024 * 1024),
        cost_estimate=pl.CostEstimate(
            flops=micros * 1_000_000_000, bytes_accessed=micros * 1_000_000, transcendentals=0
        ),
    )(*arguments)


def shards(
    homolog_activity,
    alignment_mask,
    sequence_row_mask,
    pairwise_bias,
    horizontal_projection_matrix,
    horizontal_final_matrix,
    column_query_weight,
    column_key_weight,
    vertical_content_sigmoid_matrix,
    vertical_final_matrix,
    first_operand_matrix,
    second_operand_matrix,
    outer_output_weight,
):
    parallel = lax.axis_size("dap")
    groups = lax.axis_size("grp")
    devices = parallel * groups
    both = ("dap", "grp")
    sequences, residues, width = homolog_activity.shape
    residues_overall = residues * devices
    sequences_here = sequences // parallel
    channels = first_operand_matrix.shape[1]
    depth = outer_output_weight.shape[1]
    heads_here, row_tiles, column_tiles = tile_count(pairwise_bias.shape, groups)
    head_lanes = heads_here * PER_SPLIT_DIM
    large = residues_overall > 256
    place = (lax.axis_index("dap") * groups + lax.axis_index("grp")).astype(jnp.int32).reshape(1)
    shape = jax.ShapeDtypeStruct

    def exchange(value, mask):
        return lax.ppermute(value, both, [(at, at ^ mask) for at in range(devices)])

    def to_all(value):
        return lax.all_to_all(value, both, split_axis=0, concat_axis=0, tiled=True)

    half_tiles = heads_here // 2 * row_tiles * column_tiles
    bias_out, keep = call(
        functools.partial(share_kernel, groups),
        (shape((devices, half_tiles + 1, 8, LANES), BF16), shape((8, LANES), F32)),
        (alignment_mask.T, sequence_row_mask.reshape(1, sequences), pairwise_bias),
        scratch=[
            pltpu.VMEM((residues, sequences), jnp.int32),
            pltpu.VMEM((1, sequences), jnp.int32),
            pltpu.VMEM(pairwise_bias.shape, BF16),
            pltpu.SemaphoreType.DMA((3,)),
        ],
        micros=1,
        fetch=True,
    )
    own_bias = to_all(bias_out)
    other_bias = exchange(own_bias, groups)
    row_out_weight = jnp.stack(
        [horizontal_final_matrix]
        + [exchange(horizontal_final_matrix, relative) for relative in range(1, groups)]
    )

    right_tiles = channels * sequences // LANES
    row_slots = sequences_here * (width // LANES)
    rows_out, left = call(
        functools.partial(prepare_kernel, (groups, sequences_here)),
        (
            shape((devices, row_slots + right_tiles // 4, residues, LANES), BF16),
            shape((sequences * residues, channels), BF16),
        ),
        (homolog_activity, keep, first_operand_matrix.T, second_operand_matrix.T),
        mib=56 if large else 32,
    )
    rows_in = to_all(rows_out)
    right = rows_in[:, row_slots:]
    right_across = exchange(right, 2 * groups)
    right_parts = (right, exchange(right, groups), right_across, exchange(right_across, groups))

    mix_out, keep_all = call(
        functools.partial(row_kernel, (groups, sequences_here, row_tiles, column_tiles)),
        (
            shape((devices, sequences_here, residues, head_lanes), BF16),
            shape((residues_overall, LANES), BF16),
        ),
        (
            place,
            own_bias,
            other_bias,
            rows_in,
            horizontal_projection_matrix.transpose(1, 0, 2),
        ),
        scratch=[pltpu.VMEM((sequences_here, residues_overall, head_lanes), BF16)] * 3
        + [pltpu.VMEM((sequences_here, residues_overall, head_lanes), F32)],
        scalars=1,
        mib=60 if large else 32,
    )
    mix_in = to_all(mix_out)

    pairwise_update = call(
        functools.partial(outer_kernel, (groups, sequences, 2)),
        shape((residues, residues_overall, depth), BF16),
        (
            place,
            keep_all,
            *right_parts,
            left,
            keep,
            outer_output_weight.reshape(channels, channels, depth).transpose(1, 0, 2),
        ),
        scratch=[pltpu.VMEM((residues, channels * sequences, depth), BF16)],
        scalars=1,
        mib=60 if large else 32,
    )

    alignment_output = call(
        functools.partial(column_kernel, groups),
        shape((sequences, residues, width), BF16),
        (
            place,
            homolog_activity,
            mix_in.reshape(parallel, groups, sequences_here, residues, head_lanes),
            keep,
            row_out_weight,
            column_query_weight,
            column_key_weight,
            vertical_content_sigmoid_matrix.transpose(1, 0, 2),
            vertical_final_matrix,
        ),
        scalars=1,
        mib=56 if large else 32,
        micros=3,
    )
    return (alignment_output, pairwise_update)


def solution(mesh):
    return jax.shard_map(
        shards,
        mesh=mesh,
        in_specs=(
            P(None, ("dap", "grp"), None),
            P(None, ("dap", "grp")),
            P(),
            P(None, "dap", "grp"),
            P(None, None, "grp"),
            P("grp", None),
            P(),
            P(),
            P(),
            P(),
            P(),
            P(),
            P(),
        ),
        out_specs=(P(None, ("dap", "grp"), None), P(("dap", "grp"), None, None)),
        check_vma=False,
    )
```

```python
import functools

import jax
import jax.numpy as jnp
from jax import lax
from jax.experimental import pallas as pl
from jax.experimental.pallas import tpu as pltpu
from jax.sharding import PartitionSpec as P

PER_SPLIT_DIM = 32
LANES = 128
MASKED = -1000000000.0
F32 = jnp.float32
BF16 = jnp.bfloat16


def matmul(lhs, rhs):
    return jnp.dot(lhs, rhs, preferred_element_type=F32)


def matmul_nt(lhs, rhs):
    return lax.dot_general(lhs, rhs, (((1,), (1,)), ((), ())), preferred_element_type=F32)


def matmul_tn(lhs, rhs):
    return lax.dot_general(lhs, rhs, (((0,), (0,)), ((), ())), preferred_element_type=F32)


def rows_of(shape):
    return lax.broadcasted_iota(jnp.int32, shape, 0)


def lanes_of(shape):
    return lax.broadcasted_iota(jnp.int32, shape, 1)


def quotient(values, divisor):
    return lax.shift_right_logical(values, divisor.bit_length() - 1)


def remainder(values, divisor):
    return values & (divisor - 1)


def one_hot(condition):
    return condition.astype(F32).astype(BF16)


def flat_rows(tiles):
    blocks, sublanes, lanes = tiles.shape
    return tiles.astype(F32).reshape(blocks * sublanes, lanes).astype(BF16)


def layer_normalize(widened):
    centered = widened - jnp.mean(widened, axis=-1, keepdims=True)
    variance = jnp.mean(centered * centered, axis=-1, keepdims=True)
    return (centered * lax.rsqrt(variance + 1e-05)).astype(BF16)


def residue_major(sequences, residues):
    total = sequences * residues
    row, lane = rows_of((total, total)), lanes_of((total, total))
    return one_hot(lane == remainder(row, sequences) * residues + quotient(row, sequences))


def tile_count(bias_shape, groups):
    heads, bias_rows, bias_columns = bias_shape
    return heads // groups, bias_rows // 8, bias_columns // LANES


def share_kernel(
    groups, mask_hbm, present_hbm, bias_hbm, out_ref, keep_ref, mask_ref, present_ref, bias_ref,
    sems,
):
    pairs = ((bias_hbm, bias_ref), (mask_hbm, mask_ref), (present_hbm, present_ref))
    copies = [
        pltpu.make_async_copy(source, target, sems.at[at])
        for at, (source, target) in enumerate(pairs)
    ]
    for copy in copies:
        copy.start()
    for copy in copies:
        copy.wait()
    heads_here, row_tiles, column_tiles = tile_count(bias_ref.shape, groups)
    half_heads = heads_here // 2
    sequences = mask_ref.shape[1]
    keep = (mask_ref[...] * present_ref[...]).astype(F32)
    if sequences < LANES:
        keep = jnp.pad(keep, ((0, 0), (0, LANES - sequences)))
    keep_ref[...] = keep
    keep_tile = keep.astype(BF16)
    for target in range(out_ref.shape[0]):
        part, group = divmod(target, groups)
        slot = 0
        for head in range(half_heads):
            for row in range(row_tiles):
                for column in range(column_tiles):
                    out_ref[target, slot] = bias_ref[
                        group * heads_here + part % 2 * half_heads + head,
                        row * 8 : (row + 1) * 8,
                        column * LANES : (column + 1) * LANES,
                    ]
                    slot += 1
        out_ref[target, slot] = keep_tile


def prepare_kernel(
    sizes, x_ref, keep_ref, left_w_ref, right_w_ref, rows_ref, left_ref
):
    groups, sequences_here = sizes
    sequences, residues, width = x_ref.shape
    total = sequences * residues
    channels = left_w_ref.shape[0]
    keep = keep_ref[:, :sequences]
    normed = layer_normalize(x_ref[...].astype(F32).reshape(total, width))
    normed_tiles = normed.astype(F32).reshape(sequences, residues, width).astype(BF16)
    halves = width // LANES
    for part in range(sequences // sequences_here):
        for own in range(sequences_here):
            for half in range(halves):
                for group in range(groups):
                    rows_ref[part * groups + group, own * halves + half] = normed_tiles[
                        part * sequences_here + own, :, half * LANES : (half + 1) * LANES
                    ]

    to_residue_major = residue_major(sequences, residues)
    left = matmul_nt(normed, left_w_ref[...]).astype(BF16)
    left = matmul(to_residue_major, left)
    pick = one_hot(
        quotient(rows_of((total, residues)), sequences) == lanes_of((total, residues))
    )
    own_keep = matmul(pick, keep.astype(BF16))
    at_sequence = remainder(rows_of((total, sequences)), sequences) == lanes_of((total, sequences))
    own_keep = jnp.sum(jnp.where(at_sequence, own_keep, 0.0), axis=1, keepdims=True)
    left_ref[...] = (left * own_keep).astype(BF16)

    right = matmul_nt(normed, right_w_ref[...]).astype(BF16)
    residue_pick = one_hot(
        remainder(lanes_of((residues, total)), residues) == rows_of((residues, total))
    )
    per_tile = LANES // sequences
    spread = one_hot(
        remainder(lanes_of((sequences, LANES)), sequences) == rows_of((sequences, LANES))
    )
    keep_spread = matmul(keep.astype(BF16), spread)
    same_sequence = quotient(rows_of((total, LANES)), residues) == remainder(
        lanes_of((total, LANES)), sequences
    )
    for tile in range(channels // per_tile):
        select = one_hot(
            rows_of((channels, LANES))
            == tile * per_tile + quotient(lanes_of((channels, LANES)), sequences)
        )
        expanded = jnp.where(same_sequence, matmul(right, select), 0.0).astype(BF16)
        result = (matmul(residue_pick, expanded) * keep_spread).astype(BF16)
        quarter, slot = divmod(tile, channels // per_tile // 4)
        for target in range(rows_ref.shape[0]):
            if target // groups % 4 == quarter:
                rows_ref[target, sequences_here * halves + slot] = result


def attend_half(
    sizes, place_ref, bias_ref, key_keep_ref, query_ref, key_ref, value_ref, other, block_rows,
    finish,
):
    groups, row_tiles, column_tiles = sizes
    sequences_here, residues_overall, head_lanes = query_ref.shape
    half_heads = head_lanes // PER_SPLIT_DIM // 2
    side = (quotient(place_ref[0], groups) & 1) ^ other

    def attend(block):
        start = block * block_rows
        parts = block_rows // (row_tiles * 8)
        head_of = quotient(lanes_of((residues_overall, head_lanes)), PER_SPLIT_DIM)
        query_head = quotient(lanes_of((block_rows, head_lanes)), PER_SPLIT_DIM)
        biases = []
        for head in range(half_heads):
            columns = []
            for group in range(groups):
                for column in range(column_tiles):
                    pieces = []
                    for at in range(parts):
                        for row in range(row_tiles):
                            slot = (head * row_tiles + row) * column_tiles + column
                            source = (block * parts + at) * groups + group
                            pieces.append(bias_ref[source, slot].astype(F32))
                    columns.append(jnp.concatenate(pieces, axis=0))
            biases.append(jnp.concatenate(columns, axis=1))
        for own in range(sequences_here):
            queries = query_ref[own, pl.ds(start, block_rows), :]
            keys, values = key_ref[own], value_ref[own]
            keep_row = key_keep_ref[own : own + 1, :] > 0.5
            total = jnp.zeros((block_rows, 2 * head_lanes), F32)
            for at in range(half_heads):
                head = side * half_heads + at
                query_part = jnp.where(query_head == head, queries, jnp.zeros_like(queries))
                scores = matmul_nt(query_part, keys) + biases[at]
                scores = jnp.where(keep_row, scores, MASKED)
                scores = scores - jnp.max(scores, axis=1, keepdims=True)
                weights = jnp.exp(scores).astype(BF16)
                mine = head_of == head
                value_part = jnp.where(mine, values, jnp.zeros_like(values))
                total = total + matmul(
                    weights, jnp.concatenate([value_part, one_hot(mine)], axis=1)
                )
            here = quotient(query_head, half_heads) == side
            mixed = total[:, :head_lanes] / jnp.where(here, total[:, head_lanes:], 1.0)
            finish(block, own, start, mixed)

    if residues_overall == block_rows:
        attend(0)
    else:
        pl.loop(0, residues_overall // block_rows)(attend)


def first_row_kernel(
    sizes, place_ref, bias_ref, rows_ref, weight_ref,
    part_ref, keep_all_ref, key_keep_ref, query_ref, key_ref, value_ref, gate_ref,
):
    groups, row_tiles, column_tiles = sizes
    sequences_here = query_ref.shape[0]
    halves = weight_ref.shape[1] // LANES
    half_heads = weight_ref.shape[2] // PER_SPLIT_DIM // 2
    query_factor = PER_SPLIT_DIM ** (-0.5)
    for own in range(sequences_here):
        normed = jnp.concatenate(
            [flat_rows(rows_ref[:, own * halves + half]) for half in range(halves)], axis=1
        )
        query_ref[own] = (matmul(normed, weight_ref[0]) * query_factor).astype(BF16)
        key_ref[own] = matmul(normed, weight_ref[1]).astype(BF16)
        value_ref[own] = matmul(normed, weight_ref[2]).astype(BF16)
        gate_ref[own] = jax.nn.sigmoid(matmul(normed, weight_ref[3]))

    keep_all = flat_rows(bias_ref[:, half_heads * row_tiles * column_tiles])
    keep_all_ref[...] = keep_all
    part = quotient(place_ref[0], groups)
    chosen = one_hot(lanes_of((8, LANES)) == part * sequences_here + rows_of((8, LANES)))
    key_keep_ref[...] = matmul_nt(chosen, keep_all)
    block_rows = min(query_ref.shape[1], 256)

    def finish(block, own, start, mixed):
        part_ref[own, pl.ds(start, block_rows), :] = mixed

    attend_half(
        sizes, place_ref, bias_ref, key_keep_ref, query_ref, key_ref, value_ref, 0, block_rows,
        finish,
    )


def second_row_kernel(
    sizes, place_ref, bias_ref, rows_ref, part_ref, key_keep_ref, query_ref, key_ref, value_ref,
    gate_ref, mix_ref, right_ref,
):
    _, _, residues, head_lanes = mix_ref.shape
    block_rows = min(query_ref.shape[1], 256)
    count = block_rows // residues

    def finish(block, own, start, mixed):
        rows = pl.ds(start, block_rows)
        mixed = (part_ref[own, rows, :] + mixed) * gate_ref[own, rows, :]
        mix_ref[pl.ds(block * count, count), own] = mixed.reshape(
            count, residues, head_lanes
        ).astype(BF16)

    attend_half(
        sizes, place_ref, bias_ref, key_keep_ref, query_ref, key_ref, value_ref, 1, block_rows,
        finish,
    )
    tiles = right_ref.shape[1]
    right_ref[...] = rows_ref[:, rows_ref.shape[1] - tiles :]


def outer_kernel(
    sizes, place_ref, keep_all_ref, right0, right1, right2, right3, left_ref, keep_ref,
    weight_ref, out_ref, mixed_s,
):
    groups, sequences, pair = sizes
    residues = keep_ref.shape[0]
    channels, _, depth = weight_ref.shape
    quarter = quotient(place_ref[0], groups) & 3
    left = left_ref[...]
    quarter_channels = channels // 4
    for at in range(0, channels, 2):
        channel = (quarter ^ (at // quarter_channels)) * quarter_channels + at % quarter_channels
        weights = jnp.concatenate([weight_ref[channel], weight_ref[channel + 1]], axis=1)
        product = matmul(left, weights).astype(BF16)
        for residue in range(residues):
            for step in range(2):
                mixed_s[residue, (at + step) * sequences : (at + step + 1) * sequences, :] = product[
                    residue * sequences : (residue + 1) * sequences,
                    step * depth : (step + 1) * depth,
                ]
    right = jnp.concatenate(
        [
            flat_rows(right_ref[:, tile])
            for right_ref in (right0, right1, right2, right3)
            for tile in range(right_ref.shape[1])
        ],
        axis=1,
    )
    keep_all = keep_all_ref[...]
    for first in range(0, residues, pair):
        members = range(first, first + pair)
        mixed = jnp.concatenate([mixed_s[residue] for residue in members], axis=1)
        keep_rows = jnp.concatenate(
            [
                jnp.broadcast_to(keep_ref[residue : residue + 1, :], (depth, LANES))
                for residue in members
            ],
            axis=0,
        ).astype(BF16)
        result = matmul(right, mixed) / matmul_nt(keep_all, keep_rows)
        for at, residue in enumerate(members):
            out_ref[residue] = result[:, at * depth : (at + 1) * depth].astype(BF16)


def column_kernel(
    sizes, place_ref, x_ref, mix_ref, keep_ref, row_out_ref, query_w_ref, key_w_ref, vg_w_ref,
    out_w_ref, out_ref,
):
    groups = sizes
    sequences, residues, width = x_ref.shape
    total = sequences * residues
    heads = query_w_ref.shape[1] // PER_SPLIT_DIM
    query_factor = PER_SPLIT_DIM ** (-0.5)
    own_group = place_ref[0] & (groups - 1)
    after = x_ref[...].astype(F32).reshape(total, width)
    for at in range(groups):
        group = own_group ^ at
        mixed = mix_ref[:, pl.ds(group, 1)]
        mixed = mixed.astype(F32).reshape(total, mixed.shape[-1]).astype(BF16)
        after = after + matmul(mixed, row_out_ref[at])
    after = after.astype(BF16).astype(F32)
    permutation = residue_major(sequences, residues)
    normed = matmul(permutation, layer_normalize(after)).astype(BF16)
    queries = (matmul(normed, query_w_ref[...]) * query_factor).astype(BF16)
    keys = matmul(normed, key_w_ref[...]).astype(BF16)
    values = matmul(normed, vg_w_ref[0]).astype(BF16)
    gate = jax.nn.sigmoid(matmul(normed, vg_w_ref[1]))

    together = max(1, min(residues, 256 // sequences))
    span = together * sequences
    head_rows = heads * sequences
    inner = heads * PER_SPLIT_DIM
    block_diagonal = quotient(rows_of((head_rows, inner)), sequences) == quotient(
        lanes_of((head_rows, inner)), PER_SPLIT_DIM
    )
    zero = jnp.zeros((head_rows, inner), BF16)

    def by_head(part):
        return jnp.where(block_diagonal, jnp.concatenate([part] * heads, axis=0), zero)

    mixes = []
    for first in range(0, residues, together):
        base = first * sequences
        query_span = queries[base : base + span]
        owner = quotient(rows_of((span, inner)), sequences)
        scores = jnp.zeros((head_rows, span), F32)
        for at in range(together):
            key_part = by_head(keys[base + at * sequences : base + (at + 1) * sequences])
            query_part = jnp.where(owner == at, query_span, jnp.zeros_like(query_span))
            scores = scores + matmul_nt(key_part, query_part)
        spread = one_hot(
            rows_of((residues, span)) == first + quotient(lanes_of((residues, span)), sequences)
        )
        key_keep = matmul_tn(keep_ref[...].astype(BF16), spread)[:sequences]
        scores = scores.reshape(heads, sequences, span)
        scores = jnp.where(key_keep[None] > 0.5, scores, MASKED)
        scores = jnp.exp(scores - jnp.max(scores, axis=1, keepdims=True))
        weights = scores / jnp.sum(scores, axis=1, keepdims=True)
        weights = weights.reshape(head_rows, span).T.astype(BF16)
        for at in range(together):
            value_part = by_head(values[base + at * sequences : base + (at + 1) * sequences])
            mixes.append(matmul(weights[at * sequences : (at + 1) * sequences], value_part))
    mixed = (jnp.concatenate(mixes, axis=0) * gate).astype(BF16)
    mixed = matmul_tn(permutation, mixed).astype(BF16)
    result = after + matmul(mixed, out_w_ref[...])
    out_ref[...] = result.reshape(sequences, residues, width).astype(BF16)


def call(kernel, outs, arguments, scratch=(), scalars=0, mib=32, micros=2, fetch=False):
    vmem = pl.BlockSpec(memory_space=pltpu.VMEM)
    read = pl.BlockSpec(memory_space=pltpu.HBM) if fetch else vmem
    smem = pl.BlockSpec(memory_space=pltpu.SMEM)
    return pl.pallas_call(
        kernel,
        out_shape=outs,
        in_specs=[smem] * scalars + [read] * (len(arguments) - scalars),
        out_specs=jax.tree.map(lambda _: vmem, outs),
        scratch_shapes=list(scratch),
        compiler_params=pltpu.CompilerParams(vmem_limit_bytes=mib * 1024 * 1024),
        cost_estimate=pl.CostEstimate(
            flops=micros * 1_000_000_000, bytes_accessed=micros * 1_000_000, transcendentals=0
        ),
    )(*arguments)


def shards(
    homolog_activity,
    alignment_mask,
    sequence_row_mask,
    pairwise_bias,
    horizontal_projection_matrix,
    horizontal_final_matrix,
    column_query_weight,
    column_key_weight,
    vertical_content_sigmoid_matrix,
    vertical_final_matrix,
    first_operand_matrix,
    second_operand_matrix,
    outer_output_weight,
):
    parallel = lax.axis_size("dap")
    groups = lax.axis_size("grp")
    devices = parallel * groups
    both = ("dap", "grp")
    sequences, residues, width = homolog_activity.shape
    residues_overall = residues * devices
    sequences_here = sequences // parallel
    channels = first_operand_matrix.shape[1]
    depth = outer_output_weight.shape[1]
    heads_here, row_tiles, column_tiles = tile_count(pairwise_bias.shape, groups)
    head_lanes = heads_here * PER_SPLIT_DIM
    large = residues_overall > 256
    place = (lax.axis_index("dap") * groups + lax.axis_index("grp")).astype(jnp.int32).reshape(1)
    shape = jax.ShapeDtypeStruct

    def exchange(value, mask):
        return lax.ppermute(value, both, [(at, at ^ mask) for at in range(devices)])

    def to_all(value):
        return lax.all_to_all(value, both, split_axis=0, concat_axis=0, tiled=True)

    half_tiles = heads_here // 2 * row_tiles * column_tiles
    bias_out, keep = call(
        functools.partial(share_kernel, groups),
        (shape((devices, half_tiles + 1, 8, LANES), BF16), shape((8, LANES), F32)),
        (alignment_mask.T, sequence_row_mask.reshape(1, sequences), pairwise_bias),
        scratch=[
            pltpu.VMEM((residues, sequences), jnp.int32),
            pltpu.VMEM((1, sequences), jnp.int32),
            pltpu.VMEM(pairwise_bias.shape, BF16),
            pltpu.SemaphoreType.DMA((3,)),
        ],
        micros=1,
        fetch=True,
        mib=62,
    )
    own_bias = to_all(bias_out)
    row_out_weight = jnp.stack(
        [horizontal_final_matrix]
        + [exchange(horizontal_final_matrix, relative) for relative in range(1, groups)]
    )

    right_tiles = channels * sequences // LANES
    row_slots = sequences_here * (width // LANES)
    rows_out, left = call(
        functools.partial(prepare_kernel, (groups, sequences_here)),
        (
            shape((devices, row_slots + right_tiles // 4, residues, LANES), BF16),
            shape((sequences * residues, channels), BF16),
        ),
        (homolog_activity, keep, first_operand_matrix.T, second_operand_matrix.T),
        mib=56 if large else 32,
    )
    rows_in = to_all(rows_out)
    row_weight = horizontal_projection_matrix.transpose(1, 0, 2)
    outer_weight = outer_output_weight.reshape(channels, channels, depth).transpose(1, 0, 2)
    content_weight = vertical_content_sigmoid_matrix.transpose(1, 0, 2)
    own_bias, rows_in, row_weight, outer_weight, content_weight, row_out_weight = (
        lax.optimization_barrier(
            (own_bias, rows_in, row_weight, outer_weight, content_weight, row_out_weight)
        )
    )
    other_bias = exchange(own_bias, groups)

    row_sizes = (groups, row_tiles, column_tiles)
    here = (sequences_here, residues_overall, head_lanes)
    part, keep_all, *projected = call(
        functools.partial(first_row_kernel, row_sizes),
        (
            shape(here, F32),
            shape((residues_overall, LANES), BF16),
            shape((8, residues_overall), F32),
            shape(here, BF16),
            shape(here, BF16),
            shape(here, BF16),
            shape(here, F32),
        ),
        (place, own_bias, rows_in, row_weight),
        scalars=1,
        mib=60 if large else 32,
    )
    mix_out, right = call(
        functools.partial(second_row_kernel, row_sizes),
        (
            shape((devices, sequences_here, residues, head_lanes), BF16),
            shape((devices, right_tiles // 4, residues, LANES), BF16),
        ),
        (place, other_bias, rows_in, part, *projected),
        scalars=1,
        mib=60 if large else 32,
    )
    right_across = exchange(right, 2 * groups)
    right_parts = (right, exchange(right, groups), right_across, exchange(right_across, groups))
    mix_in = to_all(mix_out)

    pairwise_update = call(
        functools.partial(outer_kernel, (groups, sequences, 2)),
        shape((residues, residues_overall, depth), BF16),
        (
            place,
            keep_all,
            *right_parts,
            left,
            keep,
            outer_weight,
        ),
        scratch=[pltpu.VMEM((residues, channels * sequences, depth), BF16)],
        scalars=1,
        mib=60 if large else 32,
    )

    alignment_output = call(
        functools.partial(column_kernel, groups),
        shape((sequences, residues, width), BF16),
        (
            place,
            homolog_activity,
            mix_in.reshape(parallel, groups, sequences_here, residues, head_lanes),
            keep,
            row_out_weight,
            column_query_weight,
            column_key_weight,
            content_weight,
            vertical_final_matrix,
        ),
        scalars=1,
        mib=56 if large else 32,
        micros=3,
    )
    return (alignment_output, pairwise_update)


def solution(mesh):
    return jax.shard_map(
        shards,
        mesh=mesh,
        in_specs=(
            P(None, ("dap", "grp"), None),
            P(None, ("dap", "grp")),
            P(),
            P(None, "dap", "grp"),
            P(None, None, "grp"),
            P("grp", None),
            P(),
            P(),
            P(),
            P(),
            P(),
            P(),
            P(),
        ),
        out_specs=(P(None, ("dap", "grp"), None), P(("dap", "grp"), None, None)),
        check_vma=False,
    )
```

```python
import functools

import jax
import jax.numpy as jnp
from jax import lax
from jax.experimental import pallas as pl
from jax.experimental.pallas import tpu as pltpu
from jax.sharding import PartitionSpec as P

PER_SPLIT_DIM = 32
LANES = 128
MASKED = -1000000000.0
F32 = jnp.float32
BF16 = jnp.bfloat16


def matmul(lhs, rhs):
    return jnp.dot(lhs, rhs, preferred_element_type=F32)


def matmul_nt(lhs, rhs):
    return lax.dot_general(lhs, rhs, (((1,), (1,)), ((), ())), preferred_element_type=F32)


def matmul_tn(lhs, rhs):
    return lax.dot_general(lhs, rhs, (((0,), (0,)), ((), ())), preferred_element_type=F32)


def rows_of(shape):
    return lax.broadcasted_iota(jnp.int32, shape, 0)


def lanes_of(shape):
    return lax.broadcasted_iota(jnp.int32, shape, 1)


def quotient(values, divisor):
    return lax.shift_right_logical(values, divisor.bit_length() - 1)


def remainder(values, divisor):
    return values & (divisor - 1)


def one_hot(condition):
    return condition.astype(F32).astype(BF16)


def flat_rows(tiles):
    blocks, sublanes, lanes = tiles.shape
    return tiles.astype(F32).reshape(blocks * sublanes, lanes).astype(BF16)


def layer_normalize(widened):
    centered = widened - jnp.mean(widened, axis=-1, keepdims=True)
    variance = jnp.mean(centered * centered, axis=-1, keepdims=True)
    return (centered * lax.rsqrt(variance + 1e-05)).astype(BF16)


def residue_major(sequences, residues):
    total = sequences * residues
    row, lane = rows_of((total, total)), lanes_of((total, total))
    return one_hot(lane == remainder(row, sequences) * residues + quotient(row, sequences))


def tile_count(bias_shape, groups):
    heads, bias_rows, bias_columns = bias_shape
    return heads // groups, bias_rows // 8, bias_columns // LANES


def prepare_kernel(
    sizes, bias_hbm, mask_hbm, present_hbm, x_hbm, left_w_hbm, right_w_hbm,
    rows_ref, left_ref, keep_ref,
    bias_ref, mask_ref, present_ref, x_ref, left_w_ref, right_w_ref, sems,
):
    groups, sequences_here = sizes
    sources = (bias_hbm, mask_hbm, present_hbm, x_hbm, left_w_hbm, right_w_hbm)
    targets = (bias_ref, mask_ref, present_ref, x_ref, left_w_ref, right_w_ref)
    copies = [
        pltpu.make_async_copy(source, target, sems.at[at])
        for at, (source, target) in enumerate(zip(sources, targets))
    ]
    for copy in copies:
        copy.start()
    for copy in copies[:3]:
        copy.wait()
    sequences, residues, width = x_ref.shape
    total = sequences * residues
    channels = left_w_ref.shape[0]
    heads_here, row_tiles, column_tiles = tile_count(bias_ref.shape, groups)
    half_heads = heads_here // 2
    keep = (mask_ref[...] * present_ref[...]).astype(F32)
    keep_padded = jnp.pad(keep, ((0, 0), (0, LANES - sequences))) if sequences < LANES else keep
    keep_ref[...] = keep_padded
    keep_tile = keep_padded.astype(BF16)
    last = rows_ref.shape[1] - 1
    for target in range(rows_ref.shape[0]):
        part, group = divmod(target, groups)
        slot = last - half_heads * row_tiles * column_tiles
        for head in range(half_heads):
            for row in range(row_tiles):
                for column in range(column_tiles):
                    rows_ref[target, slot] = bias_ref[
                        group * heads_here + part % 2 * half_heads + head,
                        row * 8 : (row + 1) * 8,
                        column * LANES : (column + 1) * LANES,
                    ]
                    slot += 1
        rows_ref[target, last] = keep_tile
    for copy in copies[3:]:
        copy.wait()

    normed = layer_normalize(x_ref[...].astype(F32).reshape(total, width))
    normed_tiles = normed.astype(F32).reshape(sequences, residues, width).astype(BF16)
    halves = width // LANES
    for part in range(sequences // sequences_here):
        for own in range(sequences_here):
            for half in range(halves):
                for group in range(groups):
                    rows_ref[part * groups + group, own * halves + half] = normed_tiles[
                        part * sequences_here + own, :, half * LANES : (half + 1) * LANES
                    ]

    to_residue_major = residue_major(sequences, residues)
    left = matmul_nt(normed, left_w_ref[...]).astype(BF16)
    left = matmul(to_residue_major, left)
    pick = one_hot(
        quotient(rows_of((total, residues)), sequences) == lanes_of((total, residues))
    )
    own_keep = matmul(pick, keep.astype(BF16))
    at_sequence = remainder(rows_of((total, sequences)), sequences) == lanes_of((total, sequences))
    own_keep = jnp.sum(jnp.where(at_sequence, own_keep, 0.0), axis=1, keepdims=True)
    left_ref[...] = (left * own_keep).astype(BF16)

    right = matmul_nt(normed, right_w_ref[...]).astype(BF16)
    residue_pick = one_hot(
        remainder(lanes_of((residues, total)), residues) == rows_of((residues, total))
    )
    per_tile = LANES // sequences
    spread = one_hot(
        remainder(lanes_of((sequences, LANES)), sequences) == rows_of((sequences, LANES))
    )
    keep_spread = matmul(keep.astype(BF16), spread)
    same_sequence = quotient(rows_of((total, LANES)), residues) == remainder(
        lanes_of((total, LANES)), sequences
    )
    for tile in range(channels // per_tile):
        select = one_hot(
            rows_of((channels, LANES))
            == tile * per_tile + quotient(lanes_of((channels, LANES)), sequences)
        )
        expanded = jnp.where(same_sequence, matmul(right, select), 0.0).astype(BF16)
        result = (matmul(residue_pick, expanded) * keep_spread).astype(BF16)
        quarter, slot = divmod(tile, channels // per_tile // 4)
        for target in range(rows_ref.shape[0]):
            if target // groups % 4 == quarter:
                rows_ref[target, sequences_here * halves + slot] = result


def attend_half(
    sizes, place_ref, bias_ref, first_slot, key_keep_ref, query_ref, key_ref, value_ref, other,
    block_rows, finish,
):
    groups, row_tiles, column_tiles = sizes
    sequences_here, residues_overall, head_lanes = query_ref.shape
    half_heads = head_lanes // PER_SPLIT_DIM // 2
    side = (quotient(place_ref[0], groups) & 1) ^ other

    def attend(block):
        start = block * block_rows
        parts = block_rows // (row_tiles * 8)
        head_of = quotient(lanes_of((residues_overall, head_lanes)), PER_SPLIT_DIM)
        query_head = quotient(lanes_of((block_rows, head_lanes)), PER_SPLIT_DIM)
        biases = []
        for head in range(half_heads):
            columns = []
            for group in range(groups):
                for column in range(column_tiles):
                    pieces = []
                    for at in range(parts):
                        for row in range(row_tiles):
                            slot = (head * row_tiles + row) * column_tiles + column
                            slot += first_slot
                            source = (block * parts + at) * groups + group
                            pieces.append(bias_ref[source, slot].astype(F32))
                    columns.append(jnp.concatenate(pieces, axis=0))
            biases.append(jnp.concatenate(columns, axis=1))
        for own in range(sequences_here):
            queries = query_ref[own, pl.ds(start, block_rows), :]
            keys, values = key_ref[own], value_ref[own]
            keep_row = key_keep_ref[own : own + 1, :] > 0.5
            total = jnp.zeros((block_rows, 2 * head_lanes), F32)
            for at in range(half_heads):
                head = side * half_heads + at
                query_part = jnp.where(query_head == head, queries, jnp.zeros_like(queries))
                scores = matmul_nt(query_part, keys) + biases[at]
                scores = jnp.where(keep_row, scores, MASKED)
                scores = scores - jnp.max(scores, axis=1, keepdims=True)
                weights = jnp.exp(scores).astype(BF16)
                mine = head_of == head
                value_part = jnp.where(mine, values, jnp.zeros_like(values))
                total = total + matmul(
                    weights, jnp.concatenate([value_part, one_hot(mine)], axis=1)
                )
            here = quotient(query_head, half_heads) == side
            mixed = total[:, :head_lanes] / jnp.where(here, total[:, head_lanes:], 1.0)
            finish(block, own, start, mixed)

    if residues_overall == block_rows:
        attend(0)
    else:
        pl.loop(0, residues_overall // block_rows)(attend)


def first_row_kernel(
    sizes, place_ref, rows_ref, weight_ref,
    right_ref, part_ref, keep_all_ref, key_keep_ref, query_ref, key_ref, value_ref, gate_ref,
):
    groups = sizes[0]
    sequences_here = query_ref.shape[0]
    halves = weight_ref.shape[1] // LANES
    query_factor = PER_SPLIT_DIM ** (-0.5)
    for own in range(sequences_here):
        normed = jnp.concatenate(
            [flat_rows(rows_ref[:, own * halves + half]) for half in range(halves)], axis=1
        )
        query_ref[own] = (matmul(normed, weight_ref[0]) * query_factor).astype(BF16)
        key_ref[own] = matmul(normed, weight_ref[1]).astype(BF16)
        value_ref[own] = matmul(normed, weight_ref[2]).astype(BF16)
        gate_ref[own] = jax.nn.sigmoid(matmul(normed, weight_ref[3]))

    first = sequences_here * halves
    tiles = right_ref.shape[1]
    right_ref[...] = rows_ref[:, first : first + tiles]
    keep_all = flat_rows(rows_ref[:, rows_ref.shape[1] - 1])
    keep_all_ref[...] = keep_all
    part = quotient(place_ref[0], groups)
    chosen = one_hot(lanes_of((8, LANES)) == part * sequences_here + rows_of((8, LANES)))
    key_keep_ref[...] = matmul_nt(chosen, keep_all)
    block_rows = min(query_ref.shape[1], 256)

    def finish(block, own, start, mixed):
        part_ref[own, pl.ds(start, block_rows), :] = mixed

    attend_half(
        sizes, place_ref, rows_ref, first + tiles, key_keep_ref, query_ref, key_ref, value_ref, 0,
        block_rows, finish,
    )


def second_row_kernel(
    sizes, place_ref, swapped_ref, part_ref, key_keep_ref, query_ref, key_ref, value_ref,
    gate_ref, mix_ref,
):
    _, _, residues, head_lanes = mix_ref.shape
    block_rows = min(query_ref.shape[1], 256)
    count = block_rows // residues

    def finish(block, own, start, mixed):
        rows = pl.ds(start, block_rows)
        mixed = (part_ref[own, rows, :] + mixed) * gate_ref[own, rows, :]
        mix_ref[pl.ds(block * count, count), own] = mixed.reshape(
            count, residues, head_lanes
        ).astype(BF16)

    tiles = swapped_ref.shape[1] - head_lanes // PER_SPLIT_DIM // 2 * sizes[1] * sizes[2]
    attend_half(
        sizes, place_ref, swapped_ref, tiles, key_keep_ref, query_ref, key_ref, value_ref, 1,
        block_rows, finish,
    )


def outer_kernel(
    sizes, place_ref, keep_all_ref, right0, right1, right2, right3, left_ref, keep_ref,
    weight_ref, out_ref, mixed_s,
):
    groups, sequences, pair = sizes
    residues = keep_ref.shape[0]
    channels, _, depth = weight_ref.shape
    quarter = quotient(place_ref[0], groups) & 3
    left = left_ref[...]
    quarter_channels = channels // 4
    for at in range(0, channels, 2):
        channel = (quarter ^ (at // quarter_channels)) * quarter_channels + at % quarter_channels
        weights = jnp.concatenate([weight_ref[channel], weight_ref[channel + 1]], axis=1)
        product = matmul(left, weights).astype(BF16)
        for residue in range(residues):
            for step in range(2):
                mixed_s[residue, (at + step) * sequences : (at + step + 1) * sequences, :] = product[
                    residue * sequences : (residue + 1) * sequences,
                    step * depth : (step + 1) * depth,
                ]
    right = jnp.concatenate(
        [
            flat_rows(right_ref[:, tile])
            for right_ref in (right0, right1, right2, right3)
            for tile in range(right0.shape[1])
        ],
        axis=1,
    )
    keep_all = keep_all_ref[...]
    for first in range(0, residues, pair):
        members = range(first, first + pair)
        mixed = jnp.concatenate([mixed_s[residue] for residue in members], axis=1)
        keep_rows = jnp.concatenate(
            [
                jnp.broadcast_to(keep_ref[residue : residue + 1, :], (depth, LANES))
                for residue in members
            ],
            axis=0,
        ).astype(BF16)
        result = matmul(right, mixed) / matmul_nt(keep_all, keep_rows)
        for at, residue in enumerate(members):
            out_ref[residue] = result[:, at * depth : (at + 1) * depth].astype(BF16)


def column_kernel(
    sizes, place_ref, x_ref, mix_ref, keep_ref, row_out_ref, query_w_ref, key_w_ref, vg_w_ref,
    out_w_ref, out_ref,
):
    groups = sizes
    sequences, residues, width = x_ref.shape
    total = sequences * residues
    heads = query_w_ref.shape[1] // PER_SPLIT_DIM
    query_factor = PER_SPLIT_DIM ** (-0.5)
    own_group = place_ref[0] & (groups - 1)
    after = x_ref[...].astype(F32).reshape(total, width)
    for at in range(groups):
        group = own_group ^ at
        mixed = mix_ref[:, pl.ds(group, 1)]
        mixed = mixed.astype(F32).reshape(total, mixed.shape[-1]).astype(BF16)
        after = after + matmul(mixed, row_out_ref[at])
    after = after.astype(BF16).astype(F32)
    permutation = residue_major(sequences, residues)
    normed = matmul(permutation, layer_normalize(after)).astype(BF16)
    queries = (matmul(normed, query_w_ref[...]) * query_factor).astype(BF16)
    keys = matmul(normed, key_w_ref[...]).astype(BF16)
    values = matmul(normed, vg_w_ref[0]).astype(BF16)
    gate = jax.nn.sigmoid(matmul(normed, vg_w_ref[1]))

    together = max(1, min(residues, 256 // sequences))
    span = together * sequences
    head_rows = heads * sequences
    inner = heads * PER_SPLIT_DIM
    block_diagonal = quotient(rows_of((head_rows, inner)), sequences) == quotient(
        lanes_of((head_rows, inner)), PER_SPLIT_DIM
    )
    zero = jnp.zeros((head_rows, inner), BF16)

    def by_head(part):
        return jnp.where(block_diagonal, jnp.concatenate([part] * heads, axis=0), zero)

    mixes = []
    for first in range(0, residues, together):
        base = first * sequences
        query_span = queries[base : base + span]
        owner = quotient(rows_of((span, inner)), sequences)
        scores = jnp.zeros((head_rows, span), F32)
        for at in range(together):
            key_part = by_head(keys[base + at * sequences : base + (at + 1) * sequences])
            query_part = jnp.where(owner == at, query_span, jnp.zeros_like(query_span))
            scores = scores + matmul_nt(key_part, query_part)
        spread = one_hot(
            rows_of((residues, span)) == first + quotient(lanes_of((residues, span)), sequences)
        )
        key_keep = matmul_tn(keep_ref[...].astype(BF16), spread)[:sequences]
        scores = scores.reshape(heads, sequences, span)
        scores = jnp.where(key_keep[None] > 0.5, scores, MASKED)
        scores = jnp.exp(scores - jnp.max(scores, axis=1, keepdims=True))
        weights = scores / jnp.sum(scores, axis=1, keepdims=True)
        weights = weights.reshape(head_rows, span).T.astype(BF16)
        for at in range(together):
            value_part = by_head(values[base + at * sequences : base + (at + 1) * sequences])
            mixes.append(matmul(weights[at * sequences : (at + 1) * sequences], value_part))
    mixed = (jnp.concatenate(mixes, axis=0) * gate).astype(BF16)
    mixed = matmul_tn(permutation, mixed).astype(BF16)
    result = after + matmul(mixed, out_w_ref[...])
    out_ref[...] = result.reshape(sequences, residues, width).astype(BF16)


def call(kernel, outs, arguments, scratch=(), scalars=0, mib=32, micros=2, fetch=False):
    vmem = pl.BlockSpec(memory_space=pltpu.VMEM)
    read = pl.BlockSpec(memory_space=pltpu.HBM) if fetch else vmem
    smem = pl.BlockSpec(memory_space=pltpu.SMEM)
    return pl.pallas_call(
        kernel,
        out_shape=outs,
        in_specs=[smem] * scalars + [read] * (len(arguments) - scalars),
        out_specs=jax.tree.map(lambda _: vmem, outs),
        scratch_shapes=list(scratch),
        compiler_params=pltpu.CompilerParams(vmem_limit_bytes=mib * 1024 * 1024),
        cost_estimate=pl.CostEstimate(
            flops=micros * 1_000_000_000, bytes_accessed=micros * 1_000_000, transcendentals=0
        ),
    )(*arguments)


def shards(
    homolog_activity,
    alignment_mask,
    sequence_row_mask,
    pairwise_bias,
    horizontal_projection_matrix,
    horizontal_final_matrix,
    column_query_weight,
    column_key_weight,
    vertical_content_sigmoid_matrix,
    vertical_final_matrix,
    first_operand_matrix,
    second_operand_matrix,
    outer_output_weight,
):
    parallel = lax.axis_size("dap")
    groups = lax.axis_size("grp")
    devices = parallel * groups
    both = ("dap", "grp")
    sequences, residues, width = homolog_activity.shape
    residues_overall = residues * devices
    sequences_here = sequences // parallel
    channels = first_operand_matrix.shape[1]
    depth = outer_output_weight.shape[1]
    heads_here, row_tiles, column_tiles = tile_count(pairwise_bias.shape, groups)
    head_lanes = heads_here * PER_SPLIT_DIM
    large = residues_overall > 256
    place = (lax.axis_index("dap") * groups + lax.axis_index("grp")).astype(jnp.int32).reshape(1)
    shape = jax.ShapeDtypeStruct

    def exchange(value, mask):
        return lax.ppermute(value, both, [(at, at ^ mask) for at in range(devices)])

    def to_all(value):
        return lax.all_to_all(value, both, split_axis=0, concat_axis=0, tiled=True)

    row_out_weight = jnp.stack(
        [horizontal_final_matrix]
        + [exchange(horizontal_final_matrix, relative) for relative in range(1, groups)]
    )

    right_tiles = channels * sequences // LANES
    row_slots = sequences_here * (width // LANES)
    half_tiles = heads_here // 2 * row_tiles * column_tiles
    operands = (
        pairwise_bias,
        alignment_mask.T,
        sequence_row_mask.reshape(1, sequences),
        homolog_activity,
        first_operand_matrix.T,
        second_operand_matrix.T,
    )
    rows_out, left, keep = call(
        functools.partial(prepare_kernel, (groups, sequences_here)),
        (
            shape(
                (devices, row_slots + right_tiles // 4 + half_tiles + 1, residues, LANES), BF16
            ),
            shape((sequences * residues, channels), BF16),
            shape((residues, LANES), F32),
        ),
        operands,
        scratch=[pltpu.VMEM(operand.shape, operand.dtype) for operand in operands]
        + [pltpu.SemaphoreType.DMA((len(operands),))],
        fetch=True,
        mib=62,
    )
    rows_in = to_all(rows_out)

    row_weight = horizontal_projection_matrix.transpose(1, 0, 2)
    outer_weight = outer_output_weight.reshape(channels, channels, depth).transpose(1, 0, 2)
    content_weight = vertical_content_sigmoid_matrix.transpose(1, 0, 2)
    rows_in, row_weight, outer_weight, content_weight, row_out_weight = lax.optimization_barrier(
        (rows_in, row_weight, outer_weight, content_weight, row_out_weight)
    )
    swapped = exchange(rows_in[:, row_slots:-1], groups)

    row_sizes = (groups, row_tiles, column_tiles)
    here = (sequences_here, residues_overall, head_lanes)
    right, part, keep_all, *projected = call(
        functools.partial(first_row_kernel, row_sizes),
        (
            shape((devices, right_tiles // 4, residues, LANES), BF16),
            shape(here, F32),
            shape((residues_overall, LANES), BF16),
            shape((8, residues_overall), F32),
            shape(here, BF16),
            shape(here, BF16),
            shape(here, BF16),
            shape(here, F32),
        ),
        (place, rows_in, row_weight),
        scalars=1,
        mib=60 if large else 32,
    )
    right_across = exchange(right, 2 * groups)
    mix_out = call(
        functools.partial(second_row_kernel, row_sizes),
        shape((devices, sequences_here, residues, head_lanes), BF16),
        (place, swapped, part, *projected),
        scalars=1,
        mib=60 if large else 32,
    )
    mix_in = to_all(mix_out)

    pairwise_update = call(
        functools.partial(outer_kernel, (groups, sequences, 2)),
        shape((residues, residues_overall, depth), BF16),
        (
            place,
            keep_all,
            right,
            swapped,
            right_across,
            exchange(right_across, groups),
            left,
            keep,
            outer_weight,
        ),
        scratch=[pltpu.VMEM((residues, channels * sequences, depth), BF16)],
        scalars=1,
        mib=60 if large else 32,
    )

    alignment_output = call(
        functools.partial(column_kernel, groups),
        shape((sequences, residues, width), BF16),
        (
            place,
            homolog_activity,
            mix_in.reshape(parallel, groups, sequences_here, residues, head_lanes),
            keep,
            row_out_weight,
            column_query_weight,
            column_key_weight,
            content_weight,
            vertical_final_matrix,
        ),
        scalars=1,
        mib=56 if large else 32,
        micros=3,
    )
    return (alignment_output, pairwise_update)


def solution(mesh):
    return jax.shard_map(
        shards,
        mesh=mesh,
        in_specs=(
            P(None, ("dap", "grp"), None),
            P(None, ("dap", "grp")),
            P(),
            P(None, "dap", "grp"),
            P(None, None, "grp"),
            P("grp", None),
            P(),
            P(),
            P(),
            P(),
            P(),
            P(),
            P(),
        ),
        out_specs=(P(None, ("dap", "grp"), None), P(("dap", "grp"), None, None)),
        check_vma=False,
    )
```

```python
import functools

import jax
import jax.numpy as jnp
from jax import lax
from jax.experimental import pallas as pl
from jax.experimental.pallas import tpu as pltpu
from jax.sharding import PartitionSpec as P

PER_SPLIT_DIM = 32
LANES = 128
MASKED = -1000000000.0
F32 = jnp.float32
BF16 = jnp.bfloat16


def matmul(lhs, rhs):
    return jnp.dot(lhs, rhs, preferred_element_type=F32)


def matmul_nt(lhs, rhs):
    return lax.dot_general(lhs, rhs, (((1,), (1,)), ((), ())), preferred_element_type=F32)


def matmul_tn(lhs, rhs):
    return lax.dot_general(lhs, rhs, (((0,), (0,)), ((), ())), preferred_element_type=F32)


def rows_of(shape):
    return lax.broadcasted_iota(jnp.int32, shape, 0)


def lanes_of(shape):
    return lax.broadcasted_iota(jnp.int32, shape, 1)


def quotient(values, divisor):
    return lax.shift_right_logical(values, divisor.bit_length() - 1)


def remainder(values, divisor):
    return values & (divisor - 1)


def one_hot(condition):
    return condition.astype(F32).astype(BF16)


def flat_rows(tiles):
    blocks, sublanes, lanes = tiles.shape
    return tiles.astype(F32).reshape(blocks * sublanes, lanes).astype(BF16)


def layer_normalize(widened):
    centered = widened - jnp.mean(widened, axis=-1, keepdims=True)
    variance = jnp.mean(centered * centered, axis=-1, keepdims=True)
    return (centered * lax.rsqrt(variance + 1e-05)).astype(BF16)


def residue_major(sequences, residues):
    total = sequences * residues
    row, lane = rows_of((total, total)), lanes_of((total, total))
    return one_hot(lane == remainder(row, sequences) * residues + quotient(row, sequences))


def tile_count(bias_shape, groups):
    heads, bias_rows, bias_columns = bias_shape
    return heads // groups, bias_rows // 8, bias_columns // LANES


def share_kernel(
    sizes, bias_hbm, mask_hbm, present_hbm, x_hbm, rows_ref, keep_ref,
    bias_ref, mask_ref, present_ref, x_ref, sems,
):
    groups, sequences_here = sizes
    sources = (bias_hbm, mask_hbm, present_hbm, x_hbm)
    targets = (bias_ref, mask_ref, present_ref, x_ref)
    copies = [
        pltpu.make_async_copy(source, target, sems.at[at])
        for at, (source, target) in enumerate(zip(sources, targets))
    ]
    for copy in copies:
        copy.start()
    for copy in copies[:3]:
        copy.wait()
    sequences, residues, width = x_ref.shape
    heads_here, row_tiles, column_tiles = tile_count(bias_ref.shape, groups)
    half_heads = heads_here // 2
    keep = (mask_ref[...] * present_ref[...]).astype(F32)
    keep_padded = jnp.pad(keep, ((0, 0), (0, LANES - sequences))) if sequences < LANES else keep
    keep_ref[...] = keep_padded
    keep_tile = keep_padded.astype(BF16)
    last = rows_ref.shape[1] - 1
    for target in range(rows_ref.shape[0]):
        part, group = divmod(target, groups)
        slot = last - half_heads * row_tiles * column_tiles
        for head in range(half_heads):
            for row in range(row_tiles):
                for column in range(column_tiles):
                    rows_ref[target, slot] = bias_ref[
                        group * heads_here + part % 2 * half_heads + head,
                        row * 8 : (row + 1) * 8,
                        column * LANES : (column + 1) * LANES,
                    ]
                    slot += 1
        rows_ref[target, last] = keep_tile
    copies[3].wait()
    halves = width // LANES
    for part in range(sequences // sequences_here):
        for own in range(sequences_here):
            for half in range(halves):
                tile = x_ref[
                    part * sequences_here + own, :, half * LANES : (half + 1) * LANES
                ]
                for group in range(groups):
                    rows_ref[part * groups + group, own * halves + half] = tile


def factor_kernel(groups, x_ref, keep_ref, left_w_ref, right_w_ref, right_ref, left_ref):
    sequences, residues, width = x_ref.shape
    total = sequences * residues
    channels = left_w_ref.shape[0]
    keep = keep_ref[:, :sequences]
    normed = layer_normalize(x_ref[...].astype(F32).reshape(total, width))
    left = matmul_nt(normed, left_w_ref[...]).astype(BF16)
    left = matmul(residue_major(sequences, residues), left)
    pick = one_hot(
        quotient(rows_of((total, residues)), sequences) == lanes_of((total, residues))
    )
    own_keep = matmul(pick, keep.astype(BF16))
    at_sequence = remainder(rows_of((total, sequences)), sequences) == lanes_of((total, sequences))
    own_keep = jnp.sum(jnp.where(at_sequence, own_keep, 0.0), axis=1, keepdims=True)
    left_ref[...] = (left * own_keep).astype(BF16)

    right = matmul_nt(normed, right_w_ref[...]).astype(BF16)
    residue_pick = one_hot(
        remainder(lanes_of((residues, total)), residues) == rows_of((residues, total))
    )
    per_tile = LANES // sequences
    spread = one_hot(
        remainder(lanes_of((sequences, LANES)), sequences) == rows_of((sequences, LANES))
    )
    keep_spread = matmul(keep.astype(BF16), spread)
    same_sequence = quotient(rows_of((total, LANES)), residues) == remainder(
        lanes_of((total, LANES)), sequences
    )
    for tile in range(channels // per_tile):
        select = one_hot(
            rows_of((channels, LANES))
            == tile * per_tile + quotient(lanes_of((channels, LANES)), sequences)
        )
        expanded = jnp.where(same_sequence, matmul(right, select), 0.0).astype(BF16)
        result = (matmul(residue_pick, expanded) * keep_spread).astype(BF16)
        core, slot = divmod(tile, right_ref.shape[1])
        for target in range(right_ref.shape[0]):
            if target // groups % 2 == core:
                right_ref[target, slot] = result


def attend_half(
    sizes, place_ref, bias_ref, first_slot, key_keep_ref, query_ref, key_ref, value_ref, other,
    block_rows, finish,
):
    groups, row_tiles, column_tiles = sizes
    sequences_here, residues_overall, head_lanes = query_ref.shape
    half_heads = head_lanes // PER_SPLIT_DIM // 2
    side = (quotient(place_ref[0], groups) & 1) ^ other

    def attend(block):
        start = block * block_rows
        parts = block_rows // (row_tiles * 8)
        head_of = quotient(lanes_of((residues_overall, head_lanes)), PER_SPLIT_DIM)
        query_head = quotient(lanes_of((block_rows, head_lanes)), PER_SPLIT_DIM)
        biases = []
        for head in range(half_heads):
            columns = []
            for group in range(groups):
                for column in range(column_tiles):
                    pieces = []
                    for at in range(parts):
                        for row in range(row_tiles):
                            slot = (head * row_tiles + row) * column_tiles + column
                            slot += first_slot
                            source = (block * parts + at) * groups + group
                            pieces.append(bias_ref[source, slot].astype(F32))
                    columns.append(jnp.concatenate(pieces, axis=0))
            biases.append(jnp.concatenate(columns, axis=1))
        for own in range(sequences_here):
            queries = query_ref[own, pl.ds(start, block_rows), :]
            keys, values = key_ref[own], value_ref[own]
            keep_row = key_keep_ref[own : own + 1, :] > 0.5
            total = jnp.zeros((block_rows, 2 * head_lanes), F32)
            for at in range(half_heads):
                head = side * half_heads + at
                query_part = jnp.where(query_head == head, queries, jnp.zeros_like(queries))
                scores = matmul_nt(query_part, keys) + biases[at]
                scores = jnp.where(keep_row, scores, MASKED)
                scores = scores - jnp.max(scores, axis=1, keepdims=True)
                weights = jnp.exp(scores).astype(BF16)
                mine = head_of == head
                value_part = jnp.where(mine, values, jnp.zeros_like(values))
                total = total + matmul(
                    weights, jnp.concatenate([value_part, one_hot(mine)], axis=1)
                )
            here = quotient(query_head, half_heads) == side
            mixed = total[:, :head_lanes] / jnp.where(here, total[:, head_lanes:], 1.0)
            finish(block, own, start, mixed)

    if residues_overall == block_rows:
        attend(0)
    else:
        pl.loop(0, residues_overall // block_rows)(attend)


def first_row_kernel(
    sizes, place_ref, rows_ref, weight_ref,
    part_ref, keep_all_ref, key_keep_ref, query_ref, key_ref, value_ref, gate_ref,
):
    groups = sizes[0]
    sequences_here = query_ref.shape[0]
    halves = weight_ref.shape[1] // LANES
    query_factor = PER_SPLIT_DIM ** (-0.5)
    for own in range(sequences_here):
        tiles = [rows_ref[:, own * halves + half].astype(F32) for half in range(halves)]
        normed = layer_normalize(
            jnp.concatenate([tile.reshape(-1, LANES) for tile in tiles], axis=1)
        )
        query_ref[own] = (matmul(normed, weight_ref[0]) * query_factor).astype(BF16)
        key_ref[own] = matmul(normed, weight_ref[1]).astype(BF16)
        value_ref[own] = matmul(normed, weight_ref[2]).astype(BF16)
        gate_ref[own] = jax.nn.sigmoid(matmul(normed, weight_ref[3]))

    keep_all = flat_rows(rows_ref[:, rows_ref.shape[1] - 1])
    keep_all_ref[...] = keep_all
    part = quotient(place_ref[0], groups)
    chosen = one_hot(lanes_of((8, LANES)) == part * sequences_here + rows_of((8, LANES)))
    key_keep_ref[...] = matmul_nt(chosen, keep_all)
    block_rows = min(query_ref.shape[1], 256)

    def finish(block, own, start, mixed):
        part_ref[own, pl.ds(start, block_rows), :] = mixed

    attend_half(
        sizes, place_ref, rows_ref, sequences_here * halves, key_keep_ref, query_ref, key_ref,
        value_ref, 0, block_rows, finish,
    )


def second_row_kernel(
    sizes, place_ref, swapped_ref, part_ref, key_keep_ref, query_ref, key_ref, value_ref,
    gate_ref, mix_ref,
):
    _, _, residues, head_lanes = mix_ref.shape
    block_rows = min(query_ref.shape[1], 256)
    count = block_rows // residues

    def finish(block, own, start, mixed):
        rows = pl.ds(start, block_rows)
        mixed = (part_ref[own, rows, :] + mixed) * gate_ref[own, rows, :]
        mix_ref[pl.ds(block * count, count), own] = mixed.reshape(
            count, residues, head_lanes
        ).astype(BF16)

    attend_half(
        sizes, place_ref, swapped_ref, 0, key_keep_ref, query_ref, key_ref, value_ref, 1,
        block_rows, finish,
    )


def outer_kernel(
    sizes, place_ref, keep_all_ref, own_right_ref, other_right_ref, left_ref, keep_ref,
    weight_ref, out_ref, mixed_s,
):
    groups, sequences, pair = sizes
    residues = keep_ref.shape[0]
    channels, _, depth = weight_ref.shape
    core = quotient(place_ref[0], groups) & 1
    left = left_ref[...]
    half_channels = channels // 2
    for at in range(0, channels, 2):
        channel = (core ^ (at // half_channels)) * half_channels + at % half_channels
        weights = jnp.concatenate([weight_ref[channel], weight_ref[channel + 1]], axis=1)
        product = matmul(left, weights).astype(BF16)
        for residue in range(residues):
            for step in range(2):
                mixed_s[residue, (at + step) * sequences : (at + step + 1) * sequences, :] = product[
                    residue * sequences : (residue + 1) * sequences,
                    step * depth : (step + 1) * depth,
                ]
    right = jnp.concatenate(
        [
            flat_rows(right_ref[:, tile])
            for right_ref in (own_right_ref, other_right_ref)
            for tile in range(right_ref.shape[1])
        ],
        axis=1,
    )
    keep_all = keep_all_ref[...]
    for first in range(0, residues, pair):
        members = range(first, first + pair)
        mixed = jnp.concatenate([mixed_s[residue] for residue in members], axis=1)
        keep_rows = jnp.concatenate(
            [
                jnp.broadcast_to(keep_ref[residue : residue + 1, :], (depth, LANES))
                for residue in members
            ],
            axis=0,
        ).astype(BF16)
        result = matmul(right, mixed) / matmul_nt(keep_all, keep_rows)
        for at, residue in enumerate(members):
            out_ref[residue] = result[:, at * depth : (at + 1) * depth].astype(BF16)


def column_kernel(
    sizes, place_ref, x_ref, mix_ref, keep_ref, row_out_ref, query_w_ref, key_w_ref, vg_w_ref,
    out_w_ref, out_ref,
):
    groups = sizes
    sequences, residues, width = x_ref.shape
    total = sequences * residues
    heads = query_w_ref.shape[1] // PER_SPLIT_DIM
    query_factor = PER_SPLIT_DIM ** (-0.5)
    own_group = place_ref[0] & (groups - 1)
    after = x_ref[...].astype(F32).reshape(total, width)
    for at in range(groups):
        group = own_group ^ at
        mixed = mix_ref[:, pl.ds(group, 1)]
        mixed = mixed.astype(F32).reshape(total, mixed.shape[-1]).astype(BF16)
        after = after + matmul(mixed, row_out_ref[at])
    after = after.astype(BF16).astype(F32)
    permutation = residue_major(sequences, residues)
    normed = matmul(permutation, layer_normalize(after)).astype(BF16)
    queries = (matmul(normed, query_w_ref[...]) * query_factor).astype(BF16)
    keys = matmul(normed, key_w_ref[...]).astype(BF16)
    values = matmul(normed, vg_w_ref[0]).astype(BF16)
    gate = jax.nn.sigmoid(matmul(normed, vg_w_ref[1]))

    together = max(1, min(residues, 256 // sequences))
    span = together * sequences
    head_rows = heads * sequences
    inner = heads * PER_SPLIT_DIM
    block_diagonal = quotient(rows_of((head_rows, inner)), sequences) == quotient(
        lanes_of((head_rows, inner)), PER_SPLIT_DIM
    )
    zero = jnp.zeros((head_rows, inner), BF16)

    def by_head(part):
        return jnp.where(block_diagonal, jnp.concatenate([part] * heads, axis=0), zero)

    mixes = []
    for first in range(0, residues, together):
        base = first * sequences
        query_span = queries[base : base + span]
        owner = quotient(rows_of((span, inner)), sequences)
        scores = jnp.zeros((head_rows, span), F32)
        for at in range(together):
            key_part = by_head(keys[base + at * sequences : base + (at + 1) * sequences])
            query_part = jnp.where(owner == at, query_span, jnp.zeros_like(query_span))
            scores = scores + matmul_nt(key_part, query_part)
        spread = one_hot(
            rows_of((residues, span)) == first + quotient(lanes_of((residues, span)), sequences)
        )
        key_keep = matmul_tn(keep_ref[...].astype(BF16), spread)[:sequences]
        scores = scores.reshape(heads, sequences, span)
        scores = jnp.where(key_keep[None] > 0.5, scores, MASKED)
        scores = jnp.exp(scores - jnp.max(scores, axis=1, keepdims=True))
        weights = scores / jnp.sum(scores, axis=1, keepdims=True)
        weights = weights.reshape(head_rows, span).T.astype(BF16)
        for at in range(together):
            value_part = by_head(values[base + at * sequences : base + (at + 1) * sequences])
            mixes.append(matmul(weights[at * sequences : (at + 1) * sequences], value_part))
    mixed = (jnp.concatenate(mixes, axis=0) * gate).astype(BF16)
    mixed = matmul_tn(permutation, mixed).astype(BF16)
    result = after + matmul(mixed, out_w_ref[...])
    out_ref[...] = result.reshape(sequences, residues, width).astype(BF16)


def call(kernel, outs, arguments, scratch=(), scalars=0, mib=32, micros=2, fetch=False):
    vmem = pl.BlockSpec(memory_space=pltpu.VMEM)
    read = pl.BlockSpec(memory_space=pltpu.HBM) if fetch else vmem
    smem = pl.BlockSpec(memory_space=pltpu.SMEM)
    return pl.pallas_call(
        kernel,
        out_shape=outs,
        in_specs=[smem] * scalars + [read] * (len(arguments) - scalars),
        out_specs=jax.tree.map(lambda _: vmem, outs),
        scratch_shapes=list(scratch),
        compiler_params=pltpu.CompilerParams(vmem_limit_bytes=mib * 1024 * 1024),
        cost_estimate=pl.CostEstimate(
            flops=int(micros * 1e9), bytes_accessed=int(micros * 1e6), transcendentals=0
        ),
    )(*arguments)


def shards(
    homolog_activity,
    alignment_mask,
    sequence_row_mask,
    pairwise_bias,
    horizontal_projection_matrix,
    horizontal_final_matrix,
    column_query_weight,
    column_key_weight,
    vertical_content_sigmoid_matrix,
    vertical_final_matrix,
    first_operand_matrix,
    second_operand_matrix,
    outer_output_weight,
):
    parallel = lax.axis_size("dap")
    groups = lax.axis_size("grp")
    devices = parallel * groups
    both = ("dap", "grp")
    sequences, residues, width = homolog_activity.shape
    residues_overall = residues * devices
    sequences_here = sequences // parallel
    channels = first_operand_matrix.shape[1]
    depth = outer_output_weight.shape[1]
    heads_here, row_tiles, column_tiles = tile_count(pairwise_bias.shape, groups)
    head_lanes = heads_here * PER_SPLIT_DIM
    large = residues_overall > 256
    place = (lax.axis_index("dap") * groups + lax.axis_index("grp")).astype(jnp.int32).reshape(1)
    shape = jax.ShapeDtypeStruct

    def exchange(value, mask):
        return lax.ppermute(value, both, [(at, at ^ mask) for at in range(devices)])

    def to_all(value):
        return lax.all_to_all(value, both, split_axis=0, concat_axis=0, tiled=True)

    row_out_weight = jnp.stack(
        [horizontal_final_matrix]
        + [exchange(horizontal_final_matrix, relative) for relative in range(1, groups)]
    )

    right_tiles = channels * sequences // LANES
    row_slots = sequences_here * (width // LANES)
    half_tiles = heads_here // 2 * row_tiles * column_tiles
    operands = (
        pairwise_bias,
        alignment_mask.T,
        sequence_row_mask.reshape(1, sequences),
        homolog_activity,
    )
    rows_out, keep = call(
        functools.partial(share_kernel, (groups, sequences_here)),
        (
            shape((devices, row_slots + half_tiles + 1, residues, LANES), BF16),
            shape((residues, LANES), F32),
        ),
        operands,
        scratch=[pltpu.VMEM(operand.shape, operand.dtype) for operand in operands]
        + [pltpu.SemaphoreType.DMA((len(operands),))],
        fetch=True,
        mib=62,
    )
    rows_in = to_all(rows_out)
    right_out, left = call(
        functools.partial(factor_kernel, groups),
        (
            shape((devices, right_tiles // 2, residues, LANES), BF16),
            shape((sequences * residues, channels), BF16),
        ),
        (homolog_activity, keep, first_operand_matrix.T, second_operand_matrix.T),
        mib=56 if large else 32,
    )
    own_right = to_all(right_out)

    row_weight = horizontal_projection_matrix.transpose(1, 0, 2)
    outer_weight = outer_output_weight.reshape(channels, channels, depth).transpose(1, 0, 2)
    content_weight = vertical_content_sigmoid_matrix.transpose(1, 0, 2)
    rows_in, row_weight, outer_weight, content_weight, row_out_weight = lax.optimization_barrier(
        (rows_in, row_weight, outer_weight, content_weight, row_out_weight)
    )
    other_bias = exchange(rows_in[:, row_slots:-1], groups)

    row_sizes = (groups, row_tiles, column_tiles)
    here = (sequences_here, residues_overall, head_lanes)
    part, keep_all, *projected = call(
        functools.partial(first_row_kernel, row_sizes),
        (
            shape(here, F32),
            shape((residues_overall, LANES), BF16),
            shape((8, residues_overall), F32),
            shape(here, BF16),
            shape(here, BF16),
            shape(here, BF16),
            shape(here, F32),
        ),
        (place, rows_in, row_weight),
        scalars=1,
        mib=60 if large else 32,
        micros=0.1,
    )
    mix_out = call(
        functools.partial(second_row_kernel, row_sizes),
        shape((devices, sequences_here, residues, head_lanes), BF16),
        (place, other_bias, part, *projected),
        scalars=1,
        mib=60 if large else 32,
        micros=0.1,
    )
    mix_in = to_all(mix_out)
    late_right, _ = lax.optimization_barrier((own_right, mix_out))
    other_right = exchange(late_right, groups)

    pairwise_update = call(
        functools.partial(outer_kernel, (groups, sequences, 2)),
        shape((residues, residues_overall, depth), BF16),
        (
            place,
            keep_all,
            own_right,
            other_right,
            left,
            keep,
            outer_weight,
        ),
        scratch=[pltpu.VMEM((residues, channels * sequences, depth), BF16)],
        scalars=1,
        mib=60 if large else 32,
    )

    alignment_output = call(
        functools.partial(column_kernel, groups),
        shape((sequences, residues, width), BF16),
        (
            place,
            homolog_activity,
            mix_in.reshape(parallel, groups, sequences_here, residues, head_lanes),
            keep,
            row_out_weight,
            column_query_weight,
            column_key_weight,
            content_weight,
            vertical_final_matrix,
        ),
        scalars=1,
        mib=56 if large else 32,
        micros=3,
    )
    return (alignment_output, pairwise_update)


def solution(mesh):
    return jax.shard_map(
        shards,
        mesh=mesh,
        in_specs=(
            P(None, ("dap", "grp"), None),
            P(None, ("dap", "grp")),
            P(),
            P(None, "dap", "grp"),
            P(None, None, "grp"),
            P("grp", None),
            P(),
            P(),
            P(),
            P(),
            P(),
            P(),
            P(),
        ),
        out_specs=(P(None, ("dap", "grp"), None), P(("dap", "grp"), None, None)),
        check_vma=False,
    )
```

```python
import functools

import jax
import jax.numpy as jnp
from jax import lax
from jax.experimental import pallas as pl
from jax.experimental.pallas import tpu as pltpu
from jax.sharding import PartitionSpec as P

PER_SPLIT_DIM = 32
LANES = 128
MASKED = -1000000000.0
F32 = jnp.float32
BF16 = jnp.bfloat16


def matmul(lhs, rhs):
    return jnp.dot(lhs, rhs, preferred_element_type=F32)


def matmul_nt(lhs, rhs):
    return lax.dot_general(lhs, rhs, (((1,), (1,)), ((), ())), preferred_element_type=F32)


def matmul_tn(lhs, rhs):
    return lax.dot_general(lhs, rhs, (((0,), (0,)), ((), ())), preferred_element_type=F32)


def rows_of(shape):
    return lax.broadcasted_iota(jnp.int32, shape, 0)


def lanes_of(shape):
    return lax.broadcasted_iota(jnp.int32, shape, 1)


def quotient(values, divisor):
    return lax.shift_right_logical(values, divisor.bit_length() - 1)


def remainder(values, divisor):
    return values & (divisor - 1)


def one_hot(condition):
    return condition.astype(F32).astype(BF16)


def flat_rows(tiles):
    blocks, sublanes, lanes = tiles.shape
    return tiles.astype(F32).reshape(blocks * sublanes, lanes).astype(BF16)


def layer_normalize(widened):
    centered = widened - jnp.mean(widened, axis=-1, keepdims=True)
    variance = jnp.mean(centered * centered, axis=-1, keepdims=True)
    return (centered * lax.rsqrt(variance + 1e-05)).astype(BF16)


def residue_major(sequences, residues):
    total = sequences * residues
    row, lane = rows_of((total, total)), lanes_of((total, total))
    return one_hot(lane == remainder(row, sequences) * residues + quotient(row, sequences))


def tile_count(bias_shape, groups):
    heads, bias_rows, bias_columns = bias_shape
    return heads // groups, bias_rows // 8, bias_columns // LANES


def share_kernel(
    sizes, bias_hbm, mask_hbm, present_hbm, x_hbm, rows_ref, keep_ref,
    bias_ref, mask_ref, present_ref, x_ref, sems,
):
    groups, sequences_here = sizes
    sources = (bias_hbm, mask_hbm, present_hbm, x_hbm)
    targets = (bias_ref, mask_ref, present_ref, x_ref)
    copies = [
        pltpu.make_async_copy(source, target, sems.at[at])
        for at, (source, target) in enumerate(zip(sources, targets))
    ]
    for copy in copies:
        copy.start()
    for copy in copies[:3]:
        copy.wait()
    sequences, residues, width = x_ref.shape
    heads_here, row_tiles, column_tiles = tile_count(bias_ref.shape, groups)
    half_heads = heads_here // 2
    keep = (mask_ref[...] * present_ref[...]).astype(F32)
    keep_padded = jnp.pad(keep, ((0, 0), (0, LANES - sequences))) if sequences < LANES else keep
    keep_ref[...] = keep_padded
    keep_tile = keep_padded.astype(BF16)
    last = rows_ref.shape[1] - 1
    for target in range(rows_ref.shape[0]):
        part, group = divmod(target, groups)
        slot = last - half_heads * row_tiles * column_tiles
        for head in range(half_heads):
            for row in range(row_tiles):
                for column in range(column_tiles):
                    rows_ref[target, slot] = bias_ref[
                        group * heads_here + part % 2 * half_heads + head,
                        row * 8 : (row + 1) * 8,
                        column * LANES : (column + 1) * LANES,
                    ]
                    slot += 1
        rows_ref[target, last] = keep_tile
    copies[3].wait()
    halves = width // LANES
    for part in range(sequences // sequences_here):
        for own in range(sequences_here):
            for half in range(halves):
                tile = x_ref[
                    part * sequences_here + own, :, half * LANES : (half + 1) * LANES
                ]
                for group in range(groups):
                    rows_ref[part * groups + group, own * halves + half] = tile


def factor_kernel(x_ref, keep_ref, left_w_ref, right_w_ref, right_ref, left_ref):
    sequences, residues, width = x_ref.shape
    total = sequences * residues
    channels = left_w_ref.shape[0]
    keep = keep_ref[:, :sequences]
    normed = layer_normalize(x_ref[...].astype(F32).reshape(total, width))
    left = matmul_nt(normed, left_w_ref[...]).astype(BF16)
    left = matmul(residue_major(sequences, residues), left)
    pick = one_hot(
        quotient(rows_of((total, residues)), sequences) == lanes_of((total, residues))
    )
    own_keep = matmul(pick, keep.astype(BF16))
    at_sequence = remainder(rows_of((total, sequences)), sequences) == lanes_of((total, sequences))
    own_keep = jnp.sum(jnp.where(at_sequence, own_keep, 0.0), axis=1, keepdims=True)
    left_ref[...] = (left * own_keep).astype(BF16)

    right = matmul_nt(normed, right_w_ref[...]).astype(BF16)
    residue_pick = one_hot(
        remainder(lanes_of((residues, total)), residues) == rows_of((residues, total))
    )
    per_tile = LANES // sequences
    spread = one_hot(
        remainder(lanes_of((sequences, LANES)), sequences) == rows_of((sequences, LANES))
    )
    keep_spread = matmul(keep.astype(BF16), spread)
    same_sequence = quotient(rows_of((total, LANES)), residues) == remainder(
        lanes_of((total, LANES)), sequences
    )
    for tile in range(channels // per_tile):
        select = one_hot(
            rows_of((channels, LANES))
            == tile * per_tile + quotient(lanes_of((channels, LANES)), sequences)
        )
        expanded = jnp.where(same_sequence, matmul(right, select), 0.0).astype(BF16)
        result = (matmul(residue_pick, expanded) * keep_spread).astype(BF16)
        right_ref[tile] = result


def attend_half(
    sizes, place_ref, bias_ref, first_slot, key_keep_ref, query_ref, key_ref, value_ref, other,
    block_rows, finish,
):
    groups, row_tiles, column_tiles = sizes
    sequences_here, residues_overall, head_lanes = query_ref.shape
    half_heads = head_lanes // PER_SPLIT_DIM // 2
    side = (quotient(place_ref[0], groups) & 1) ^ other

    def attend(block):
        start = block * block_rows
        parts = block_rows // (row_tiles * 8)
        head_of = quotient(lanes_of((residues_overall, head_lanes)), PER_SPLIT_DIM)
        query_head = quotient(lanes_of((block_rows, head_lanes)), PER_SPLIT_DIM)
        biases = []
        for head in range(half_heads):
            columns = []
            for group in range(groups):
                for column in range(column_tiles):
                    pieces = []
                    for at in range(parts):
                        for row in range(row_tiles):
                            slot = (head * row_tiles + row) * column_tiles + column
                            slot += first_slot
                            source = (block * parts + at) * groups + group
                            pieces.append(bias_ref[source, slot].astype(F32))
                    columns.append(jnp.concatenate(pieces, axis=0))
            biases.append(jnp.concatenate(columns, axis=1))
        for own in range(sequences_here):
            queries = query_ref[own, pl.ds(start, block_rows), :]
            keys, values = key_ref[own], value_ref[own]
            keep_row = key_keep_ref[own : own + 1, :] > 0.5
            total = jnp.zeros((block_rows, 2 * head_lanes), F32)
            for at in range(half_heads):
                head = side * half_heads + at
                query_part = jnp.where(query_head == head, queries, jnp.zeros_like(queries))
                scores = matmul_nt(query_part, keys) + biases[at]
                scores = jnp.where(keep_row, scores, MASKED)
                scores = scores - jnp.max(scores, axis=1, keepdims=True)
                weights = jnp.exp(scores).astype(BF16)
                mine = head_of == head
                value_part = jnp.where(mine, values, jnp.zeros_like(values))
                total = total + matmul(
                    weights, jnp.concatenate([value_part, one_hot(mine)], axis=1)
                )
            here = quotient(query_head, half_heads) == side
            mixed = total[:, :head_lanes] / jnp.where(here, total[:, head_lanes:], 1.0)
            finish(block, own, start, mixed)

    if residues_overall == block_rows:
        attend(0)
    else:
        pl.loop(0, residues_overall // block_rows)(attend)


def first_row_kernel(
    sizes, place_ref, rows_ref, weight_ref,
    part_ref, keep_all_ref, key_keep_ref, query_ref, key_ref, value_ref, gate_ref,
):
    groups = sizes[0]
    sequences_here = query_ref.shape[0]
    halves = weight_ref.shape[1] // LANES
    query_factor = PER_SPLIT_DIM ** (-0.5)
    for own in range(sequences_here):
        tiles = [rows_ref[:, own * halves + half].astype(F32) for half in range(halves)]
        normed = layer_normalize(
            jnp.concatenate([tile.reshape(-1, LANES) for tile in tiles], axis=1)
        )
        query_ref[own] = (matmul(normed, weight_ref[0]) * query_factor).astype(BF16)
        key_ref[own] = matmul(normed, weight_ref[1]).astype(BF16)
        value_ref[own] = matmul(normed, weight_ref[2]).astype(BF16)
        gate_ref[own] = jax.nn.sigmoid(matmul(normed, weight_ref[3]))

    keep_all = flat_rows(rows_ref[:, rows_ref.shape[1] - 1])
    keep_all_ref[...] = keep_all
    part = quotient(place_ref[0], groups)
    chosen = one_hot(lanes_of((8, LANES)) == part * sequences_here + rows_of((8, LANES)))
    key_keep_ref[...] = matmul_nt(chosen, keep_all)
    block_rows = min(query_ref.shape[1], 256)

    def finish(block, own, start, mixed):
        part_ref[own, pl.ds(start, block_rows), :] = mixed

    attend_half(
        sizes, place_ref, rows_ref, sequences_here * halves, key_keep_ref, query_ref, key_ref,
        value_ref, 0, block_rows, finish,
    )


def second_row_kernel(
    sizes, place_ref, swapped_ref, part_ref, key_keep_ref, query_ref, key_ref, value_ref,
    gate_ref, mix_ref,
):
    _, _, residues, head_lanes = mix_ref.shape
    block_rows = min(query_ref.shape[1], 256)
    count = block_rows // residues

    def finish(block, own, start, mixed):
        rows = pl.ds(start, block_rows)
        mixed = (part_ref[own, rows, :] + mixed) * gate_ref[own, rows, :]
        mix_ref[pl.ds(block * count, count), own] = mixed.reshape(
            count, residues, head_lanes
        ).astype(BF16)

    attend_half(
        sizes, place_ref, swapped_ref, 0, key_keep_ref, query_ref, key_ref, value_ref, 1,
        block_rows, finish,
    )


def outer_kernel(
    sizes, place_ref, keep_all_ref, *refs
):
    groups, sequences, pair, masks = sizes
    right_refs = refs[: len(masks)]
    left_ref, keep_ref, weight_ref, out_ref, mixed_s, right_s = refs[len(masks) :]
    residues = keep_ref.shape[0]
    channels, _, depth = weight_ref.shape
    left = left_ref[...]
    for channel in range(0, channels, 2):
        weights = jnp.concatenate([weight_ref[channel], weight_ref[channel + 1]], axis=1)
        product = matmul(left, weights).astype(BF16)
        for residue in range(residues):
            for step in range(2):
                mixed_s[
                    residue, (channel + step) * sequences : (channel + step + 1) * sequences, :
                ] = product[
                    residue * sequences : (residue + 1) * sequences,
                    step * depth : (step + 1) * depth,
                ]
    for mask, right_ref in zip(masks, right_refs):
        for at in range(right_ref.shape[0]):
            right_s[place_ref[0] ^ (mask + at * 4 * groups)] = right_ref[at]
    right = jnp.concatenate(
        [flat_rows(right_s[:, tile]) for tile in range(right_s.shape[1])], axis=1
    )
    keep_all = keep_all_ref[...]
    for first in range(0, residues, pair):
        members = range(first, first + pair)
        mixed = jnp.concatenate([mixed_s[residue] for residue in members], axis=1)
        keep_rows = jnp.concatenate(
            [
                jnp.broadcast_to(keep_ref[residue : residue + 1, :], (depth, LANES))
                for residue in members
            ],
            axis=0,
        ).astype(BF16)
        result = matmul(right, mixed) / matmul_nt(keep_all, keep_rows)
        for at, residue in enumerate(members):
            out_ref[residue] = result[:, at * depth : (at + 1) * depth].astype(BF16)


def column_kernel(
    sizes, place_ref, x_ref, mix_ref, keep_ref, row_out_ref, query_w_ref, key_w_ref, vg_w_ref,
    out_w_ref, out_ref,
):
    groups = sizes
    sequences, residues, width = x_ref.shape
    total = sequences * residues
    heads = query_w_ref.shape[1] // PER_SPLIT_DIM
    query_factor = PER_SPLIT_DIM ** (-0.5)
    own_group = place_ref[0] & (groups - 1)
    after = x_ref[...].astype(F32).reshape(total, width)
    for at in range(groups):
        group = own_group ^ at
        mixed = mix_ref[:, pl.ds(group, 1)]
        mixed = mixed.astype(F32).reshape(total, mixed.shape[-1]).astype(BF16)
        after = after + matmul(mixed, row_out_ref[at])
    after = after.astype(BF16).astype(F32)
    permutation = residue_major(sequences, residues)
    normed = matmul(permutation, layer_normalize(after)).astype(BF16)
    queries = (matmul(normed, query_w_ref[...]) * query_factor).astype(BF16)
    keys = matmul(normed, key_w_ref[...]).astype(BF16)
    values = matmul(normed, vg_w_ref[0]).astype(BF16)
    gate = jax.nn.sigmoid(matmul(normed, vg_w_ref[1]))

    together = max(1, min(residues, 256 // sequences))
    span = together * sequences
    head_rows = heads * sequences
    inner = heads * PER_SPLIT_DIM
    block_diagonal = quotient(rows_of((head_rows, inner)), sequences) == quotient(
        lanes_of((head_rows, inner)), PER_SPLIT_DIM
    )
    zero = jnp.zeros((head_rows, inner), BF16)

    def by_head(part):
        return jnp.where(block_diagonal, jnp.concatenate([part] * heads, axis=0), zero)

    mixes = []
    for first in range(0, residues, together):
        base = first * sequences
        query_span = queries[base : base + span]
        owner = quotient(rows_of((span, inner)), sequences)
        scores = jnp.zeros((head_rows, span), F32)
        for at in range(together):
            key_part = by_head(keys[base + at * sequences : base + (at + 1) * sequences])
            query_part = jnp.where(owner == at, query_span, jnp.zeros_like(query_span))
            scores = scores + matmul_nt(key_part, query_part)
        spread = one_hot(
            rows_of((residues, span)) == first + quotient(lanes_of((residues, span)), sequences)
        )
        key_keep = matmul_tn(keep_ref[...].astype(BF16), spread)[:sequences]
        scores = scores.reshape(heads, sequences, span)
        scores = jnp.where(key_keep[None] > 0.5, scores, MASKED)
        scores = jnp.exp(scores - jnp.max(scores, axis=1, keepdims=True))
        weights = scores / jnp.sum(scores, axis=1, keepdims=True)
        weights = weights.reshape(head_rows, span).T.astype(BF16)
        for at in range(together):
            value_part = by_head(values[base + at * sequences : base + (at + 1) * sequences])
            mixes.append(matmul(weights[at * sequences : (at + 1) * sequences], value_part))
    mixed = (jnp.concatenate(mixes, axis=0) * gate).astype(BF16)
    mixed = matmul_tn(permutation, mixed).astype(BF16)
    result = after + matmul(mixed, out_w_ref[...])
    out_ref[...] = result.reshape(sequences, residues, width).astype(BF16)


def call(kernel, outs, arguments, scratch=(), scalars=0, mib=32, micros=2, fetch=False):
    vmem = pl.BlockSpec(memory_space=pltpu.VMEM)
    read = pl.BlockSpec(memory_space=pltpu.HBM) if fetch else vmem
    smem = pl.BlockSpec(memory_space=pltpu.SMEM)
    return pl.pallas_call(
        kernel,
        out_shape=outs,
        in_specs=[smem] * scalars + [read] * (len(arguments) - scalars),
        out_specs=jax.tree.map(lambda _: vmem, outs),
        scratch_shapes=list(scratch),
        compiler_params=pltpu.CompilerParams(vmem_limit_bytes=mib * 1024 * 1024),
        cost_estimate=pl.CostEstimate(
            flops=int(micros * 1e9), bytes_accessed=int(micros * 1e6), transcendentals=0
        ),
    )(*arguments)


def shards(
    homolog_activity,
    alignment_mask,
    sequence_row_mask,
    pairwise_bias,
    horizontal_projection_matrix,
    horizontal_final_matrix,
    column_query_weight,
    column_key_weight,
    vertical_content_sigmoid_matrix,
    vertical_final_matrix,
    first_operand_matrix,
    second_operand_matrix,
    outer_output_weight,
):
    parallel = lax.axis_size("dap")
    groups = lax.axis_size("grp")
    devices = parallel * groups
    both = ("dap", "grp")
    sequences, residues, width = homolog_activity.shape
    residues_overall = residues * devices
    sequences_here = sequences // parallel
    channels = first_operand_matrix.shape[1]
    depth = outer_output_weight.shape[1]
    heads_here, row_tiles, column_tiles = tile_count(pairwise_bias.shape, groups)
    head_lanes = heads_here * PER_SPLIT_DIM
    large = residues_overall > 256
    place = (lax.axis_index("dap") * groups + lax.axis_index("grp")).astype(jnp.int32).reshape(1)
    shape = jax.ShapeDtypeStruct

    def exchange(value, mask):
        return lax.ppermute(value, both, [(at, at ^ mask) for at in range(devices)])

    def to_all(value):
        return lax.all_to_all(value, both, split_axis=0, concat_axis=0, tiled=True)

    row_out_weight = jnp.stack(
        [horizontal_final_matrix]
        + [exchange(horizontal_final_matrix, relative) for relative in range(1, groups)]
    )

    right_tiles = channels * sequences // LANES
    row_slots = sequences_here * (width // LANES)
    half_tiles = heads_here // 2 * row_tiles * column_tiles
    operands = (
        pairwise_bias,
        alignment_mask.T,
        sequence_row_mask.reshape(1, sequences),
        homolog_activity,
    )
    rows_out, keep = call(
        functools.partial(share_kernel, (groups, sequences_here)),
        (
            shape((devices, row_slots + half_tiles + 1, residues, LANES), BF16),
            shape((residues, LANES), F32),
        ),
        operands,
        scratch=[pltpu.VMEM(operand.shape, operand.dtype) for operand in operands]
        + [pltpu.SemaphoreType.DMA((len(operands),))],
        fetch=True,
        mib=62,
    )
    rows_in = to_all(rows_out)
    right_out, left = call(
        factor_kernel,
        (
            shape((right_tiles, residues, LANES), BF16),
            shape((sequences * residues, channels), BF16),
        ),
        (homolog_activity, keep, first_operand_matrix.T, second_operand_matrix.T),
        mib=56 if large else 32,
    )
    right = right_out[None]
    mask = 4 * groups
    while mask < devices:
        right = jnp.concatenate([right, exchange(right, mask)])
        mask *= 2

    row_weight = horizontal_projection_matrix.transpose(1, 0, 2)
    outer_weight = outer_output_weight.reshape(channels, channels, depth).transpose(1, 0, 2)
    content_weight = vertical_content_sigmoid_matrix.transpose(1, 0, 2)
    right_masks, right_parts = [0], [right]
    for mask in (2 * groups, *range(1, groups)):
        right_masks.append(mask)
        right_parts.append(exchange(right, mask))
    rows_in, row_weight, outer_weight, content_weight, row_out_weight, _ = (
        lax.optimization_barrier(
            (rows_in, row_weight, outer_weight, content_weight, row_out_weight, right)
        )
    )
    other_bias = exchange(rows_in[:, row_slots:-1], groups)

    row_sizes = (groups, row_tiles, column_tiles)
    here = (sequences_here, residues_overall, head_lanes)
    part, keep_all, *projected = call(
        functools.partial(first_row_kernel, row_sizes),
        (
            shape(here, F32),
            shape((residues_overall, LANES), BF16),
            shape((8, residues_overall), F32),
            shape(here, BF16),
            shape(here, BF16),
            shape(here, BF16),
            shape(here, F32),
        ),
        (place, rows_in, row_weight),
        scalars=1,
        mib=60 if large else 32,
        micros=0.1,
    )
    mix_out = call(
        functools.partial(second_row_kernel, row_sizes),
        shape((devices, sequences_here, residues, head_lanes), BF16),
        (place, other_bias, part, *projected),
        scalars=1,
        mib=60 if large else 32,
        micros=0.1,
    )
    mix_in = to_all(mix_out)
    *late_parts, _ = lax.optimization_barrier((*right_parts, mix_out))
    for mask in range(1, groups):
        right_masks.append(2 * groups + mask)
        late_parts.append(exchange(late_parts[1], mask))
    right_masks += [mask + groups for mask in right_masks]
    late_parts += [exchange(late_part, groups) for late_part in late_parts]

    pairwise_update = call(
        functools.partial(outer_kernel, (groups, sequences, 2, tuple(right_masks))),
        shape((residues, residues_overall, depth), BF16),
        (
            place,
            keep_all,
            *late_parts,
            left,
            keep,
            outer_weight,
        ),
        scratch=[
            pltpu.VMEM((residues, channels * sequences, depth), BF16),
            pltpu.VMEM((devices, right_tiles, residues, LANES), BF16),
        ],
        scalars=1,
        mib=60 if large else 32,
    )

    alignment_output = call(
        functools.partial(column_kernel, groups),
        shape((sequences, residues, width), BF16),
        (
            place,
            homolog_activity,
            mix_in.reshape(parallel, groups, sequences_here, residues, head_lanes),
            keep,
            row_out_weight,
            column_query_weight,
            column_key_weight,
            content_weight,
            vertical_final_matrix,
        ),
        scalars=1,
        mib=56 if large else 32,
        micros=3,
    )
    return (alignment_output, pairwise_update)


def solution(mesh):
    return jax.shard_map(
        shards,
        mesh=mesh,
        in_specs=(
            P(None, ("dap", "grp"), None),
            P(None, ("dap", "grp")),
            P(),
            P(None, "dap", "grp"),
            P(None, None, "grp"),
            P("grp", None),
            P(),
            P(),
            P(),
            P(),
            P(),
            P(),
            P(),
        ),
        out_specs=(P(None, ("dap", "grp"), None), P(("dap", "grp"), None, None)),
        check_vma=False,
    )
```

```python
import functools

import jax
import jax.numpy as jnp
from jax import lax
from jax.experimental import pallas as pl
from jax.experimental.pallas import tpu as pltpu
from jax.sharding import PartitionSpec as P

PER_SPLIT_DIM = 32
LANES = 128
MASKED = -1000000000.0
F32 = jnp.float32
BF16 = jnp.bfloat16


def matmul(lhs, rhs):
    return jnp.dot(lhs, rhs, preferred_element_type=F32)


def matmul_nt(lhs, rhs):
    return lax.dot_general(lhs, rhs, (((1,), (1,)), ((), ())), preferred_element_type=F32)


def matmul_tn(lhs, rhs):
    return lax.dot_general(lhs, rhs, (((0,), (0,)), ((), ())), preferred_element_type=F32)


def rows_of(shape):
    return lax.broadcasted_iota(jnp.int32, shape, 0)


def lanes_of(shape):
    return lax.broadcasted_iota(jnp.int32, shape, 1)


def quotient(values, divisor):
    return lax.shift_right_logical(values, divisor.bit_length() - 1)


def remainder(values, divisor):
    return values & (divisor - 1)


def one_hot(condition):
    return condition.astype(F32).astype(BF16)


def flat_rows(tiles):
    blocks, sublanes, lanes = tiles.shape
    return tiles.astype(F32).reshape(blocks * sublanes, lanes).astype(BF16)


def layer_normalize(widened):
    centered = widened - jnp.mean(widened, axis=-1, keepdims=True)
    variance = jnp.mean(centered * centered, axis=-1, keepdims=True)
    return (centered * lax.rsqrt(variance + 1e-05)).astype(BF16)


def residue_major(sequences, residues):
    total = sequences * residues
    row, lane = rows_of((total, total)), lanes_of((total, total))
    return one_hot(lane == remainder(row, sequences) * residues + quotient(row, sequences))


def tile_count(bias_shape, groups):
    heads, bias_rows, bias_columns = bias_shape
    return heads // groups, bias_rows // 8, bias_columns // LANES


def share_kernel(
    sizes, bias_hbm, mask_hbm, present_hbm, x_hbm, rows_ref, keep_ref,
    bias_ref, mask_ref, present_ref, x_ref, sems,
):
    groups, sequences_here = sizes
    sources = (bias_hbm, mask_hbm, present_hbm, x_hbm)
    targets = (bias_ref, mask_ref, present_ref, x_ref)
    copies = [
        pltpu.make_async_copy(source, target, sems.at[at])
        for at, (source, target) in enumerate(zip(sources, targets))
    ]
    for copy in copies:
        copy.start()
    for copy in copies[:3]:
        copy.wait()
    sequences, residues, width = x_ref.shape
    heads_here, row_tiles, column_tiles = tile_count(bias_ref.shape, groups)
    half_heads = heads_here // 2
    keep = (mask_ref[...] * present_ref[...]).astype(F32)
    keep_padded = jnp.pad(keep, ((0, 0), (0, LANES - sequences))) if sequences < LANES else keep
    keep_ref[...] = keep_padded
    keep_tile = keep_padded.astype(BF16)
    last = rows_ref.shape[1] - 1
    for target in range(rows_ref.shape[0]):
        part, group = divmod(target, groups)
        slot = last - half_heads * row_tiles * column_tiles
        for head in range(half_heads):
            for row in range(row_tiles):
                for column in range(column_tiles):
                    rows_ref[target, slot] = bias_ref[
                        group * heads_here + part % 2 * half_heads + head,
                        row * 8 : (row + 1) * 8,
                        column * LANES : (column + 1) * LANES,
                    ]
                    slot += 1
        rows_ref[target, last] = keep_tile
    copies[3].wait()
    halves = width // LANES
    for part in range(sequences // sequences_here):
        for own in range(sequences_here):
            for half in range(halves):
                tile = x_ref[
                    part * sequences_here + own, :, half * LANES : (half + 1) * LANES
                ]
                for group in range(groups):
                    rows_ref[part * groups + group, own * halves + half] = tile


def factor_kernel(x_ref, keep_ref, left_w_ref, right_w_ref, right_ref, left_ref):
    sequences, residues, width = x_ref.shape
    total = sequences * residues
    channels = left_w_ref.shape[0]
    keep = keep_ref[:, :sequences]
    normed = layer_normalize(x_ref[...].astype(F32).reshape(total, width))
    left = matmul_nt(normed, left_w_ref[...]).astype(BF16)
    left = matmul(residue_major(sequences, residues), left)
    pick = one_hot(
        quotient(rows_of((total, residues)), sequences) == lanes_of((total, residues))
    )
    own_keep = matmul(pick, keep.astype(BF16))
    at_sequence = remainder(rows_of((total, sequences)), sequences) == lanes_of((total, sequences))
    own_keep = jnp.sum(jnp.where(at_sequence, own_keep, 0.0), axis=1, keepdims=True)
    left_ref[...] = (left * own_keep).astype(BF16)

    right = matmul_nt(normed, right_w_ref[...]).astype(BF16)
    residue_pick = one_hot(
        remainder(lanes_of((residues, total)), residues) == rows_of((residues, total))
    )
    per_tile = LANES // sequences
    spread = one_hot(
        remainder(lanes_of((sequences, LANES)), sequences) == rows_of((sequences, LANES))
    )
    keep_spread = matmul(keep.astype(BF16), spread)
    same_sequence = quotient(rows_of((total, LANES)), residues) == remainder(
        lanes_of((total, LANES)), sequences
    )
    for tile in range(channels // per_tile):
        select = one_hot(
            rows_of((channels, LANES))
            == tile * per_tile + quotient(lanes_of((channels, LANES)), sequences)
        )
        expanded = jnp.where(same_sequence, matmul(right, select), 0.0).astype(BF16)
        result = (matmul(residue_pick, expanded) * keep_spread).astype(BF16)
        right_ref[tile] = result


def attend_half(
    sizes, place_ref, bias_ref, first_slot, key_keep_ref, query_ref, key_ref, value_ref, other,
    block_rows, finish,
):
    groups, row_tiles, column_tiles = sizes
    sequences_here, residues_overall, head_lanes = query_ref.shape
    half_heads = head_lanes // PER_SPLIT_DIM // 2
    side = (quotient(place_ref[0], groups) & 1) ^ other

    def attend(block):
        start = block * block_rows
        parts = block_rows // (row_tiles * 8)
        head_of = quotient(lanes_of((residues_overall, head_lanes)), PER_SPLIT_DIM)
        query_head = quotient(lanes_of((block_rows, head_lanes)), PER_SPLIT_DIM)
        biases = []
        for head in range(half_heads):
            columns = []
            for group in range(groups):
                for column in range(column_tiles):
                    pieces = []
                    for at in range(parts):
                        for row in range(row_tiles):
                            slot = (head * row_tiles + row) * column_tiles + column
                            slot += first_slot
                            source = (block * parts + at) * groups + group
                            pieces.append(bias_ref[source, slot].astype(F32))
                    columns.append(jnp.concatenate(pieces, axis=0))
            biases.append(jnp.concatenate(columns, axis=1))
        for own in range(sequences_here):
            queries = query_ref[own, pl.ds(start, block_rows), :]
            keys, values = key_ref[own], value_ref[own]
            keep_row = key_keep_ref[own : own + 1, :] > 0.5
            total = jnp.zeros((block_rows, 2 * head_lanes), F32)
            for at in range(half_heads):
                head = side * half_heads + at
                query_part = jnp.where(query_head == head, queries, jnp.zeros_like(queries))
                scores = matmul_nt(query_part, keys) + biases[at]
                scores = jnp.where(keep_row, scores, MASKED)
                scores = scores - jnp.max(scores, axis=1, keepdims=True)
                weights = jnp.exp(scores).astype(BF16)
                mine = head_of == head
                value_part = jnp.where(mine, values, jnp.zeros_like(values))
                total = total + matmul(
                    weights, jnp.concatenate([value_part, one_hot(mine)], axis=1)
                )
            here = quotient(query_head, half_heads) == side
            mixed = total[:, :head_lanes] / jnp.where(here, total[:, head_lanes:], 1.0)
            finish(block, own, start, mixed)

    if residues_overall == block_rows:
        attend(0)
    else:
        pl.loop(0, residues_overall // block_rows)(attend)


def first_row_kernel(
    sizes, place_ref, rows_ref, weight_ref,
    part_ref, keep_all_ref, key_keep_ref, query_ref, key_ref, value_ref, gate_ref,
):
    groups = sizes[0]
    sequences_here = query_ref.shape[0]
    halves = weight_ref.shape[1] // LANES
    query_factor = PER_SPLIT_DIM ** (-0.5)
    for own in range(sequences_here):
        tiles = [rows_ref[:, own * halves + half].astype(F32) for half in range(halves)]
        normed = layer_normalize(
            jnp.concatenate([tile.reshape(-1, LANES) for tile in tiles], axis=1)
        )
        query_ref[own] = (matmul(normed, weight_ref[0]) * query_factor).astype(BF16)
        key_ref[own] = matmul(normed, weight_ref[1]).astype(BF16)
        value_ref[own] = matmul(normed, weight_ref[2]).astype(BF16)
        gate_ref[own] = jax.nn.sigmoid(matmul(normed, weight_ref[3]))

    keep_all = flat_rows(rows_ref[:, rows_ref.shape[1] - 1])
    keep_all_ref[...] = keep_all
    part = quotient(place_ref[0], groups)
    chosen = one_hot(lanes_of((8, LANES)) == part * sequences_here + rows_of((8, LANES)))
    key_keep_ref[...] = matmul_nt(chosen, keep_all)
    block_rows = min(query_ref.shape[1], 256)

    def finish(block, own, start, mixed):
        part_ref[own, pl.ds(start, block_rows), :] = mixed

    attend_half(
        sizes, place_ref, rows_ref, sequences_here * halves, key_keep_ref, query_ref, key_ref,
        value_ref, 0, block_rows, finish,
    )


def second_row_kernel(
    sizes, place_ref, swapped_ref, part_ref, key_keep_ref, query_ref, key_ref, value_ref,
    gate_ref, mix_ref,
):
    _, _, residues, head_lanes = mix_ref.shape
    block_rows = min(query_ref.shape[1], 256)
    count = block_rows // residues

    def finish(block, own, start, mixed):
        rows = pl.ds(start, block_rows)
        mixed = (part_ref[own, rows, :] + mixed) * gate_ref[own, rows, :]
        mix_ref[pl.ds(block * count, count), own] = mixed.reshape(
            count, residues, head_lanes
        ).astype(BF16)

    attend_half(
        sizes, place_ref, swapped_ref, 0, key_keep_ref, query_ref, key_ref, value_ref, 1,
        block_rows, finish,
    )


def outer_kernel(
    sizes, place_ref, keep_all_ref, *refs
):
    groups, sequences, pair, masks = sizes
    right_refs = refs[: len(masks)]
    left_ref, keep_ref, weight_ref, out_ref, mixed_s, right_s = refs[len(masks) :]
    residues = keep_ref.shape[0]
    channels, _, depth = weight_ref.shape
    left = left_ref[...]
    for channel in range(0, channels, 2):
        weights = jnp.concatenate([weight_ref[channel], weight_ref[channel + 1]], axis=1)
        product = matmul(left, weights).astype(BF16)
        for residue in range(residues):
            for step in range(2):
                mixed_s[
                    residue, (channel + step) * sequences : (channel + step + 1) * sequences, :
                ] = product[
                    residue * sequences : (residue + 1) * sequences,
                    step * depth : (step + 1) * depth,
                ]
    for mask, right_ref in zip(masks, right_refs):
        for at in range(right_ref.shape[0]):
            right_s[place_ref[0] ^ (mask + at * 4 * groups)] = right_ref[at]
    right = jnp.concatenate(
        [flat_rows(right_s[:, tile]) for tile in range(right_s.shape[1])], axis=1
    )
    keep_all = keep_all_ref[...]
    for first in range(0, residues, pair):
        members = range(first, first + pair)
        mixed = jnp.concatenate([mixed_s[residue] for residue in members], axis=1)
        keep_rows = jnp.concatenate(
            [
                jnp.broadcast_to(keep_ref[residue : residue + 1, :], (depth, LANES))
                for residue in members
            ],
            axis=0,
        ).astype(BF16)
        result = matmul(right, mixed) / matmul_nt(keep_all, keep_rows)
        for at, residue in enumerate(members):
            out_ref[residue] = result[:, at * depth : (at + 1) * depth].astype(BF16)


def column_kernel(
    sizes, place_ref, x_ref, mix_ref, keep_ref, row_out_ref, query_w_ref, key_w_ref, vg_w_ref,
    out_w_ref, out_ref,
):
    groups = sizes
    sequences, residues, width = x_ref.shape
    total = sequences * residues
    heads = query_w_ref.shape[1] // PER_SPLIT_DIM
    query_factor = PER_SPLIT_DIM ** (-0.5)
    own_group = place_ref[0] & (groups - 1)
    after = x_ref[...].astype(F32).reshape(total, width)
    for at in range(groups):
        group = own_group ^ at
        mixed = mix_ref[:, pl.ds(group, 1)]
        mixed = mixed.astype(F32).reshape(total, mixed.shape[-1]).astype(BF16)
        after = after + matmul(mixed, row_out_ref[at])
    after = after.astype(BF16).astype(F32)
    permutation = residue_major(sequences, residues)
    normed = matmul(permutation, layer_normalize(after)).astype(BF16)
    queries = (matmul(normed, query_w_ref[...]) * query_factor).astype(BF16)
    keys = matmul(normed, key_w_ref[...]).astype(BF16)
    values = matmul(normed, vg_w_ref[0]).astype(BF16)
    gate = jax.nn.sigmoid(matmul(normed, vg_w_ref[1]))

    together = max(1, min(residues, 256 // sequences))
    span = together * sequences
    head_rows = heads * sequences
    inner = heads * PER_SPLIT_DIM
    block_diagonal = quotient(rows_of((head_rows, inner)), sequences) == quotient(
        lanes_of((head_rows, inner)), PER_SPLIT_DIM
    )
    zero = jnp.zeros((head_rows, inner), BF16)

    def by_head(part):
        return jnp.where(block_diagonal, jnp.concatenate([part] * heads, axis=0), zero)

    mixes = []
    for first in range(0, residues, together):
        base = first * sequences
        query_span = queries[base : base + span]
        owner = quotient(rows_of((span, inner)), sequences)
        scores = jnp.zeros((head_rows, span), F32)
        for at in range(together):
            key_part = by_head(keys[base + at * sequences : base + (at + 1) * sequences])
            query_part = jnp.where(owner == at, query_span, jnp.zeros_like(query_span))
            scores = scores + matmul_nt(key_part, query_part)
        spread = one_hot(
            rows_of((residues, span)) == first + quotient(lanes_of((residues, span)), sequences)
        )
        key_keep = matmul_tn(keep_ref[...].astype(BF16), spread)[:sequences]
        scores = scores.reshape(heads, sequences, span)
        scores = jnp.where(key_keep[None] > 0.5, scores, MASKED)
        scores = jnp.exp(scores - jnp.max(scores, axis=1, keepdims=True))
        weights = scores / jnp.sum(scores, axis=1, keepdims=True)
        weights = weights.reshape(head_rows, span).T.astype(BF16)
        for at in range(together):
            value_part = by_head(values[base + at * sequences : base + (at + 1) * sequences])
            mixes.append(matmul(weights[at * sequences : (at + 1) * sequences], value_part))
    mixed = (jnp.concatenate(mixes, axis=0) * gate).astype(BF16)
    mixed = matmul_tn(permutation, mixed).astype(BF16)
    result = after + matmul(mixed, out_w_ref[...])
    out_ref[...] = result.reshape(sequences, residues, width).astype(BF16)


def call(kernel, outs, arguments, scratch=(), scalars=0, mib=32, micros=2, fetch=False):
    vmem = pl.BlockSpec(memory_space=pltpu.VMEM)
    read = pl.BlockSpec(memory_space=pltpu.HBM) if fetch else vmem
    smem = pl.BlockSpec(memory_space=pltpu.SMEM)
    return pl.pallas_call(
        kernel,
        out_shape=outs,
        in_specs=[smem] * scalars + [read] * (len(arguments) - scalars),
        out_specs=jax.tree.map(lambda _: vmem, outs),
        scratch_shapes=list(scratch),
        compiler_params=pltpu.CompilerParams(vmem_limit_bytes=mib * 1024 * 1024),
        cost_estimate=pl.CostEstimate(
            flops=int(micros * 1e9), bytes_accessed=int(micros * 1e6), transcendentals=0
        ),
    )(*arguments)


def shards(
    homolog_activity,
    alignment_mask,
    sequence_row_mask,
    pairwise_bias,
    horizontal_projection_matrix,
    horizontal_final_matrix,
    column_query_weight,
    column_key_weight,
    vertical_content_sigmoid_matrix,
    vertical_final_matrix,
    first_operand_matrix,
    second_operand_matrix,
    outer_output_weight,
):
    parallel = lax.axis_size("dap")
    groups = lax.axis_size("grp")
    devices = parallel * groups
    both = ("dap", "grp")
    sequences, residues, width = homolog_activity.shape
    residues_overall = residues * devices
    sequences_here = sequences // parallel
    channels = first_operand_matrix.shape[1]
    depth = outer_output_weight.shape[1]
    heads_here, row_tiles, column_tiles = tile_count(pairwise_bias.shape, groups)
    head_lanes = heads_here * PER_SPLIT_DIM
    large = residues_overall > 256
    place = (lax.axis_index("dap") * groups + lax.axis_index("grp")).astype(jnp.int32).reshape(1)
    shape = jax.ShapeDtypeStruct

    def exchange(value, mask):
        return lax.ppermute(value, both, [(at, at ^ mask) for at in range(devices)])

    def to_all(value):
        return lax.all_to_all(value, both, split_axis=0, concat_axis=0, tiled=True)

    right_tiles = channels * sequences // LANES
    row_slots = sequences_here * (width // LANES)
    half_tiles = heads_here // 2 * row_tiles * column_tiles
    operands = (
        pairwise_bias,
        alignment_mask.T,
        sequence_row_mask.reshape(1, sequences),
        homolog_activity,
    )
    rows_out, keep = call(
        functools.partial(share_kernel, (groups, sequences_here)),
        (
            shape((devices, row_slots + half_tiles + 1, residues, LANES), BF16),
            shape((residues, LANES), F32),
        ),
        operands,
        scratch=[pltpu.VMEM(operand.shape, operand.dtype) for operand in operands]
        + [pltpu.SemaphoreType.DMA((len(operands),))],
        fetch=True,
        mib=62,
    )
    rows_in = to_all(rows_out)
    right_out, left = call(
        factor_kernel,
        (
            shape((right_tiles, residues, LANES), BF16),
            shape((sequences * residues, channels), BF16),
        ),
        (homolog_activity, keep, first_operand_matrix.T, second_operand_matrix.T),
        mib=56 if large else 32,
    )
    right = right_out[None]
    mask = 4 * groups
    while mask < devices:
        right = jnp.concatenate([right, exchange(right, mask)])
        mask *= 2

    row_weight = horizontal_projection_matrix.transpose(1, 0, 2)
    outer_weight = outer_output_weight.reshape(channels, channels, depth).transpose(1, 0, 2)
    content_weight = vertical_content_sigmoid_matrix.transpose(1, 0, 2)
    rows_in, row_weight, outer_weight, content_weight, right = lax.optimization_barrier(
        (rows_in, row_weight, outer_weight, content_weight, right)
    )
    other_bias = exchange(rows_in[:, row_slots:-1], groups)

    row_sizes = (groups, row_tiles, column_tiles)
    here = (sequences_here, residues_overall, head_lanes)
    part, keep_all, *projected = call(
        functools.partial(first_row_kernel, row_sizes),
        (
            shape(here, F32),
            shape((residues_overall, LANES), BF16),
            shape((8, residues_overall), F32),
            shape(here, BF16),
            shape(here, BF16),
            shape(here, BF16),
            shape(here, F32),
        ),
        (place, rows_in, row_weight),
        scalars=1,
        mib=60 if large else 32,
        micros=0.1,
    )
    mix_out = call(
        functools.partial(second_row_kernel, row_sizes),
        shape((devices, sequences_here, residues, head_lanes), BF16),
        (place, other_bias, part, *projected),
        scalars=1,
        mib=60 if large else 32,
        micros=0.1,
    )
    mix_in = to_all(mix_out)
    right, own_final, _ = lax.optimization_barrier((right, horizontal_final_matrix, mix_out))
    right_masks, late_parts = [0], [right]
    for mask in (2 * groups, *range(1, groups)):
        right_masks.append(mask)
        late_parts.append(exchange(right, mask))
    row_out_weight = jnp.stack(
        [own_final] + [exchange(own_final, relative) for relative in range(1, groups)]
    )
    for mask in range(1, groups):
        right_masks.append(2 * groups + mask)
        late_parts.append(exchange(late_parts[1], mask))
    right_masks += [mask + groups for mask in right_masks]
    late_parts += [exchange(late_part, groups) for late_part in late_parts]

    pairwise_update = call(
        functools.partial(outer_kernel, (groups, sequences, 2, tuple(right_masks))),
        shape((residues, residues_overall, depth), BF16),
        (
            place,
            keep_all,
            *late_parts,
            left,
            keep,
            outer_weight,
        ),
        scratch=[
            pltpu.VMEM((residues, channels * sequences, depth), BF16),
            pltpu.VMEM((devices, right_tiles, residues, LANES), BF16),
        ],
        scalars=1,
        mib=60 if large else 32,
    )

    alignment_output = call(
        functools.partial(column_kernel, groups),
        shape((sequences, residues, width), BF16),
        (
            place,
            homolog_activity,
            mix_in.reshape(parallel, groups, sequences_here, residues, head_lanes),
            keep,
            row_out_weight,
            column_query_weight,
            column_key_weight,
            content_weight,
            vertical_final_matrix,
        ),
        scalars=1,
        mib=56 if large else 32,
        micros=3,
    )
    return (alignment_output, pairwise_update)


def solution(mesh):
    return jax.shard_map(
        shards,
        mesh=mesh,
        in_specs=(
            P(None, ("dap", "grp"), None),
            P(None, ("dap", "grp")),
            P(),
            P(None, "dap", "grp"),
            P(None, None, "grp"),
            P("grp", None),
            P(),
            P(),
            P(),
            P(),
            P(),
            P(),
            P(),
        ),
        out_specs=(P(None, ("dap", "grp"), None), P(("dap", "grp"), None, None)),
        check_vma=False,
    )
```

```python
import functools

import jax
import jax.numpy as jnp
from jax import lax
from jax.experimental import pallas as pl
from jax.experimental.pallas import tpu as pltpu
from jax.sharding import PartitionSpec as P

PER_SPLIT_DIM = 32
LANES = 128
MASKED = -1000000000.0
F32 = jnp.float32
BF16 = jnp.bfloat16


def matmul(lhs, rhs):
    return jnp.dot(lhs, rhs, preferred_element_type=F32)


def matmul_nt(lhs, rhs):
    return lax.dot_general(lhs, rhs, (((1,), (1,)), ((), ())), preferred_element_type=F32)


def matmul_tn(lhs, rhs):
    return lax.dot_general(lhs, rhs, (((0,), (0,)), ((), ())), preferred_element_type=F32)


def rows_of(shape):
    return lax.broadcasted_iota(jnp.int32, shape, 0)


def lanes_of(shape):
    return lax.broadcasted_iota(jnp.int32, shape, 1)


def quotient(values, divisor):
    return lax.shift_right_logical(values, divisor.bit_length() - 1)


def remainder(values, divisor):
    return values & (divisor - 1)


def one_hot(condition):
    return condition.astype(F32).astype(BF16)


def flat_rows(tiles):
    blocks, sublanes, lanes = tiles.shape
    return tiles.astype(F32).reshape(blocks * sublanes, lanes).astype(BF16)


def layer_normalize(widened):
    centered = widened - jnp.mean(widened, axis=-1, keepdims=True)
    variance = jnp.mean(centered * centered, axis=-1, keepdims=True)
    return (centered * lax.rsqrt(variance + 1e-05)).astype(BF16)


def residue_major(sequences, residues):
    total = sequences * residues
    row, lane = rows_of((total, total)), lanes_of((total, total))
    return one_hot(lane == remainder(row, sequences) * residues + quotient(row, sequences))


def tile_count(bias_shape, groups):
    heads, bias_rows, bias_columns = bias_shape
    return heads // groups, bias_rows // 8, bias_columns // LANES


def share_kernel(
    sizes, bias_hbm, mask_hbm, present_hbm, x_hbm, rows_ref, keep_ref,
    bias_ref, mask_ref, present_ref, x_ref, sems,
):
    groups, sequences_here = sizes
    sources = (bias_hbm, mask_hbm, present_hbm, x_hbm)
    targets = (bias_ref, mask_ref, present_ref, x_ref)
    copies = [
        pltpu.make_async_copy(source, target, sems.at[at])
        for at, (source, target) in enumerate(zip(sources, targets))
    ]
    for copy in copies:
        copy.start()
    for copy in copies[:3]:
        copy.wait()
    sequences, residues, width = x_ref.shape
    heads_here, row_tiles, column_tiles = tile_count(bias_ref.shape, groups)
    half_heads = heads_here // 2
    keep = (mask_ref[...] * present_ref[...]).astype(F32)
    keep_padded = jnp.pad(keep, ((0, 0), (0, LANES - sequences))) if sequences < LANES else keep
    keep_ref[...] = keep_padded
    keep_tile = keep_padded.astype(BF16)
    last = rows_ref.shape[1] - 1
    for target in range(rows_ref.shape[0]):
        part, group = divmod(target, groups)
        slot = last - half_heads * row_tiles * column_tiles
        for head in range(half_heads):
            for row in range(row_tiles):
                for column in range(column_tiles):
                    rows_ref[target, slot] = bias_ref[
                        group * heads_here + part % 2 * half_heads + head,
                        row * 8 : (row + 1) * 8,
                        column * LANES : (column + 1) * LANES,
                    ]
                    slot += 1
        rows_ref[target, last] = keep_tile
    copies[3].wait()
    halves = width // LANES
    for part in range(sequences // sequences_here):
        for own in range(sequences_here):
            for half in range(halves):
                tile = x_ref[
                    part * sequences_here + own, :, half * LANES : (half + 1) * LANES
                ]
                for group in range(groups):
                    rows_ref[part * groups + group, own * halves + half] = tile


def factor_kernel(x_ref, keep_ref, left_w_ref, right_w_ref, right_ref, left_ref):
    sequences, residues, width = x_ref.shape
    total = sequences * residues
    channels = left_w_ref.shape[0]
    keep = keep_ref[:, :sequences]
    normed = layer_normalize(x_ref[...].astype(F32).reshape(total, width))
    left = matmul_nt(normed, left_w_ref[...]).astype(BF16)
    left = matmul(residue_major(sequences, residues), left)
    pick = one_hot(
        quotient(rows_of((total, residues)), sequences) == lanes_of((total, residues))
    )
    own_keep = matmul(pick, keep.astype(BF16))
    at_sequence = remainder(rows_of((total, sequences)), sequences) == lanes_of((total, sequences))
    own_keep = jnp.sum(jnp.where(at_sequence, own_keep, 0.0), axis=1, keepdims=True)
    left_ref[...] = (left * own_keep).astype(BF16)

    right = matmul_nt(normed, right_w_ref[...]).astype(BF16)
    residue_pick = one_hot(
        remainder(lanes_of((residues, total)), residues) == rows_of((residues, total))
    )
    per_tile = LANES // sequences
    spread = one_hot(
        remainder(lanes_of((sequences, LANES)), sequences) == rows_of((sequences, LANES))
    )
    keep_spread = matmul(keep.astype(BF16), spread)
    same_sequence = quotient(rows_of((total, LANES)), residues) == remainder(
        lanes_of((total, LANES)), sequences
    )
    for tile in range(channels // per_tile):
        select = one_hot(
            rows_of((channels, LANES))
            == tile * per_tile + quotient(lanes_of((channels, LANES)), sequences)
        )
        expanded = jnp.where(same_sequence, matmul(right, select), 0.0).astype(BF16)
        result = (matmul(residue_pick, expanded) * keep_spread).astype(BF16)
        right_ref[tile] = result


def attend_half(
    sizes, place_ref, bias_ref, first_slot, key_keep_ref, query_ref, key_ref, value_ref, other,
    block_rows, finish,
):
    groups, row_tiles, column_tiles = sizes
    sequences_here, residues_overall, head_lanes = query_ref.shape
    half_heads = head_lanes // PER_SPLIT_DIM // 2
    side = (quotient(place_ref[0], groups) & 1) ^ other

    def attend(block):
        start = block * block_rows
        parts = block_rows // (row_tiles * 8)
        head_of = quotient(lanes_of((residues_overall, head_lanes)), PER_SPLIT_DIM)
        query_head = quotient(lanes_of((block_rows, head_lanes)), PER_SPLIT_DIM)
        biases = []
        for head in range(half_heads):
            columns = []
            for group in range(groups):
                for column in range(column_tiles):
                    pieces = []
                    for at in range(parts):
                        for row in range(row_tiles):
                            slot = (head * row_tiles + row) * column_tiles + column
                            slot += first_slot
                            source = (block * parts + at) * groups + group
                            pieces.append(bias_ref[source, slot].astype(F32))
                    columns.append(jnp.concatenate(pieces, axis=0))
            biases.append(jnp.concatenate(columns, axis=1))
        for own in range(sequences_here):
            queries = query_ref[own, pl.ds(start, block_rows), :]
            keys, values = key_ref[own], value_ref[own]
            keep_row = key_keep_ref[own : own + 1, :] > 0.5
            total = jnp.zeros((block_rows, 2 * head_lanes), F32)
            for at in range(half_heads):
                head = side * half_heads + at
                query_part = jnp.where(query_head == head, queries, jnp.zeros_like(queries))
                scores = matmul_nt(query_part, keys) + biases[at]
                scores = jnp.where(keep_row, scores, MASKED)
                scores = scores - jnp.max(scores, axis=1, keepdims=True)
                weights = jnp.exp(scores).astype(BF16)
                mine = head_of == head
                value_part = jnp.where(mine, values, jnp.zeros_like(values))
                total = total + matmul(
                    weights, jnp.concatenate([value_part, one_hot(mine)], axis=1)
                )
            here = quotient(query_head, half_heads) == side
            mixed = total[:, :head_lanes] / jnp.where(here, total[:, head_lanes:], 1.0)
            finish(block, own, start, mixed)

    if residues_overall == block_rows:
        attend(0)
    else:
        pl.loop(0, residues_overall // block_rows)(attend)


def first_row_kernel(
    sizes, place_ref, rows_ref, weight_ref,
    part_ref, keep_all_ref, key_keep_ref, query_ref, key_ref, value_ref, gate_ref,
):
    groups = sizes[0]
    sequences_here = query_ref.shape[0]
    halves = weight_ref.shape[1] // LANES
    query_factor = PER_SPLIT_DIM ** (-0.5)
    for own in range(sequences_here):
        tiles = [rows_ref[:, own * halves + half].astype(F32) for half in range(halves)]
        normed = layer_normalize(
            jnp.concatenate([tile.reshape(-1, LANES) for tile in tiles], axis=1)
        )
        query_ref[own] = (matmul(normed, weight_ref[0]) * query_factor).astype(BF16)
        key_ref[own] = matmul(normed, weight_ref[1]).astype(BF16)
        value_ref[own] = matmul(normed, weight_ref[2]).astype(BF16)
        gate_ref[own] = jax.nn.sigmoid(matmul(normed, weight_ref[3]))

    keep_all = flat_rows(rows_ref[:, rows_ref.shape[1] - 1])
    keep_all_ref[...] = keep_all
    part = quotient(place_ref[0], groups)
    chosen = one_hot(lanes_of((8, LANES)) == part * sequences_here + rows_of((8, LANES)))
    key_keep_ref[...] = matmul_nt(chosen, keep_all)
    block_rows = min(query_ref.shape[1], 256)

    def finish(block, own, start, mixed):
        part_ref[own, pl.ds(start, block_rows), :] = mixed

    attend_half(
        sizes, place_ref, rows_ref, sequences_here * halves, key_keep_ref, query_ref, key_ref,
        value_ref, 0, block_rows, finish,
    )


def second_row_kernel(
    sizes, place_ref, swapped_ref, part_ref, key_keep_ref, query_ref, key_ref, value_ref,
    gate_ref, mix_ref,
):
    _, _, residues, head_lanes = mix_ref.shape
    block_rows = min(query_ref.shape[1], 256)
    count = block_rows // residues

    def finish(block, own, start, mixed):
        rows = pl.ds(start, block_rows)
        mixed = (part_ref[own, rows, :] + mixed) * gate_ref[own, rows, :]
        mix_ref[pl.ds(block * count, count), own] = mixed.reshape(
            count, residues, head_lanes
        ).astype(BF16)

    attend_half(
        sizes, place_ref, swapped_ref, 0, key_keep_ref, query_ref, key_ref, value_ref, 1,
        block_rows, finish,
    )


def outer_kernel(
    sizes, place_ref, keep_all_ref, *refs
):
    groups, sequences, pair, masks = sizes
    right_refs = refs[: len(masks)]
    left_ref, keep_ref, weight_ref, out_ref, mixed_s, right_s = refs[len(masks) :]
    residues = keep_ref.shape[0]
    channels, _, depth = weight_ref.shape
    left = left_ref[...]
    for channel in range(0, channels, 2):
        weights = jnp.concatenate([weight_ref[channel], weight_ref[channel + 1]], axis=1)
        product = matmul(left, weights).astype(BF16)
        for residue in range(residues):
            for step in range(2):
                mixed_s[
                    residue, (channel + step) * sequences : (channel + step + 1) * sequences, :
                ] = product[
                    residue * sequences : (residue + 1) * sequences,
                    step * depth : (step + 1) * depth,
                ]
    for mask, right_ref in zip(masks, right_refs):
        for at in range(right_ref.shape[0]):
            right_s[place_ref[0] ^ (mask + at * 4 * groups)] = right_ref[at]
    right = jnp.concatenate(
        [flat_rows(right_s[:, tile]) for tile in range(right_s.shape[1])], axis=1
    )
    keep_all = keep_all_ref[...]
    for first in range(0, residues, pair):
        members = range(first, first + pair)
        mixed = jnp.concatenate([mixed_s[residue] for residue in members], axis=1)
        keep_rows = jnp.concatenate(
            [
                jnp.broadcast_to(keep_ref[residue : residue + 1, :], (depth, LANES))
                for residue in members
            ],
            axis=0,
        ).astype(BF16)
        result = matmul(right, mixed) / matmul_nt(keep_all, keep_rows)
        for at, residue in enumerate(members):
            out_ref[residue] = result[:, at * depth : (at + 1) * depth].astype(BF16)


def column_kernel(
    sizes, place_ref, x_ref, mix_ref, keep_ref, row_out_ref, query_w_ref, key_w_ref, vg_w_ref,
    out_w_ref, out_ref,
):
    groups = sizes
    sequences, residues, width = x_ref.shape
    total = sequences * residues
    heads = query_w_ref.shape[1] // PER_SPLIT_DIM
    query_factor = PER_SPLIT_DIM ** (-0.5)
    own_group = place_ref[0] & (groups - 1)
    after = x_ref[...].astype(F32).reshape(total, width)
    for at in range(groups):
        group = own_group ^ at
        mixed = mix_ref[:, pl.ds(group, 1)]
        mixed = mixed.astype(F32).reshape(total, mixed.shape[-1]).astype(BF16)
        after = after + matmul(mixed, row_out_ref[at])
    after = after.astype(BF16).astype(F32)
    permutation = residue_major(sequences, residues)
    normed = matmul(permutation, layer_normalize(after)).astype(BF16)
    queries = (matmul(normed, query_w_ref[...]) * query_factor).astype(BF16)
    keys = matmul(normed, key_w_ref[...]).astype(BF16)
    values = matmul(normed, vg_w_ref[0]).astype(BF16)
    gate = jax.nn.sigmoid(matmul(normed, vg_w_ref[1]))

    together = max(1, min(residues, 256 // sequences))
    span = together * sequences
    head_rows = heads * sequences
    inner = heads * PER_SPLIT_DIM
    block_diagonal = quotient(rows_of((head_rows, inner)), sequences) == quotient(
        lanes_of((head_rows, inner)), PER_SPLIT_DIM
    )
    zero = jnp.zeros((head_rows, inner), BF16)

    def by_head(part):
        return jnp.where(block_diagonal, jnp.concatenate([part] * heads, axis=0), zero)

    mixes = []
    for first in range(0, residues, together):
        base = first * sequences
        query_span = queries[base : base + span]
        owner = quotient(rows_of((span, inner)), sequences)
        scores = jnp.zeros((head_rows, span), F32)
        for at in range(together):
            key_part = by_head(keys[base + at * sequences : base + (at + 1) * sequences])
            query_part = jnp.where(owner == at, query_span, jnp.zeros_like(query_span))
            scores = scores + matmul_nt(key_part, query_part)
        spread = one_hot(
            rows_of((residues, span)) == first + quotient(lanes_of((residues, span)), sequences)
        )
        key_keep = matmul_tn(keep_ref[...].astype(BF16), spread)[:sequences]
        scores = scores.reshape(heads, sequences, span)
        scores = jnp.where(key_keep[None] > 0.5, scores, MASKED)
        scores = jnp.exp(scores - jnp.max(scores, axis=1, keepdims=True))
        weights = scores / jnp.sum(scores, axis=1, keepdims=True)
        weights = weights.reshape(head_rows, span).T.astype(BF16)
        for at in range(together):
            value_part = by_head(values[base + at * sequences : base + (at + 1) * sequences])
            mixes.append(matmul(weights[at * sequences : (at + 1) * sequences], value_part))
    mixed = (jnp.concatenate(mixes, axis=0) * gate).astype(BF16)
    mixed = matmul_tn(permutation, mixed).astype(BF16)
    result = after + matmul(mixed, out_w_ref[...])
    out_ref[...] = result.reshape(sequences, residues, width).astype(BF16)


def call(kernel, outs, arguments, scratch=(), scalars=0, mib=32, micros=2, fetch=False):
    vmem = pl.BlockSpec(memory_space=pltpu.VMEM)
    read = pl.BlockSpec(memory_space=pltpu.HBM) if fetch else vmem
    smem = pl.BlockSpec(memory_space=pltpu.SMEM)
    return pl.pallas_call(
        kernel,
        out_shape=outs,
        in_specs=[smem] * scalars + [read] * (len(arguments) - scalars),
        out_specs=jax.tree.map(lambda _: vmem, outs),
        scratch_shapes=list(scratch),
        compiler_params=pltpu.CompilerParams(vmem_limit_bytes=mib * 1024 * 1024),
        cost_estimate=pl.CostEstimate(
            flops=int(micros * 1e9), bytes_accessed=int(micros * 1e6), transcendentals=0
        ),
    )(*arguments)


def shards(
    homolog_activity,
    alignment_mask,
    sequence_row_mask,
    pairwise_bias,
    horizontal_projection_matrix,
    horizontal_final_matrix,
    column_query_weight,
    column_key_weight,
    vertical_content_sigmoid_matrix,
    vertical_final_matrix,
    first_operand_matrix,
    second_operand_matrix,
    outer_output_weight,
):
    parallel = lax.axis_size("dap")
    groups = lax.axis_size("grp")
    devices = parallel * groups
    both = ("dap", "grp")
    sequences, residues, width = homolog_activity.shape
    residues_overall = residues * devices
    sequences_here = sequences // parallel
    channels = first_operand_matrix.shape[1]
    depth = outer_output_weight.shape[1]
    heads_here, row_tiles, column_tiles = tile_count(pairwise_bias.shape, groups)
    head_lanes = heads_here * PER_SPLIT_DIM
    large = residues_overall > 256
    place = (lax.axis_index("dap") * groups + lax.axis_index("grp")).astype(jnp.int32).reshape(1)
    shape = jax.ShapeDtypeStruct

    def exchange(value, mask):
        return lax.ppermute(value, both, [(at, at ^ mask) for at in range(devices)])

    def to_all(value):
        return lax.all_to_all(value, both, split_axis=0, concat_axis=0, tiled=True)

    right_tiles = channels * sequences // LANES
    row_slots = sequences_here * (width // LANES)
    half_tiles = heads_here // 2 * row_tiles * column_tiles
    operands = (
        pairwise_bias,
        alignment_mask.T,
        sequence_row_mask.reshape(1, sequences),
        homolog_activity,
    )
    rows_out, keep = call(
        functools.partial(share_kernel, (groups, sequences_here)),
        (
            shape((devices, row_slots + half_tiles + 1, residues, LANES), BF16),
            shape((residues, LANES), F32),
        ),
        operands,
        scratch=[pltpu.VMEM(operand.shape, operand.dtype) for operand in operands]
        + [pltpu.SemaphoreType.DMA((len(operands),))],
        fetch=True,
        mib=62,
    )
    rows_in = to_all(rows_out)
    right_out, left = call(
        factor_kernel,
        (
            shape((right_tiles, residues, LANES), BF16),
            shape((sequences * residues, channels), BF16),
        ),
        (homolog_activity, keep, first_operand_matrix.T, second_operand_matrix.T),
        mib=56 if large else 32,
    )
    pieces = [right_out] + [
        exchange(right_out, near * 4 * groups) for near in range(1, parallel // 4)
    ]
    right = jnp.stack(pieces)
    right_masks = [across * 2 * groups + mask for across in range(2) for mask in range(groups)]
    right_parts = [right] + [exchange(right, mask) for mask in right_masks[1:]]
    row_out_weight = jnp.stack(
        [horizontal_final_matrix]
        + [exchange(horizontal_final_matrix, relative) for relative in range(1, groups)]
    )

    row_weight = horizontal_projection_matrix.transpose(1, 0, 2)
    outer_weight = outer_output_weight.reshape(channels, channels, depth).transpose(1, 0, 2)
    content_weight = vertical_content_sigmoid_matrix.transpose(1, 0, 2)
    rows_in, row_weight, outer_weight, content_weight, row_out_weight, *right_parts = (
        lax.optimization_barrier(
            (rows_in, row_weight, outer_weight, content_weight, row_out_weight, *right_parts)
        )
    )
    other_bias = exchange(rows_in[:, row_slots:-1], groups)

    row_sizes = (groups, row_tiles, column_tiles)
    here = (sequences_here, residues_overall, head_lanes)
    part, keep_all, *projected = call(
        functools.partial(first_row_kernel, row_sizes),
        (
            shape(here, F32),
            shape((residues_overall, LANES), BF16),
            shape((8, residues_overall), F32),
            shape(here, BF16),
            shape(here, BF16),
            shape(here, BF16),
            shape(here, F32),
        ),
        (place, rows_in, row_weight),
        scalars=1,
        mib=60 if large else 32,
        micros=0.1,
    )
    mix_out = call(
        functools.partial(second_row_kernel, row_sizes),
        shape((devices, sequences_here, residues, head_lanes), BF16),
        (place, other_bias, part, *projected),
        scalars=1,
        mib=60 if large else 32,
        micros=0.1,
    )
    mix_in = to_all(mix_out)
    *late_parts, _ = lax.optimization_barrier((*right_parts, mix_out))
    right_masks += [mask + groups for mask in right_masks]
    late_parts += [exchange(late_part, groups) for late_part in late_parts]

    pairwise_update = call(
        functools.partial(outer_kernel, (groups, sequences, 2, tuple(right_masks))),
        shape((residues, residues_overall, depth), BF16),
        (
            place,
            keep_all,
            *late_parts,
            left,
            keep,
            outer_weight,
        ),
        scratch=[
            pltpu.VMEM((residues, channels * sequences, depth), BF16),
            pltpu.VMEM((devices, right_tiles, residues, LANES), BF16),
        ],
        scalars=1,
        mib=60 if large else 32,
    )

    alignment_output = call(
        functools.partial(column_kernel, groups),
        shape((sequences, residues, width), BF16),
        (
            place,
            homolog_activity,
            mix_in.reshape(parallel, groups, sequences_here, residues, head_lanes),
            keep,
            row_out_weight,
            column_query_weight,
            column_key_weight,
            content_weight,
            vertical_final_matrix,
        ),
        scalars=1,
        mib=56 if large else 32,
        micros=3,
    )
    return (alignment_output, pairwise_update)


def solution(mesh):
    return jax.shard_map(
        shards,
        mesh=mesh,
        in_specs=(
            P(None, ("dap", "grp"), None),
            P(None, ("dap", "grp")),
            P(),
            P(None, "dap", "grp"),
            P(None, None, "grp"),
            P("grp", None),
            P(),
            P(),
            P(),
            P(),
            P(),
            P(),
            P(),
        ),
        out_specs=(P(None, ("dap", "grp"), None), P(("dap", "grp"), None, None)),
        check_vma=False,
    )
```

```python
import functools

import jax
import jax.numpy as jnp
from jax import lax
from jax.experimental import pallas as pl
from jax.experimental.pallas import tpu as pltpu
from jax.sharding import PartitionSpec as P

PER_SPLIT_DIM = 32
LANES = 128
MASKED = -1000000000.0
F32 = jnp.float32
BF16 = jnp.bfloat16


def matmul(lhs, rhs):
    return jnp.dot(lhs, rhs, preferred_element_type=F32)


def matmul_nt(lhs, rhs):
    return lax.dot_general(lhs, rhs, (((1,), (1,)), ((), ())), preferred_element_type=F32)


def matmul_tn(lhs, rhs):
    return lax.dot_general(lhs, rhs, (((0,), (0,)), ((), ())), preferred_element_type=F32)


def rows_of(shape):
    return lax.broadcasted_iota(jnp.int32, shape, 0)


def lanes_of(shape):
    return lax.broadcasted_iota(jnp.int32, shape, 1)


def quotient(values, divisor):
    return lax.shift_right_logical(values, divisor.bit_length() - 1)


def remainder(values, divisor):
    return values & (divisor - 1)


def one_hot(condition):
    return condition.astype(F32).astype(BF16)


def flat_rows(tiles):
    blocks, sublanes, lanes = tiles.shape
    return tiles.astype(F32).reshape(blocks * sublanes, lanes).astype(BF16)


def layer_normalize(widened):
    centered = widened - jnp.mean(widened, axis=-1, keepdims=True)
    variance = jnp.mean(centered * centered, axis=-1, keepdims=True)
    return (centered * lax.rsqrt(variance + 1e-05)).astype(BF16)


def residue_major(sequences, residues):
    total = sequences * residues
    row, lane = rows_of((total, total)), lanes_of((total, total))
    return one_hot(lane == remainder(row, sequences) * residues + quotient(row, sequences))


def tile_count(bias_shape, groups):
    heads, bias_rows, bias_columns = bias_shape
    return heads // groups, bias_rows // 8, bias_columns // LANES


def share_kernel(
    sizes, bias_hbm, mask_hbm, present_hbm, x_hbm, rows_ref, keep_ref,
    bias_ref, mask_ref, present_ref, x_ref, sems,
):
    groups, sequences_here = sizes
    sources = (bias_hbm, mask_hbm, present_hbm, x_hbm)
    targets = (bias_ref, mask_ref, present_ref, x_ref)
    copies = [
        pltpu.make_async_copy(source, target, sems.at[at])
        for at, (source, target) in enumerate(zip(sources, targets))
    ]
    for copy in copies:
        copy.start()
    for copy in copies[:3]:
        copy.wait()
    sequences, residues, width = x_ref.shape
    heads_here, row_tiles, column_tiles = tile_count(bias_ref.shape, groups)
    half_heads = heads_here // 2
    keep = (mask_ref[...] * present_ref[...]).astype(F32)
    keep_padded = jnp.pad(keep, ((0, 0), (0, LANES - sequences))) if sequences < LANES else keep
    keep_ref[...] = keep_padded
    keep_tile = keep_padded.astype(BF16)
    last = rows_ref.shape[1] - 1
    for target in range(rows_ref.shape[0]):
        part, group = divmod(target, groups)
        slot = last - half_heads * row_tiles * column_tiles
        for head in range(half_heads):
            for row in range(row_tiles):
                for column in range(column_tiles):
                    rows_ref[target, slot] = bias_ref[
                        group * heads_here + part % 2 * half_heads + head,
                        row * 8 : (row + 1) * 8,
                        column * LANES : (column + 1) * LANES,
                    ]
                    slot += 1
        rows_ref[target, last] = keep_tile
    copies[3].wait()
    halves = width // LANES
    for part in range(sequences // sequences_here):
        for own in range(sequences_here):
            for half in range(halves):
                tile = x_ref[
                    part * sequences_here + own, :, half * LANES : (half + 1) * LANES
                ]
                for group in range(groups):
                    rows_ref[part * groups + group, own * halves + half] = tile


def factor_kernel(x_ref, keep_ref, left_w_ref, right_w_ref, right_ref, left_ref):
    sequences, residues, width = x_ref.shape
    total = sequences * residues
    channels = left_w_ref.shape[0]
    keep = keep_ref[:, :sequences]
    normed = layer_normalize(x_ref[...].astype(F32).reshape(total, width))
    left = matmul_nt(normed, left_w_ref[...]).astype(BF16)
    left = matmul(residue_major(sequences, residues), left)
    pick = one_hot(
        quotient(rows_of((total, residues)), sequences) == lanes_of((total, residues))
    )
    own_keep = matmul(pick, keep.astype(BF16))
    at_sequence = remainder(rows_of((total, sequences)), sequences) == lanes_of((total, sequences))
    own_keep = jnp.sum(jnp.where(at_sequence, own_keep, 0.0), axis=1, keepdims=True)
    left_ref[...] = (left * own_keep).astype(BF16)

    right = matmul_nt(normed, right_w_ref[...]).astype(BF16)
    residue_pick = one_hot(
        remainder(lanes_of((residues, total)), residues) == rows_of((residues, total))
    )
    per_tile = LANES // sequences
    spread = one_hot(
        remainder(lanes_of((sequences, LANES)), sequences) == rows_of((sequences, LANES))
    )
    keep_spread = matmul(keep.astype(BF16), spread)
    same_sequence = quotient(rows_of((total, LANES)), residues) == remainder(
        lanes_of((total, LANES)), sequences
    )
    for tile in range(channels // per_tile):
        select = one_hot(
            rows_of((channels, LANES))
            == tile * per_tile + quotient(lanes_of((channels, LANES)), sequences)
        )
        expanded = jnp.where(same_sequence, matmul(right, select), 0.0).astype(BF16)
        result = (matmul(residue_pick, expanded) * keep_spread).astype(BF16)
        right_ref[tile] = result


def attend_half(
    sizes, place_ref, bias_ref, first_slot, key_keep_ref, query_ref, key_ref, value_ref, other,
    block_rows, finish,
):
    groups, row_tiles, column_tiles = sizes
    sequences_here, residues_overall, head_lanes = query_ref.shape
    half_heads = head_lanes // PER_SPLIT_DIM // 2
    side = (quotient(place_ref[0], groups) & 1) ^ other

    def attend(block):
        start = block * block_rows
        parts = block_rows // (row_tiles * 8)
        head_of = quotient(lanes_of((residues_overall, head_lanes)), PER_SPLIT_DIM)
        query_head = quotient(lanes_of((block_rows, head_lanes)), PER_SPLIT_DIM)
        biases = []
        for head in range(half_heads):
            columns = []
            for group in range(groups):
                for column in range(column_tiles):
                    pieces = []
                    for at in range(parts):
                        for row in range(row_tiles):
                            slot = (head * row_tiles + row) * column_tiles + column
                            slot += first_slot
                            source = (block * parts + at) * groups + group
                            pieces.append(bias_ref[source, slot].astype(F32))
                    columns.append(jnp.concatenate(pieces, axis=0))
            biases.append(jnp.concatenate(columns, axis=1))
        for own in range(sequences_here):
            queries = query_ref[own, pl.ds(start, block_rows), :]
            keys, values = key_ref[own], value_ref[own]
            keep_row = key_keep_ref[own : own + 1, :] > 0.5
            total = jnp.zeros((block_rows, 2 * head_lanes), F32)
            for at in range(half_heads):
                head = side * half_heads + at
                query_part = jnp.where(query_head == head, queries, jnp.zeros_like(queries))
                scores = matmul_nt(query_part, keys) + biases[at]
                scores = jnp.where(keep_row, scores, MASKED)
                scores = scores - jnp.max(scores, axis=1, keepdims=True)
                weights = jnp.exp(scores).astype(BF16)
                mine = head_of == head
                value_part = jnp.where(mine, values, jnp.zeros_like(values))
                total = total + matmul(
                    weights, jnp.concatenate([value_part, one_hot(mine)], axis=1)
                )
            here = quotient(query_head, half_heads) == side
            mixed = total[:, :head_lanes] / jnp.where(here, total[:, head_lanes:], 1.0)
            finish(block, own, start, mixed)

    if residues_overall == block_rows:
        attend(0)
    else:
        pl.loop(0, residues_overall // block_rows)(attend)


def first_row_kernel(
    sizes, place_ref, rows_ref, weight_ref,
    part_ref, keep_all_ref, key_keep_ref, query_ref, key_ref, value_ref, gate_ref,
):
    groups = sizes[0]
    sequences_here = query_ref.shape[0]
    halves = weight_ref.shape[1] // LANES
    query_factor = PER_SPLIT_DIM ** (-0.5)
    for own in range(sequences_here):
        tiles = [rows_ref[:, own * halves + half].astype(F32) for half in range(halves)]
        normed = layer_normalize(
            jnp.concatenate([tile.reshape(-1, LANES) for tile in tiles], axis=1)
        )
        query_ref[own] = (matmul(normed, weight_ref[0]) * query_factor).astype(BF16)
        key_ref[own] = matmul(normed, weight_ref[1]).astype(BF16)
        value_ref[own] = matmul(normed, weight_ref[2]).astype(BF16)
        gate_ref[own] = jax.nn.sigmoid(matmul(normed, weight_ref[3]))

    keep_all = flat_rows(rows_ref[:, rows_ref.shape[1] - 1])
    keep_all_ref[...] = keep_all
    part = quotient(place_ref[0], groups)
    chosen = one_hot(lanes_of((8, LANES)) == part * sequences_here + rows_of((8, LANES)))
    key_keep_ref[...] = matmul_nt(chosen, keep_all)
    block_rows = min(query_ref.shape[1], 256)

    def finish(block, own, start, mixed):
        part_ref[own, pl.ds(start, block_rows), :] = mixed

    attend_half(
        sizes, place_ref, rows_ref, sequences_here * halves, key_keep_ref, query_ref, key_ref,
        value_ref, 0, block_rows, finish,
    )


def second_row_kernel(
    sizes, place_ref, swapped_ref, part_ref, key_keep_ref, query_ref, key_ref, value_ref,
    gate_ref, mix_ref,
):
    _, _, residues, head_lanes = mix_ref.shape
    block_rows = min(query_ref.shape[1], 256)
    count = block_rows // residues

    def finish(block, own, start, mixed):
        rows = pl.ds(start, block_rows)
        mixed = (part_ref[own, rows, :] + mixed) * gate_ref[own, rows, :]
        mix_ref[pl.ds(block * count, count), own] = mixed.reshape(
            count, residues, head_lanes
        ).astype(BF16)

    attend_half(
        sizes, place_ref, swapped_ref, 0, key_keep_ref, query_ref, key_ref, value_ref, 1,
        block_rows, finish,
    )


def outer_kernel(
    sizes, place_ref, keep_all_ref, *refs
):
    groups, sequences, pair, masks = sizes
    right_refs = refs[: len(masks)]
    left_ref, keep_ref, weight_ref, out_ref, mixed_s, right_s = refs[len(masks) :]
    residues = keep_ref.shape[0]
    channels, _, depth = weight_ref.shape
    left = left_ref[...]
    for channel in range(0, channels, 2):
        weights = jnp.concatenate([weight_ref[channel], weight_ref[channel + 1]], axis=1)
        product = matmul(left, weights).astype(BF16)
        for residue in range(residues):
            for step in range(2):
                mixed_s[
                    residue, (channel + step) * sequences : (channel + step + 1) * sequences, :
                ] = product[
                    residue * sequences : (residue + 1) * sequences,
                    step * depth : (step + 1) * depth,
                ]
    for mask, right_ref in zip(masks, right_refs):
        for at in range(right_ref.shape[0]):
            right_s[place_ref[0] ^ (mask + at * 4 * groups)] = right_ref[at]
    right = jnp.concatenate(
        [flat_rows(right_s[:, tile]) for tile in range(right_s.shape[1])], axis=1
    )
    keep_all = keep_all_ref[...]
    for first in range(0, residues, pair):
        members = range(first, first + pair)
        mixed = jnp.concatenate([mixed_s[residue] for residue in members], axis=1)
        keep_rows = jnp.concatenate(
            [
                jnp.broadcast_to(keep_ref[residue : residue + 1, :], (depth, LANES))
                for residue in members
            ],
            axis=0,
        ).astype(BF16)
        result = matmul(right, mixed) / matmul_nt(keep_all, keep_rows)
        for at, residue in enumerate(members):
            out_ref[residue] = result[:, at * depth : (at + 1) * depth].astype(BF16)


def column_kernel(
    sizes, place_ref, x_ref, mix_ref, keep_ref, row_out_ref, query_w_ref, key_w_ref, vg_w_ref,
    out_w_ref, out_ref,
):
    groups = sizes
    sequences, residues, width = x_ref.shape
    total = sequences * residues
    heads = query_w_ref.shape[1] // PER_SPLIT_DIM
    query_factor = PER_SPLIT_DIM ** (-0.5)
    own_group = place_ref[0] & (groups - 1)
    after = x_ref[...].astype(F32).reshape(total, width)
    for at in range(groups):
        group = own_group ^ at
        mixed = mix_ref[:, pl.ds(group, 1)]
        mixed = mixed.astype(F32).reshape(total, mixed.shape[-1]).astype(BF16)
        after = after + matmul(mixed, row_out_ref[at])
    after = after.astype(BF16).astype(F32)
    permutation = residue_major(sequences, residues)
    normed = matmul(permutation, layer_normalize(after)).astype(BF16)
    queries = (matmul(normed, query_w_ref[...]) * query_factor).astype(BF16)
    keys = matmul(normed, key_w_ref[...]).astype(BF16)
    values = matmul(normed, vg_w_ref[0]).astype(BF16)
    gate = jax.nn.sigmoid(matmul(normed, vg_w_ref[1]))

    together = max(1, min(residues, 256 // sequences))
    span = together * sequences
    head_rows = heads * sequences
    inner = heads * PER_SPLIT_DIM
    block_diagonal = quotient(rows_of((head_rows, inner)), sequences) == quotient(
        lanes_of((head_rows, inner)), PER_SPLIT_DIM
    )
    zero = jnp.zeros((head_rows, inner), BF16)

    def by_head(part):
        return jnp.where(block_diagonal, jnp.concatenate([part] * heads, axis=0), zero)

    mixes = []
    for first in range(0, residues, together):
        base = first * sequences
        query_span = queries[base : base + span]
        owner = quotient(rows_of((span, inner)), sequences)
        scores = jnp.zeros((head_rows, span), F32)
        for at in range(together):
            key_part = by_head(keys[base + at * sequences : base + (at + 1) * sequences])
            query_part = jnp.where(owner == at, query_span, jnp.zeros_like(query_span))
            scores = scores + matmul_nt(key_part, query_part)
        spread = one_hot(
            rows_of((residues, span)) == first + quotient(lanes_of((residues, span)), sequences)
        )
        key_keep = matmul_tn(keep_ref[...].astype(BF16), spread)[:sequences]
        scores = scores.reshape(heads, sequences, span)
        scores = jnp.where(key_keep[None] > 0.5, scores, MASKED)
        scores = jnp.exp(scores - jnp.max(scores, axis=1, keepdims=True))
        weights = scores / jnp.sum(scores, axis=1, keepdims=True)
        weights = weights.reshape(head_rows, span).T.astype(BF16)
        for at in range(together):
            value_part = by_head(values[base + at * sequences : base + (at + 1) * sequences])
            mixes.append(matmul(weights[at * sequences : (at + 1) * sequences], value_part))
    mixed = (jnp.concatenate(mixes, axis=0) * gate).astype(BF16)
    mixed = matmul_tn(permutation, mixed).astype(BF16)
    result = after + matmul(mixed, out_w_ref[...])
    out_ref[...] = result.reshape(sequences, residues, width).astype(BF16)


def call(kernel, outs, arguments, scratch=(), scalars=0, mib=32, micros=2, fetch=False):
    vmem = pl.BlockSpec(memory_space=pltpu.VMEM)
    read = pl.BlockSpec(memory_space=pltpu.HBM) if fetch else vmem
    smem = pl.BlockSpec(memory_space=pltpu.SMEM)
    return pl.pallas_call(
        kernel,
        out_shape=outs,
        in_specs=[smem] * scalars + [read] * (len(arguments) - scalars),
        out_specs=jax.tree.map(lambda _: vmem, outs),
        scratch_shapes=list(scratch),
        compiler_params=pltpu.CompilerParams(vmem_limit_bytes=mib * 1024 * 1024),
        cost_estimate=pl.CostEstimate(
            flops=int(micros * 1e9), bytes_accessed=int(micros * 1e6), transcendentals=0
        ),
    )(*arguments)


def shards(
    homolog_activity,
    alignment_mask,
    sequence_row_mask,
    pairwise_bias,
    horizontal_projection_matrix,
    horizontal_final_matrix,
    column_query_weight,
    column_key_weight,
    vertical_content_sigmoid_matrix,
    vertical_final_matrix,
    first_operand_matrix,
    second_operand_matrix,
    outer_output_weight,
):
    parallel = lax.axis_size("dap")
    groups = lax.axis_size("grp")
    devices = parallel * groups
    both = ("dap", "grp")
    sequences, residues, width = homolog_activity.shape
    residues_overall = residues * devices
    sequences_here = sequences // parallel
    channels = first_operand_matrix.shape[1]
    depth = outer_output_weight.shape[1]
    heads_here, row_tiles, column_tiles = tile_count(pairwise_bias.shape, groups)
    head_lanes = heads_here * PER_SPLIT_DIM
    large = residues_overall > 256
    place = (lax.axis_index("dap") * groups + lax.axis_index("grp")).astype(jnp.int32).reshape(1)
    shape = jax.ShapeDtypeStruct

    def exchange(value, mask):
        return lax.ppermute(value, both, [(at, at ^ mask) for at in range(devices)])

    def to_all(value):
        return lax.all_to_all(value, both, split_axis=0, concat_axis=0, tiled=True)

    right_tiles = channels * sequences // LANES
    row_slots = sequences_here * (width // LANES)
    half_tiles = heads_here // 2 * row_tiles * column_tiles
    operands = (
        pairwise_bias,
        alignment_mask.T,
        sequence_row_mask.reshape(1, sequences),
        homolog_activity,
    )
    rows_out, keep = call(
        functools.partial(share_kernel, (groups, sequences_here)),
        (
            shape((devices, row_slots + half_tiles + 1, residues, LANES), BF16),
            shape((residues, LANES), F32),
        ),
        operands,
        scratch=[pltpu.VMEM(operand.shape, operand.dtype) for operand in operands]
        + [pltpu.SemaphoreType.DMA((len(operands),))],
        fetch=True,
        mib=62,
    )
    rows_in = to_all(rows_out)
    right_out, left = call(
        factor_kernel,
        (
            shape((right_tiles, residues, LANES), BF16),
            shape((sequences * residues, channels), BF16),
        ),
        (homolog_activity, keep, first_operand_matrix.T, second_operand_matrix.T),
        mib=56 if large else 32,
    )
    right = right_out[None]
    mask = 4 * groups
    while mask < devices:
        right = jnp.concatenate([right, exchange(right, mask)])
        mask *= 2

    row_weight = horizontal_projection_matrix.transpose(1, 0, 2)
    outer_weight = outer_output_weight.reshape(channels, channels, depth).transpose(1, 0, 2)
    content_weight = vertical_content_sigmoid_matrix.transpose(1, 0, 2)
    across = exchange(right, 2 * groups)
    rows_in, row_weight, outer_weight, content_weight, _ = lax.optimization_barrier(
        (rows_in, row_weight, outer_weight, content_weight, right)
    )
    other_bias = exchange(rows_in[:, row_slots:-1], groups)

    row_sizes = (groups, row_tiles, column_tiles)
    here = (sequences_here, residues_overall, head_lanes)
    part, keep_all, *projected = call(
        functools.partial(first_row_kernel, row_sizes),
        (
            shape(here, F32),
            shape((residues_overall, LANES), BF16),
            shape((8, residues_overall), F32),
            shape(here, BF16),
            shape(here, BF16),
            shape(here, BF16),
            shape(here, F32),
        ),
        (place, rows_in, row_weight),
        scalars=1,
        mib=60 if large else 32,
        micros=0.1,
    )
    mix_out = call(
        functools.partial(second_row_kernel, row_sizes),
        shape((devices, sequences_here, residues, head_lanes), BF16),
        (place, other_bias, part, *projected),
        scalars=1,
        mib=60 if large else 32,
        micros=0.1,
    )
    mix_in = to_all(mix_out)
    right, across, own_final, _ = lax.optimization_barrier(
        (right, across, horizontal_final_matrix, mix_out)
    )
    right_masks, late_parts = [0, 2 * groups], [right, across]
    final_parts = [own_final]
    for mask in range(1, groups):
        right_masks += [mask, 2 * groups + mask]
        late_parts += [exchange(right, mask), exchange(across, mask)]
        final_parts.append(exchange(own_final, mask))
    row_out_weight = jnp.stack(final_parts)
    right_masks += [mask + groups for mask in right_masks]
    late_parts += [exchange(late_part, groups) for late_part in late_parts]

    pairwise_update = call(
        functools.partial(outer_kernel, (groups, sequences, 2, tuple(right_masks))),
        shape((residues, residues_overall, depth), BF16),
        (
            place,
            keep_all,
            *late_parts,
            left,
            keep,
            outer_weight,
        ),
        scratch=[
            pltpu.VMEM((residues, channels * sequences, depth), BF16),
            pltpu.VMEM((devices, right_tiles, residues, LANES), BF16),
        ],
        scalars=1,
        mib=60 if large else 32,
    )

    alignment_output = call(
        functools.partial(column_kernel, groups),
        shape((sequences, residues, width), BF16),
        (
            place,
            homolog_activity,
            mix_in.reshape(parallel, groups, sequences_here, residues, head_lanes),
            keep,
            row_out_weight,
            column_query_weight,
            column_key_weight,
            content_weight,
            vertical_final_matrix,
        ),
        scalars=1,
        mib=56 if large else 32,
        micros=3,
    )
    return (alignment_output, pairwise_update)


def solution(mesh):
    return jax.shard_map(
        shards,
        mesh=mesh,
        in_specs=(
            P(None, ("dap", "grp"), None),
            P(None, ("dap", "grp")),
            P(),
            P(None, "dap", "grp"),
            P(None, None, "grp"),
            P("grp", None),
            P(),
            P(),
            P(),
            P(),
            P(),
            P(),
            P(),
        ),
        out_specs=(P(None, ("dap", "grp"), None), P(("dap", "grp"), None, None)),
        check_vma=False,
    )
```
